32 devices in a mesh: lat: 4 (over y, x), lon: 2 (over core), blk: 4 (over z).
Axes of the slice: x: 2, y: 2, z: 4, core: 2. Of those that a mesh axis runs over, the one named last changes fastest.
Arguments:
- field: bfloat16 [2, 4, 6220800], P('lon', 'blk', 'lat'), may hold values from -25 to 25
- gain_one: float32 [768], P('blk'), may hold values from 0.5 to 1.5
- shift_one: float32 [768], P('blk'), may hold values from -1 to 1
- spec_w1: bfloat16 [2, 8, 96, 96], P(None, 'blk'), may hold values from -0.4375 to 0.4375
- spec_b1: float32 [2, 8, 96], P(None, 'blk'), may hold values from -1.5 to 1.5
- spec_w2: bfloat16 [2, 8, 96, 96], P(None, 'blk'), may hold values from -0.4375 to 0.4375
- spec_b2: float32 [2, 8, 96], P(None, 'blk'), may hold values from -1.5 to 1.5
- gain_two: float32 [768], P('blk'), may hold values from 0.5 to 1.5
- shift_two: float32 [768], P('blk'), may hold values from -1 to 1
- up_weight: bfloat16 [768, 3072], P(None, 'blk'), may hold values from -0.3125 to 0.3125
- up_bias: bfloat16 [3072], P('blk'), may hold values from -1.5 to 1.5
- down_weight: bfloat16 [3072, 768], P('blk'), may hold values from -0.21875 to 0.21875
- down_bias: float32 [768], P('blk'), may hold values from -1.5 to 1.5
- presence: int32 [360, 180], P('lat', 'lon'), may hold values from 0 to 20
- cotangent: bfloat16 [2, 4, 6220800], P('lon', 'blk', 'lat'), may hold values from -9 to 9
Outputs:
- mixed: bfloat16 [2, 4, 6220800], P('lon', 'blk', 'lat')
- input_grad: float32 [2, 4, 6220800], P('lon', 'blk', 'lat')
- gain_one_grad: float32 [768], P('blk')
- shift_one_grad: float32 [768], P('blk')
- spec_w1_grad: float32 [2, 8, 96, 96], P(None, 'blk')
- spec_b1_grad: float32 [2, 8, 96], P(None, 'blk')
- spec_w2_grad: float32 [2, 8, 96, 96], P(None, 'blk')
- spec_b2_grad: float32 [2, 8, 96], P(None, 'blk')
- gain_two_grad: float32 [768], P('blk')
- shift_two_grad: float32 [768], P('blk')
- up_weight_grad: float32 [768, 3072], P(None, 'blk')
- up_bias_grad: float32 [3072], P('blk')
- down_weight_grad: float32 [3072, 768], P('blk')
- down_bias_grad: float32 [768], P('blk')
The draws below stay inside these ranges and needn't reach their ends.
All inputs are finite; a program needn't handle non-finite values.
Results may differ from the reference program's by a relative error of at most 0.014.
The reference program's roundings to bfloat16 on the way count: a program that leaves them out, or rounds other values in their place, can miss the bound.
Values may be sent and summed in bfloat16 or wider, within the bound.
No kernel may reach another device: no remote copies, remote signals or barrier semaphores. Data moves between devices by JAX's collectives and lax.ppermute only.
A program may use at most 320 MiB of HBM per device.

```python
import math
import jax
import jax.numpy as jnp
import numpy as np
from jax import lax

C = 768
NB = 8
BS = 96
FF = 3072
H = 90
W = 180
VARS = 20
SNAP = 4
ROWS = 360
COLS_DEV = 90
CH_DEV = 192
CELLS = 6220800


def blocked_layout(values):
    split = values.reshape(ROWS, W // COLS_DEV, COLS_DEV, C // CH_DEV, CH_DEV)
    return split.transpose(1, 3, 0, 2, 4).reshape(W // COLS_DEV, C // CH_DEV, CELLS)


def draw_field(key, part):
    key = jax.random.fold_in(key, 11)
    row_place = jnp.arange(ROWS, dtype=jnp.float32) / ROWS
    channel_place = jnp.arange(C, dtype=jnp.float32) / C
    base = jnp.clip(jax.random.normal(key, (ROWS, W, C), jnp.float32), -5.0, 5.0)
    scales = (10.0 ** channel_place)[None, None, :] * (3.0 ** row_place)[:, None, None] / 6.0
    return blocked_layout(base * scales).astype(jnp.bfloat16)


def draw_cotangent(key, part):
    key = jax.random.fold_in(key, 23)
    row_place = jnp.arange(ROWS, dtype=jnp.float32)[:, None] / ROWS
    column_place = jnp.arange(W, dtype=jnp.float32)[None, :] / W
    base = jnp.clip(jax.random.normal(key, (ROWS, W, C), jnp.float32), -5.0, 5.0)
    scales = 3.0 ** (0.5 * (row_place + column_place)) / 1.7
    return blocked_layout(base * scales[..., None]).astype(jnp.bfloat16)


def place_ends(drawn, own_key, low, high):
    dims = drawn.shape
    spot = [jax.random.randint(jax.random.fold_in(own_key, axis), (), 0, dims[axis]) for axis in range(len(dims))]
    drawn = drawn.at[tuple(spot)].set(low)
    longest = dims.index(max(dims))
    spot[longest] = (spot[longest] + 1) % dims[longest]
    return drawn.at[tuple(spot)].set(high)


def with_spikes(result, stream_key, source, target, blocks, factor):
    def block_of(axis_at):
        return (jnp.arange(result.shape[axis_at]) // (result.shape[axis_at] // blocks)).reshape((-1,) + (1,) * (result.ndim - 1 - axis_at))

    one_side = jax.random.permutation(stream_key, blocks)[block_of(target)]
    other_side = (block_of(target) + blocks // 2) % blocks
    return jnp.where((block_of(source) == one_side) | (block_of(source) == other_side), factor * result, result)


def block_scale(stream_key, dims, pieces, low, largest):
    factor_of, own = 1.0, jax.random.fold_in(stream_key, 6)
    for dim, parts in pieces:
        heights = jnp.exp(jax.random.uniform(jax.random.fold_in(own, dim), (parts,), jnp.float32, low / len(pieces), largest / len(pieces)))
        factor_of = factor_of * jnp.repeat(heights, dims[dim] // parts).reshape([-1 if axis == dim else 1 for axis in range(len(dims))])
    return factor_of


def rank_table(number_of, slope):
    weights = [(1 << 20) // math.isqrt(grade ** slope) + 1 for grade in range(1, number_of + 1)]
    deviation = 1 + sum(weights) // (1 << 30)
    return np.cumsum(np.array([max(1, weight // deviation) for weight in weights]))


def skewed_ids(rng, extent, count, skew):
    table = rank_table(count, skew)
    pick = jax.random.randint(jax.random.fold_in(rng, 1), extent, 0, int(table[count - 1]))
    rank = jnp.searchsorted(jnp.asarray(table, jnp.int32), pick, side="right")
    return jax.random.permutation(jax.random.fold_in(rng, 2), count)[rank].astype(jnp.int32)


def normal_values(stream_key, extent, spread, limit, shards=(), kind=jnp.bfloat16):
    array = spread * jax.random.normal(stream_key, extent, jnp.float32)
    if shards:
        array = array * block_scale(stream_key, extent, shards, -0.22, 0.18)
    return jnp.clip(array, -limit, limit).astype(kind)


def bell_draw_with(stream_key, extent, spread, limit, shards, heavy, kind=jnp.bfloat16):
    entries = spread * jax.random.normal(stream_key, extent, jnp.float32)
    if shards:
        entries = entries * block_scale(stream_key, extent, shards, -0.22, 0.18)
    return jnp.clip(with_spikes(entries, jax.random.fold_in(stream_key, 3), *heavy), -limit, limit).astype(kind)


def setup_inputs(seed: int = 0) -> dict:
    streams_of = jax.random.split(jax.random.key(seed), 16)
    return {
        "field": draw_field(jax.random.fold_in(streams_of[15], 71), 0),
        "gain_one": jnp.clip(1.0 + 0.1 * jax.random.normal(streams_of[1], (C,), jnp.float32), 0.5, 1.5),
        "shift_one": normal_values(streams_of[2], (C,), 0.2, 1.0, ((0, 4),), jnp.float32),
        "spec_w1": normal_values(streams_of[3], (2, NB, BS, BS), (2 * BS) ** -0.5, 0.4375, ((1, 4),)),
        "spec_b1": normal_values(streams_of[4], (2, NB, BS), 0.3, 1.5, ((1, 4),), jnp.float32),
        "spec_w2": normal_values(streams_of[5], (2, NB, BS, BS), (2 * BS) ** -0.5, 0.4375, ((1, 4),)),
        "spec_b2": normal_values(streams_of[6], (2, NB, BS), 0.3, 1.5, ((1, 4),), jnp.float32),
        "gain_two": jnp.clip(1.0 + 0.1 * jax.random.normal(streams_of[7], (C,), jnp.float32), 0.5, 1.5),
        "shift_two": normal_values(streams_of[8], (C,), 0.2, 1.0, ((0, 4),), jnp.float32),
        "up_weight": bell_draw_with(streams_of[9], (C, FF), C ** -0.5, 0.3125, ((1, 4),), (1, 0, 4, 2.0)),
        "up_bias": normal_values(streams_of[10], (FF,), 0.3, 1.5, ((0, 4),)),
        "down_weight": bell_draw_with(streams_of[11], (FF, C), (FF // 2) ** -0.5, 0.21875, ((0, 4),), (0, 1, 4, 2.0)),
        "down_bias": normal_values(streams_of[12], (C,), 0.3, 1.5, ((0, 4),), jnp.float32),
        "presence": place_ends(skewed_ids(streams_of[13], (ROWS, W), VARS + 1, 2), jax.random.fold_in(streams_of[13], 3), 0, VARS).astype(jnp.int32),
        "cotangent": draw_cotangent(jax.random.fold_in(streams_of[15], 71), 0),
    }


EPS = 1e-05
SHRINK = 0.01
HIGH = lax.Precision.HIGHEST

@jax.custom_vjp
def low(v):
    return lax.optimization_barrier(v.astype(jnp.bfloat16)).astype(jnp.float32)

@jax.custom_vjp
def low_back(v):
    return v

def low_keep(v):
    return (low(v), None)

def low_pass(kept, grad):
    return (grad,)

def back_keep(v):
    return (v, None)

def back_low(kept, grad):
    return (low(grad),)
low.defvjp(low_keep, low_pass)
low_back.defvjp(back_keep, back_low)

def to_grid(values):
    blocked = values.reshape(W // COLS_DEV, C // CH_DEV, ROWS, COLS_DEV, CH_DEV)
    return blocked.transpose(2, 0, 3, 1, 4).reshape(ROWS, W, C)

def from_grid(values):
    split = values.reshape(ROWS, W // COLS_DEV, COLS_DEV, C // CH_DEV, CH_DEV)
    return split.transpose(1, 3, 0, 2, 4).reshape(W // COLS_DEV, C // CH_DEV, CELLS)

def layer_norm(values, gain, shift):
    center = lax.optimization_barrier(jnp.mean(values, axis=-1, keepdims=True))
    offset = values - center
    spread_sq = lax.optimization_barrier(jnp.mean(offset * offset, axis=-1, keepdims=True))
    return offset * lax.rsqrt(spread_sq + EPS) * gain + shift

def gelu_exact(values):
    return jax.nn.gelu(values, approximate=False)

def smooth_shrink(values):
    return values - SHRINK * jnp.tanh(values / SHRINK)

def complex_product(real_part, imag_part, weight, bias):
    real_out = jnp.einsum('...bi,bio->...bo', real_part, weight[0], precision=HIGH) - jnp.einsum('...bi,bio->...bo', imag_part, weight[1], precision=HIGH) + bias[0]
    imag_out = jnp.einsum('...bi,bio->...bo', imag_part, weight[0], precision=HIGH) + jnp.einsum('...bi,bio->...bo', real_part, weight[1], precision=HIGH) + bias[1]
    return (real_out, imag_out)

def spectral(normed, spec_w1, spec_b1, spec_w2, spec_b2):
    grid = normed.reshape(H, SNAP, W, C).transpose(1, 0, 2, 3)
    modes = jnp.fft.rfft2(grid, axes=(1, 2), norm='ortho')
    block_shape = modes.shape[:-1] + (NB, BS)
    mode_real = low(jnp.real(modes)).reshape(block_shape)
    mode_imag = low(jnp.imag(modes)).reshape(block_shape)
    first_real, first_imag = complex_product(mode_real, mode_imag, spec_w1, spec_b1)
    first_real = low(gelu_exact(low_back(first_real)))
    first_imag = low(gelu_exact(low_back(first_imag)))
    second_real, second_imag = complex_product(first_real, first_imag, spec_w2, spec_b2)
    second_real = low_back(second_real)
    second_imag = low_back(second_imag)
    shrunk_real = smooth_shrink(second_real)
    shrunk_imag = smooth_shrink(second_imag)
    merged = lax.complex(shrunk_real, shrunk_imag).reshape(modes.shape)
    spatial = jnp.fft.irfft2(merged, s=(H, W), axes=(1, 2), norm='ortho')
    return spatial.transpose(1, 0, 2, 3).reshape(ROWS, W, C)

def channel_mix(rows_block, gain_two, shift_two, up_weight, up_bias, down_weight, down_bias):
    normed = low(layer_norm(rows_block, gain_two, shift_two))
    up_pre = low_back(jnp.dot(normed, up_weight, precision=HIGH) + up_bias)
    up_act = low(gelu_exact(up_pre))
    return low_back(jnp.dot(up_act, down_weight, precision=HIGH) + down_bias)

def forward(field, gain_one, shift_one, spec_w1, spec_b1, spec_w2, spec_b2, gain_two, shift_two, up_weight, up_bias, down_weight, down_bias):
    normed_one = layer_norm(field, gain_one, shift_one)
    middle = spectral(normed_one, spec_w1, spec_b1, spec_w2, spec_b2) + normed_one + field

    def mix_block(rows_block):
        return channel_mix(rows_block, gain_two, shift_two, up_weight, up_bias, down_weight, down_bias)
    branch = lax.map(jax.checkpoint(mix_block), middle.reshape(SNAP, H * W, C))
    return middle + branch.reshape(ROWS, W, C)

def reference(field, gain_one, shift_one, spec_w1, spec_b1, spec_w2, spec_b2, gain_two, shift_two, up_weight, up_bias, down_weight, down_bias, presence, cotangent):
    wide = jnp.float32
    grid_in = to_grid(field.astype(wide))
    grid_cot = to_grid(cotangent.astype(wide))
    mixed, pull = jax.vjp(forward, grid_in, gain_one.astype(wide), shift_one.astype(wide), spec_w1.astype(wide), spec_b1.astype(wide), spec_w2.astype(wide), spec_b2.astype(wide), gain_two.astype(wide), shift_two.astype(wide), up_weight.astype(wide), up_bias.astype(wide), down_weight.astype(wide), down_bias.astype(wide))
    weighting = (1.0 + presence.astype(jnp.float32)) * 0.25
    grads = pull(grid_cot * weighting[..., None])
    return (from_grid(mixed).astype(jnp.bfloat16), from_grid(grads[0]), grads[1], grads[2], grads[3], grads[4], grads[5], grads[6], grads[7], grads[8], grads[9], grads[10], grads[11], grads[12])
```

```python
import functools
import math

import jax
import jax.numpy as jnp
import ml_dtypes
import numpy as np
from jax import lax
from jax.experimental import pallas as pl
from jax.experimental.pallas import tpu as pltpu
from jax.sharding import PartitionSpec as P

C = 768
BS = 96
H = 90
W = 180
EPS = 1e-05
SHRINK = 0.01
SLOTS = 96
ROW_PAD = 48
VMEM = 60 << 20
wide = jnp.float32
narrow = jnp.bfloat16


def slot_columns():
    cols = np.full((2, SLOTS // 2), -1)
    cols[0, :45] = np.arange(0, 90, 2)
    cols[1, :45] = np.arange(1, 90, 2)
    return cols.reshape(-1)


def column_table(mode_total, doubled):
    cols = slot_columns()
    place = np.concatenate([cols, cols + W // 2])
    valid = np.concatenate([cols >= 0, cols >= 0])
    freq = np.arange(mode_total)
    angle = 2.0 * np.pi * (freq[:, None] * place[None, :] % W) / W
    keep = (freq <= W // 2).astype(np.float64)
    if doubled:
        keep = keep * np.where((freq == 0) | (freq == W // 2), 1.0, 2.0)
    keep = keep[:, None] * valid[None, :] / math.sqrt(W)
    return np.concatenate([np.cos(angle) * keep, -np.sin(angle) * keep], axis=0)


def row_table(rows_total, group):
    snaps = rows_total // H
    half = rows_total // group
    slot = np.arange(group * ROW_PAD)
    row = slot // ROW_PAD * half + slot % ROW_PAD
    valid = slot % ROW_PAD < half
    step, snap = row // snaps, row % snaps
    match = (snap[:, None] == snap[None, :]) & valid[:, None] & valid[None, :]
    angle = 2.0 * np.pi * (step[:, None] * step[None, :] % H) / H
    scale = match / math.sqrt(H)
    return np.concatenate([np.cos(angle) * scale, np.sin(angle) * scale], axis=0)


def split_table(table):
    high = table.astype(ml_dtypes.bfloat16)
    rest = (table - high.astype(np.float64)).astype(ml_dtypes.bfloat16)
    return jnp.asarray(high), jnp.asarray(rest)


def dot(left, right):
    return lax.dot_general(left, right, (((1,), (0,)), ((), ())), preferred_element_type=wide)


def dot_nt(left, right):
    return lax.dot_general(left, right, (((1,), (1,)), ((), ())), preferred_element_type=wide)


def dot_tn(left, right):
    return lax.dot_general(left, right, (((0,), (0,)), ((), ())), preferred_element_type=wide)


def token_sums(values):
    ones = jnp.ones((8, values.shape[1]), narrow)
    high, rest = split(values)
    return dot_nt(ones, high) + dot_nt(ones, rest)


def split(values):
    high = values.astype(narrow)
    return high, (values - high.astype(wide)).astype(narrow)


def fine_dot(table, table_rest, values):
    high, rest = split(values)
    return dot(table, high) + (dot(table, rest) + dot(table_rest, high))


def normal_parts(values):
    cumulative = 0.5 * (1.0 + lax.erf(values * (1.0 / math.sqrt(2.0))))
    density = jnp.exp(-0.5 * values * values) * (1.0 / math.sqrt(2.0 * math.pi))
    return cumulative, density


def gelu_value(values):
    return values * (0.5 * (1.0 + lax.erf(values * (1.0 / math.sqrt(2.0)))))


def gelu_slope(values):
    cumulative, density = normal_parts(values)
    return cumulative + values * density


def norm_columns(sums):
    rows = []
    for side in range(2):
        mean = sums[side, 0:1] * (1.0 / C)
        spread = sums[side, 1:2] * (1.0 / C) - mean * mean
        rows += [mean, lax.rsqrt(spread + EPS)]
    rows.append(jnp.zeros((4, SLOTS), wide))
    return jnp.transpose(jnp.concatenate(rows, axis=0))


def swap_parts(values):
    half = values.shape[1] // 2
    return jnp.concatenate([values[:, half:], values[:, :half]], axis=1)


def part_sign(shape):
    lane = lax.broadcasted_iota(jnp.int32, shape, 1)
    return jnp.where(lane < shape[1] // 2, 1.0, -1.0).astype(wide)


def lane_tiles(lanes):
    return -(-lanes // 128)


def store_modes(scratch, row, values):
    count, lanes = values.shape
    room = lane_tiles(lanes) * 128
    if room != lanes:
        values = jnp.concatenate([values, jnp.zeros((count, room - lanes), wide)], axis=1)
    for tile, ref in enumerate(scratch):
        ref[pl.ds(row, count, stride=ROW_PAD), :] = values[:, 128 * tile : 128 * (tile + 1)]


def load_modes(scratch, row, count, lanes):
    pieces = [ref[pl.ds(row, count, stride=ROW_PAD), :] for ref in scratch]
    return jnp.concatenate(pieces, axis=1)[:, :lanes]


def flush_modes(scratch, parts):
    group, _, _, lanes = parts[0].shape
    share = sum(part.shape[1] for part in parts)
    for tile, ref in enumerate(scratch):
        width = min(128, lanes - 128 * tile)
        block = ref[...].reshape(group, share, ROW_PAD, 128)
        first = 0
        for part in parts:
            last = first + part.shape[1]
            part[:, :, :, 128 * tile : 128 * tile + width] = block[
                :, first:last, :, :width
            ].astype(part.dtype)
            first = last


def fill_modes(scratch, parts):
    group, _, _, lanes = parts[0].shape
    share = sum(part.shape[1] for part in parts)
    for tile, ref in enumerate(scratch):
        width = min(128, lanes - 128 * tile)
        first = 0
        for part in parts:
            count = part.shape[1]
            block = part[:, :, :, 128 * tile : 128 * tile + width].astype(wide)
            for g in range(group):
                start = (g * share + first) * ROW_PAD
                ref[start : start + count * ROW_PAD, :width] = block[g].reshape(
                    count * ROW_PAD, width
                )
            first += count


def mode_parts(share):
    return (share - share // 2, share // 2)


def mode_scratch(mode_total, lanes):
    return [pltpu.VMEM((mode_total * ROW_PAD, 128), wide)] * lane_tiles(lanes)


def params():
    return pltpu.CompilerParams(vmem_limit_bytes=VMEM)


def cost(flops, moved):
    return pl.CostEstimate(flops=int(flops), bytes_accessed=int(moved), transcendentals=0)


def full(shape):
    return pl.BlockSpec(shape, lambda *_: (0,) * len(shape))


def shape_of(shape, kind):
    return jax.ShapeDtypeStruct(shape, kind)


FLAT_ROWS = 18


def from_flat_kernel(with_sums, flat, out, *rest):
    scratch = rest[-1]
    scratch[...] = flat[0].astype(wide).reshape(scratch.shape)
    empty = jnp.zeros((3, 192), wide)
    for q in range(FLAT_ROWS):
        first = scratch[pl.ds(135 * q, 45, stride=3), :]
        second = scratch[pl.ds(135 * q + 1, 45, stride=3), :]
        third = scratch[pl.ds(135 * q + 2, 45, stride=3), :]
        even = jnp.concatenate([first, second[:, :64]], axis=1)
        odd = jnp.concatenate([second[:, 64:], third], axis=1)
        tile = jnp.concatenate([even, empty, odd, empty], axis=0)
        out[q] = tile.astype(narrow)
        if with_sums:
            total, total_sq = token_sums(tile), token_sums(tile * tile)
            rest[0][q] = jnp.concatenate([total[:1], total_sq[:1]], axis=0)


def from_flat(flat, rows, chans, with_sums):
    if chans != 192:
        grid = flat.reshape(rows, 45, 2, chans).transpose(0, 2, 1, 3)
        grid = jnp.pad(grid, ((0, 0), (0, 0), (0, 3), (0, 0))).reshape(rows, SLOTS, chans)
        if not with_sums:
            return grid
        wider = grid.astype(wide)
        return grid, jnp.stack([jnp.sum(wider, axis=2), jnp.sum(wider * wider, axis=2)], axis=1)
    block = FLAT_ROWS * 90 * chans
    out_specs = [pl.BlockSpec((FLAT_ROWS, SLOTS, chans), lambda i: (i, 0, 0))]
    out_shape = [shape_of((rows, SLOTS, chans), narrow)]
    if with_sums:
        out_specs.append(pl.BlockSpec((FLAT_ROWS, 2, SLOTS), lambda i: (i, 0, 0)))
        out_shape.append(shape_of((rows, 2, SLOTS), wide))
    outs = pl.pallas_call(
        functools.partial(from_flat_kernel, with_sums),
        grid=(rows // FLAT_ROWS,),
        in_specs=[pl.BlockSpec((1, 1, block), lambda i: (0, 0, i))],
        out_specs=out_specs,
        out_shape=out_shape,
        scratch_shapes=[pltpu.VMEM((block // 128, 128), wide)],
        compiler_params=params(),
        cost_estimate=cost(1e6, 1e5),
        name="from_flat",
    )(flat)
    return outs if with_sums else outs[0]


def write_flat(scratch, row, tile):
    even, odd = tile[0:45], tile[48:93]
    scratch[pl.ds(135 * row, 45, stride=3), :] = even[:, :128]
    scratch[pl.ds(135 * row + 1, 45, stride=3), :] = jnp.concatenate(
        [even[:, 128:], odd[:, :64]], axis=1
    )
    scratch[pl.ds(135 * row + 2, 45, stride=3), :] = odd[:, 64:]


PAIR_ROWS = 9


def to_flat_kernel(pairs, flat, scratch):
    chans = pairs.shape[1] // 2
    second = pl.program_id(0) == 1
    for q in range(PAIR_ROWS):
        pair = pairs[q * SLOTS : (q + 1) * SLOTS, :].astype(wide)
        write_flat(scratch, q, jnp.where(second, pair[:, chans:], pair[:, :chans]))
    flat[0] = scratch[...].reshape(1, scratch.shape[0] * 128).astype(flat.dtype)


def plain_flat(grid):
    rows, _, chans = grid.shape
    kept = grid.reshape(rows, 2, SLOTS // 2, chans)[:, :, :45].transpose(0, 2, 1, 3)
    return kept.reshape(1, 1, rows * 90 * chans)


def to_flat(pairs):
    chans = pairs.shape[1] // 2
    if chans != 192:
        grid = pairs[: 45 * SLOTS].reshape(45, SLOTS, 2, chans).transpose(2, 0, 1, 3)
        return plain_flat(grid.reshape(90, SLOTS, chans))
    block = PAIR_ROWS * 90 * chans
    steps = 45 // PAIR_ROWS
    return pl.pallas_call(
        to_flat_kernel,
        grid=(2, steps),
        in_specs=[pl.BlockSpec((PAIR_ROWS * SLOTS, 2 * chans), lambda h, i: (i, 0))],
        out_specs=pl.BlockSpec((1, 1, block), lambda h, i: (0, 0, h * steps + i)),
        out_shape=shape_of((1, 1, 90 * 90 * chans), pairs.dtype),
        scratch_shapes=[pltpu.VMEM((block // 128, 128), wide)],
        compiler_params=params(),
        cost_estimate=cost(1e6, 1e5),
        name="to_flat",
    )(pairs)


def final_tile(base, field, sums, grad_sums):
    mean = sums[0:1] * (1.0 / C)
    spread = sums[1:2] * (1.0 / C) - mean * mean
    inverse = lax.rsqrt(spread + EPS)
    shift = inverse * grad_sums[0:1] * (1.0 / C)
    slope = inverse * inverse * grad_sums[1:2] * (1.0 / C)
    cols = jnp.transpose(
        jnp.concatenate([mean, shift, slope, jnp.zeros((5, SLOTS), wide)], axis=0)
    )
    return base - cols[:, 1:2] - (field.astype(wide) - cols[:, 0:1]) * cols[:, 2:3]


def final_kernel(base, field, sums, grad_sums, flat, scratch):
    for q in range(FLAT_ROWS):
        write_flat(scratch, q, final_tile(base[q], field[q], sums[q], grad_sums[q]))
    flat[0] = scratch[...].reshape(1, scratch.shape[0] * 128)


def final_grid_kernel(base, field, sums, grad_sums, out):
    for q in range(FLAT_ROWS):
        out[q] = final_tile(base[q], field[q], sums[q], grad_sums[q])


def final_flat(base, field, sums, grad_sums):
    rows, _, chans = base.shape
    block = FLAT_ROWS * 90 * chans
    tiles = pl.BlockSpec((FLAT_ROWS, SLOTS, chans), lambda i: (i, 0, 0))
    pairs = pl.BlockSpec((FLAT_ROWS, 2, SLOTS), lambda i: (i, 0, 0))
    common = dict(
        grid=(rows // FLAT_ROWS,),
        in_specs=[tiles, tiles, pairs, pairs],
        compiler_params=params(),
        cost_estimate=cost(1e6, 1e5),
        name="final_flat",
    )
    if chans != 192:
        return plain_flat(
            pl.pallas_call(
                final_grid_kernel,
                out_specs=tiles,
                out_shape=shape_of(base.shape, wide),
                **common,
            )(base, field, sums, grad_sums)
        )
    return pl.pallas_call(
        final_kernel,
        out_specs=pl.BlockSpec((1, 1, block), lambda i: (0, 0, i)),
        out_shape=shape_of((1, 1, rows * 90 * chans), wide),
        scratch_shapes=[pltpu.VMEM((block // 128, 128), wide)],
        **common,
    )(base, field, sums, grad_sums)


STEP = 9


def spread_norm_kernel(field, sums, gain, shift, table, table_rest, out_a, out_b, *scratch):
    step = pl.program_id(0)
    for q in range(STEP):
        cols = norm_columns(sums[:, q])
        sides = []
        for side in range(2):
            centered = field[side, q].astype(wide) - cols[:, 2 * side : 2 * side + 1]
            normed = centered * cols[:, 2 * side + 1 : 2 * side + 2] * gain[...] + shift[...]
            sides.append(normed)
        modes = fine_dot(table[...], table_rest[...], jnp.concatenate(sides, axis=0))
        count = modes.shape[0] // 2
        store_modes(
            scratch, step * STEP + q, jnp.concatenate([modes[:count], modes[count:]], axis=1)
        )
    finish_spread(step, scratch, (out_a, out_b))


def spread_kernel(grad, table, out_a, out_b, *scratch):
    step = pl.program_id(0)
    for q in range(STEP):
        pair = grad[q * SLOTS : (q + 1) * SLOTS, :]
        chans = pair.shape[1] // 2
        modes = dot(table[...], jnp.concatenate([pair[:, :chans], pair[:, chans:]], axis=0))
        count = modes.shape[0] // 2
        store_modes(
            scratch, step * STEP + q, jnp.concatenate([modes[:count], modes[count:]], axis=1)
        )
    finish_spread(step, scratch, (out_a, out_b))


def finish_spread(step, scratch, out):
    @pl.when(step == 0)
    def _():
        count = scratch[0].shape[0] // ROW_PAD
        for row in range(45, ROW_PAD):
            for ref in scratch:
                ref[pl.ds(row, count, stride=ROW_PAD), :] = jnp.zeros((count, 128), wide)

    @pl.when(step == pl.num_programs(0) - 1)
    def _():
        flush_modes(scratch, out)


def spread(inputs, in_specs, kernel, tables, group, lanes, kind, name):
    mode_total = tables[0].shape[0] // 2
    outs = [(group, count, ROW_PAD, lanes) for count in mode_parts(mode_total // group)]
    return pl.pallas_call(
        kernel,
        grid=(45 // STEP,),
        in_specs=in_specs + [full(table.shape) for table in tables],
        out_specs=[full(out) for out in outs],
        out_shape=[shape_of(out, kind) for out in outs],
        scratch_shapes=mode_scratch(mode_total, lanes),
        compiler_params=params(),
        cost_estimate=cost(1e6, 1e5),
        name=name,
    )(*inputs, *tables)


TOKEN_STEP = 8
TOKEN_HALVES = ((0, 24), (24, 21))


def collect_kernel(first, modes_a, modes_b, field, sums, gain, shift, table, out, *scratch):
    step = pl.program_id(0)

    @pl.when(step == 0)
    def _():
        fill_modes(scratch, (modes_a, modes_b))

    for q in range(TOKEN_STEP):
        row = first + step * TOKEN_STEP + q
        spatial = spatial_rows(scratch, row, table, modes_a.shape[3])
        cols = norm_columns(sums[:, q])
        sides = []
        for side in range(2):
            centered = field[side, q].astype(wide) - cols[:, 2 * side : 2 * side + 1]
            normed = centered * cols[:, 2 * side + 1 : 2 * side + 2] * gain[...] + shift[...]
            sides.append(spatial[side] + normed + centered)
        pair = jnp.where(row < 45, jnp.concatenate(sides, axis=1), 0.0)
        out[q * SLOTS : (q + 1) * SLOTS, :] = pair.astype(narrow)


def spatial_rows(scratch, row, table, lanes):
    count = table.shape[0] // 2
    pair = load_modes(scratch, row, count, lanes).astype(narrow)
    stacked = jnp.concatenate([pair[:, : lanes // 2], pair[:, lanes // 2 :]], axis=0)
    spatial = dot_tn(table[...], stacked)
    return spatial[:SLOTS], spatial[SLOTS:]


def collect(modes, field, sums, gain, shift, table, rows, tokens):
    chans = field.shape[3]
    first, count = rows
    skip = first // TOKEN_STEP
    mode_total = table.shape[0] // 2
    return pl.pallas_call(
        functools.partial(collect_kernel, first),
        grid=(-(-count // TOKEN_STEP),),
        in_specs=[full(part.shape) for part in modes]
        + [
            pl.BlockSpec((2, TOKEN_STEP, SLOTS, chans), lambda i: (0, i + skip, 0, 0)),
            pl.BlockSpec((2, TOKEN_STEP, 2, SLOTS), lambda i: (0, i + skip, 0, 0)),
            full(gain.shape),
            full(shift.shape),
            full(table.shape),
        ],
        out_specs=pl.BlockSpec((TOKEN_STEP * SLOTS, 2 * chans), lambda i: (i, 0)),
        out_shape=shape_of((tokens, 2 * chans), narrow),
        scratch_shapes=mode_scratch(mode_total, 2 * chans),
        compiler_params=params(),
        cost_estimate=cost(1e6, 1e5),
        name="collect_norm",
    )(*modes, field, sums, gain, shift, table)


def collect_back_kernel(modes_a, modes_b, grad, field, sums, gain, table, base, parts, small, *scratch):
    step = pl.program_id(0)

    @pl.when(step == 0)
    def _():
        fill_modes(scratch, (modes_a, modes_b))
        small[...] = jnp.zeros(small.shape, wide)

    gain_sum = jnp.zeros((1, gain.shape[1]), wide)
    shift_sum = jnp.zeros((1, gain.shape[1]), wide)
    for q in range(STEP):
        spatial = spatial_rows(scratch, step * STEP + q, table, modes_a.shape[3])
        cols = norm_columns(sums[:, q])
        pair = grad[q * SLOTS : (q + 1) * SLOTS, :].astype(wide)
        chans = pair.shape[1] // 2
        for side in range(2):
            inverse = cols[:, 2 * side + 1 : 2 * side + 2]
            normed = (field[side, q].astype(wide) - cols[:, 2 * side : 2 * side + 1]) * inverse
            middle = pair[:, side * chans : (side + 1) * chans]
            total = middle + spatial[side]
            scaled = total * gain[...]
            base[side, q] = middle + inverse * scaled
            turned = scaled * normed
            parts[side, q] = jnp.concatenate(
                [token_sums(scaled)[:1], token_sums(turned)[:1]], axis=0
            )
            gain_sum = gain_sum + jnp.sum(total * normed, axis=0, keepdims=True)
            shift_sum = shift_sum + jnp.sum(total, axis=0, keepdims=True)
    small[0:1] += gain_sum
    small[1:2] += shift_sum


def collect_back(modes, grad, field, sums, gain, table):
    chans = field.shape[3]
    mode_total = table.shape[0] // 2
    return pl.pallas_call(
        collect_back_kernel,
        grid=(45 // STEP,),
        in_specs=[
            *[full(part.shape) for part in modes],
            pl.BlockSpec((STEP * SLOTS, 2 * chans), lambda i: (i, 0)),
            pl.BlockSpec((2, STEP, SLOTS, chans), lambda i: (0, i, 0, 0)),
            pl.BlockSpec((2, STEP, 2, SLOTS), lambda i: (0, i, 0, 0)),
            full(gain.shape),
            full(table.shape),
        ],
        out_specs=[
            pl.BlockSpec((2, STEP, SLOTS, chans), lambda i: (0, i, 0, 0)),
            pl.BlockSpec((2, STEP, 2, SLOTS), lambda i: (0, i, 0, 0)),
            full((8, chans)),
        ],
        out_shape=[
            shape_of(field.shape, wide),
            shape_of(sums.shape, wide),
            shape_of((8, chans), wide),
        ],
        scratch_shapes=mode_scratch(mode_total, 2 * chans),
        compiler_params=params(),
        cost_estimate=cost(1e6, 1e5),
        name="collect_back",
    )(*modes, grad, field, sums, gain, table)


def turn_rows(both):
    count = both.shape[0] // 2
    turned = swap_parts(both[count:])
    return both[:count] + turned * part_sign(turned.shape)


def return_rows(table, values):
    both = dot(table[...], values.astype(narrow))
    count = both.shape[0] // 2
    turned = swap_parts(both[count:])
    return both[:count] - turned * part_sign(turned.shape)


def shrink_bend(values):
    return jnp.tanh(values * (1.0 / SHRINK))


def spectral_kernel(modes, table, table_rest, w1, b1, w2, b2, out, low, act):
    rows = modes.shape[0] * ROW_PAD
    lanes = modes.shape[3]
    exact = fine_dot(table[...], table_rest[...], modes[...].reshape(rows, lanes))
    coarse = turn_rows(exact).astype(narrow)
    low[0] = coarse
    bent = gelu_value(dot(coarse, w1[...]) + b1[...]).astype(narrow)
    act[0] = bent
    second = dot(bent, w2[...]) + b2[...]
    shrunk = second - SHRINK * shrink_bend(second)
    out[...] = return_rows(table, shrunk).astype(narrow).reshape(out.shape)


def spectral(modes, table, table_rest, w1, b1, w2, b2):
    group, share, _, lanes = modes.shape
    rows = group * ROW_PAD
    mode_block = pl.BlockSpec((group, 1, ROW_PAD, lanes), lambda i: (0, i, 0, 0))
    kept_block = pl.BlockSpec((1, rows, lanes), lambda i: (i, 0, 0))
    return pl.pallas_call(
        spectral_kernel,
        grid=(share,),
        in_specs=[mode_block] + [full(x.shape) for x in (table, table_rest, w1, b1, w2, b2)],
        out_specs=[mode_block, kept_block, kept_block],
        out_shape=[
            shape_of(modes.shape, narrow),
            shape_of((share, rows, lanes), narrow),
            shape_of((share, rows, lanes), narrow),
        ],
        compiler_params=params(),
        cost_estimate=cost(1e6, 1e5),
        name="spectral",
    )(modes, table, table_rest, w1, b1, w2, b2)


def spectral_back_kernel(modes, low, act, table, w1, b1, w2, b2, *rest):
    before, (out, *outs) = rest[: -4 - bool(len(rest) > 4)], rest[-4 - bool(len(rest) > 4) :]
    second_part = bool(before)
    grads, (small, g1, g2) = (outs[0] if second_part else None), outs[-3:]
    rows = modes.shape[0] * ROW_PAD
    lanes = modes.shape[3]

    @pl.when(pl.program_id(0) == 0)
    def _():
        for k, ref in enumerate((small, g1, g2)):
            ref[...] = before[k][...] if second_part else jnp.zeros(ref.shape, wide)

    back = turn_rows(dot(table[...], modes[...].reshape(rows, lanes)))
    bent = act[0]
    bend = shrink_bend(dot(bent, w2[...]) + b2[...])
    second = (back * (bend * bend)).astype(narrow)
    g2[...] += dot_tn(bent, second)
    small[1:2] += jnp.sum(second.astype(wide), axis=0, keepdims=True)
    coarse = low[0]
    slope = gelu_slope(dot(coarse, w1[...]) + b1[...])
    first = (dot_nt(second, w2[...]) * slope).astype(narrow)
    g1[...] += dot_tn(coarse, first)
    small[0:1] += jnp.sum(first.astype(wide), axis=0, keepdims=True)
    out[...] = return_rows(table, dot_nt(first, w1[...])).astype(narrow).reshape(out.shape)
    if not second_part:
        return

    @pl.when(pl.program_id(0) == pl.num_programs(0) - 1)
    def _():
        half = lanes // 2
        at = 0
        for outer in (g1[...], g2[...]):
            for part in (
                outer[:half, :half] + outer[half:, half:],
                outer[:half, half:] - outer[half:, :half],
            ):
                for j in range(half // BS):
                    block = slice(j * BS, (j + 1) * BS)
                    grads[at : at + BS, :] = part[block, block]
                    at += BS


def spectral_back(modes, low, act, table, w1, b1, w2, b2, before=()):
    group, share, _, lanes = modes.shape
    rows = group * ROW_PAD
    mode_block = pl.BlockSpec((group, 1, ROW_PAD, lanes), lambda i: (0, i, 0, 0))
    kept_block = pl.BlockSpec((1, rows, lanes), lambda i: (i, 0, 0))
    sums = [shape_of((8, lanes), wide)] + [shape_of((lanes, lanes), wide)] * 2
    outs = [shape_of(modes.shape, narrow)]
    scratch = []
    if before:
        outs += [shape_of((2 * lanes, BS), wide), sums[0]]
        scratch = [pltpu.VMEM(sums[1].shape, wide)] * 2
    else:
        outs += sums
    return pl.pallas_call(
        spectral_back_kernel,
        grid=(share,),
        in_specs=[mode_block, kept_block, kept_block]
        + [full(x.shape) for x in (table, w1, b1, w2, b2, *before)],
        out_specs=[mode_block] + [full(out.shape) for out in outs[1:]],
        out_shape=outs,
        scratch_shapes=scratch,
        compiler_params=params(),
        cost_estimate=cost(1e6, 1e5),
        name="spectral_back",
    )(modes, low, act, table, w1, b1, w2, b2, *before)


def block_matrix_kernel(w1, w2, out1, out2):
    for weight, out in ((w1, out1), (w2, out2)):
        blocks = weight.shape[1]
        empty = jnp.zeros((BS, BS), wide)
        rows = []
        for part in range(2):
            for block in range(blocks):
                real, imag = weight[0, block].astype(wide), weight[1, block].astype(wide)
                pair = (real, imag) if part == 0 else (-imag, real)
                rows.append(
                    jnp.concatenate(
                        [piece if k == block else empty for piece in pair for k in range(blocks)],
                        axis=1,
                    )
                )
        out[...] = jnp.concatenate(rows, axis=0).astype(narrow)


def block_matrices(w1, w2):
    lanes = 2 * w1.shape[1] * BS
    return pl.pallas_call(
        block_matrix_kernel,
        out_shape=[shape_of((lanes, lanes), narrow)] * 2,
        compiler_params=params(),
        cost_estimate=cost(1e6, 1e5),
        name="block_matrices",
    )(w1, w2)


FF_TILE = 256
WEIGHT_ROWS = 128


def token_tile(values, side, start, count):
    chans = values[0].shape[2] // 2
    return jnp.concatenate(
        [
            source[0, pl.ds(start, count), side * chans : (side + 1) * chans]
            for source in values
        ],
        axis=1,
    ).astype(wide)


def norm_two(values):
    mean = jnp.mean(values, axis=1, keepdims=True)
    offset = values - mean
    inverse = lax.rsqrt(jnp.mean(offset * offset, axis=1, keepdims=True) + EPS)
    return offset * inverse, inverse


def mlp_kernel(
    tile,
    blks,
    place,
    *refs,
):
    middle, cot = refs[:blks], refs[blks : 2 * blks]
    refs = refs[2 * blks :]
    mlp_body(tile, place, middle, cot, *refs[:3], refs[3:7], refs[7:11], *refs[11:])


def mlp_body(
    tile,
    here,
    middle,
    cot,
    cols,
    gain,
    shift,
    ups,
    downs,
    up_bias,
    down_bias,
    *rest,
):
    before_refs = rest[:-13]
    mixed_kept, mixed_sent, middle_grad = rest[-13:-10]
    weight_grads, (bias_grad, small) = rest[-10:-6], rest[-6:-4]
    tokens_in, grads_in, branch, grad_sum = rest[-4:]
    first_core = here[1] == 0
    step = pl.program_id(0)
    share = middle[0].shape[1]
    pieces = share // tile

    @pl.when(step == 0)
    def _():
        small[...] = before_refs[5][...] if before_refs else jnp.zeros(small.shape, wide)
        for side in range(2):

            @pl.loop(0, pieces)
            def _(piece):
                start = pl.multiple_of(piece * tile, 16)
                place = pl.ds(pl.multiple_of(side * share + piece * tile, 16), tile)
                normed, _ = norm_two(token_tile(middle, side, start, tile))
                tokens_in[place, :] = (normed * gain[...] + shift[...]).astype(narrow)
                weight = cols[place, 1:2]
                grad = (token_tile(cot, side, start, tile) * weight).astype(narrow)
                grads_in[place, :] = grad
                small[0:1] += jnp.sum(grad.astype(wide), axis=0, keepdims=True)
                branch[place, :] = jnp.zeros((tile, C), wide)
                grad_sum[place, :] = jnp.zeros((tile, C), wide)

    up_tile = jnp.concatenate(
        [
            jnp.where(first_core, ups[k][0, j], ups[2 + k][0, j])
            for j in range(ups[0].shape[1])
            for k in range(2)
        ],
        axis=0,
    )
    down_tile = jnp.concatenate(
        [jnp.where(first_core, downs[2 + k][0, 0], downs[k][0, 0]) for k in range(2)], axis=0
    )
    tokens, grads = tokens_in[...], grads_in[...]
    before = dot(tokens, up_tile) + up_bias[...]
    cumulative, density = normal_parts(before)
    hidden = (before * cumulative).astype(narrow)
    before_grad = (dot_nt(grads, down_tile) * (cumulative + before * density)).astype(narrow)
    branch[...] += dot(hidden, down_tile)
    grad_sum[...] += dot_nt(before_grad, up_tile)
    rows = up_tile.shape[1] // 2
    for which, total in enumerate((dot_tn(before_grad, tokens), dot_tn(hidden, grads))):
        first, second = total[:rows], total[rows:]
        parts = (
            jnp.where(first_core, first, second),
            jnp.where(first_core, second, first),
        )
        for k, part in enumerate(parts):
            if before_refs:
                part = part + before_refs[2 * which + k][0].astype(wide)
            weight_grads[2 * which + k][0] = part.astype(narrow)
    bias_total = jnp.sum(before_grad.astype(wide), axis=0, keepdims=True)
    bias_grad[...] = bias_total + before_refs[4][...] if before_refs else bias_total

    @pl.when(step == pl.num_programs(0) - 1)
    def _():
        for side in range(2):

            @pl.loop(0, pieces)
            def _(piece):
                start = pl.multiple_of(piece * tile, 16)
                place = pl.ds(pl.multiple_of(side * share + piece * tile, 16), tile)
                values = token_tile(middle, side, start, tile)
                normed, inverse = norm_two(values)
                result = (
                    values + cols[place, 0:1] + (branch[place, :] + down_bias[...])
                ).astype(narrow)
                grad = grad_sum[place, :]
                small[1:2] += jnp.sum(grad * normed, axis=0, keepdims=True)
                small[2:3] += jnp.sum(grad, axis=0, keepdims=True)
                scaled = grad * gain[...]
                back = inverse * (
                    scaled
                    - jnp.mean(scaled, axis=1, keepdims=True)
                    - normed * jnp.mean(scaled * normed, axis=1, keepdims=True)
                )
                whole = token_tile(cot, side, start, tile) * cols[place, 1:2] + back
                whole = whole.astype(narrow)
                chans = middle[0].shape[2] // 2

                def put(out):
                    for b in range(len(middle)):
                        out[b, pl.ds(start, tile), :] = result[:, b * chans : (b + 1) * chans]

                pl.when(here[1] == side)(lambda: put(mixed_kept))
                pl.when(here[1] != side)(lambda: put(mixed_sent))
                for b in range(len(middle)):
                    lanes = slice(side * chans, (side + 1) * chans)
                    middle_grad[b, pl.ds(start, tile), lanes] = whole[
                        :, b * chans : (b + 1) * chans
                    ]


def mlp(middle, cot, cols, gain, shift, weights, up_bias, down_bias, before):
    blks, share, lanes = middle.shape
    count = 2 * share
    ff_here = weights[0].shape[3]
    per = ff_here // FF_TILE if ff_here % FF_TILE == 0 else 1
    width = ff_here // per
    tile = share // 4 if share % 64 == 0 else share // 2
    by_source = [
        pl.BlockSpec((1, share, lanes), lambda i, at, b=b: (b, 0, 0)) for b in range(blks)
    ]
    by_ring = [
        pl.BlockSpec((1, share, lanes), lambda i, at, b=b: ((at[0] + blks - b) % blks, 0, 0))
        for b in range(blks)
    ]
    grad_out = pl.BlockSpec((1, width // 2, C), lambda i, at: (i // per, i % per, 0))
    bias_out = pl.BlockSpec((1, width), lambda i, at: (0, i))
    groups = weights[0].shape[1]
    down_weights = weights
    if ff_here != C:
        down_weights = []
        for first in (0, 2):
            whole = jnp.stack(weights[first : first + 2], axis=2).reshape(blks, ff_here, C)
            down_weights += jnp.split(whole[:, None], 2, axis=2)
    return pl.pallas_call(
        functools.partial(mlp_kernel, tile, blks),
        grid_spec=pltpu.PrefetchScalarGridSpec(
            num_scalar_prefetch=1,
            grid=(blks * per,),
            in_specs=by_source
            + by_ring
            + [
                full(cols.shape),
                full(gain.shape),
                full(shift.shape),
                *[
                    pl.BlockSpec(
                        (1, groups, WEIGHT_ROWS, width), lambda i, at: (i // per, 0, 0, i % per)
                    )
                ]
                * 4,
                *[
                    pl.BlockSpec((1, 1, width // 2, C), lambda i, at: (i // per, i % per, 0, 0))
                ]
                * 4,
                bias_out,
                full(down_bias.shape),
            ]
            + ([grad_out] * 4 + [bias_out, full((8, C))] if before else []),
            out_specs=[
                full((blks, share, lanes // 2)),
                full((blks, share, lanes // 2)),
                full(middle.shape),
                *[grad_out] * 4,
                bias_out,
                full((8, C)),
            ],
            scratch_shapes=[
                pltpu.VMEM((count, C), narrow),
                pltpu.VMEM((count, C), narrow),
                pltpu.VMEM((count, C), wide),
                pltpu.VMEM((count, C), wide),
            ],
        ),
        out_shape=[
            shape_of((blks, share, lanes // 2), narrow),
            shape_of((blks, share, lanes // 2), narrow),
            shape_of(middle.shape, narrow),
            *[shape_of((blks, ff_here // 2, C), narrow)] * 4,
            shape_of((1, blks * ff_here), wide),
            shape_of((8, C), wide),
        ],
        compiler_params=params(),
        cost_estimate=cost(1e6, 1e5),
        name="channel_mlp",
    )(
        jnp.stack([lax.axis_index("blk"), lax.axis_index("lon")]).astype(jnp.int32),
        *([middle] * blks),
        *([cot] * blks),
        cols,
        gain,
        shift,
        *weights,
        *down_weights,
        up_bias,
        down_bias,
        *before,
    )


def weight_grads_kernel(pieces, up, down):
    lons = pieces.shape[1]
    for which, out in ((0, up), (1, down)):
        halves = [
            jnp.concatenate([pieces[lat, lon, which] for lat in range(pieces.shape[0])], axis=0)
            for lon in range(lons)
        ]
        rows = halves[0].shape[0]
        group = FF_TILE // 2 if 2 * rows % FF_TILE == 0 else rows
        tiles = [half[k : k + group] for k in range(0, rows, group) for half in halves]
        grad = jnp.concatenate(tiles, axis=0).astype(wide)
        out[...] = jnp.transpose(grad) if which == 0 else grad


def weight_grads(pieces, lons, ff_here):
    pieces = pieces.reshape((-1, lons) + pieces.shape[1:])
    return pl.pallas_call(
        weight_grads_kernel,
        out_shape=[shape_of((C, ff_here), wide), shape_of((ff_here, C), wide)],
        compiler_params=params(),
        cost_estimate=cost(1e6, 1e5),
        name="weight_grads",
    )(pieces)


def swap_first(values, axes):
    return lax.all_to_all(values, axes, split_axis=0, concat_axis=0, tiled=True)


def shifted(values, axis, by):
    size = lax.axis_size(axis)
    return lax.ppermute(values, axis, [(i, (i + by) % size) for i in range(size)])


def other_core(values):
    return lax.ppermute(values, "lon", [(0, 1), (1, 0)])


def pick(values, index):
    return lax.dynamic_index_in_dim(values, index, 0, keepdims=False)


def ring(values, axis):
    return [values] + [shifted(values, axis, by) for by in range(1, lax.axis_size(axis))]


def send(values, axis):
    size, here = lax.axis_size(axis), lax.axis_index(axis)
    pieces = [pick(values, here)]
    for by in range(1, size):
        pieces.append(shifted(pick(values, (here + by) % size), axis, by))
    return pieces


def send_across(values, axis):
    size, here = lax.axis_size(axis), lax.axis_index(axis)
    pieces = [pick(values, here)]
    for by in range(1, size):
        turn = [(i, i ^ by) for i in range(size)]
        pieces.append(lax.ppermute(pick(values, here ^ by), axis, turn))
    return pieces


def in_order(halves):
    size, blk = len(halves[0]), lax.axis_index("blk")
    lanes = halves[0][0].shape[1]
    out = jnp.zeros((sum(size * half[0].shape[0] for half in halves), lanes), halves[0][0].dtype)
    first = 0
    for half in halves:
        share = half[0].shape[0]
        for by, piece in enumerate(half):
            place = first + (blk - by) % size * share
            out = lax.dynamic_update_slice_in_dim(out, piece, place, 0)
        first += size * share
    return out


def lat_broadcast(values):
    count = lax.axis_size("lat")
    return swap_first(jnp.broadcast_to(values[None], (count,) + values.shape), "lat")


def grid_broadcast(values):
    count = lax.axis_size("lat") * lax.axis_size("lon")
    return swap_first(jnp.broadcast_to(values[None], (count,) + values.shape), ("lat", "lon"))


def tied(*values):
    return lax.optimization_barrier(values)


def per_device(
    field,
    gain_one,
    shift_one,
    spec_w1,
    spec_b1,
    spec_w2,
    spec_b2,
    gain_two,
    shift_two,
    up_weight,
    up_bias,
    down_weight,
    down_bias,
    presence,
    cotangent,
):
    rows, cols = presence.shape
    chans = gain_one.shape[0]
    lats, lons, blks = (lax.axis_size(name) for name in ("lat", "lon", "blk"))
    blk, lon = lax.axis_index("blk"), lax.axis_index("lon")
    grid_axes = ("lat", "lon")
    group = lats * lons
    half = rows // lons
    blocks = spec_w1.shape[1]
    mode_total = (W // 2 + group) // group * group
    lanes = 2 * chans
    ff_here = up_bias.shape[0]
    ahead, ahead_rest = split_table(column_table(mode_total, False))
    doubled, _ = split_table(column_table(mode_total, True))
    turn, turn_rest = split_table(row_table(rows * lats, group))
    gain_row, shift_row = gain_one[None, :], shift_one[None, :]

    weight_own = jnp.where(lon == 0, up_weight, down_weight.reshape(up_weight.shape))
    weight_own = weight_own.reshape(-1, 2, WEIGHT_ROWS, ff_here)
    weights = [lax.all_gather(weight_own[:, k], "blk", axis=0, tiled=False) for k in range(2)]

    field_cols, sums_part = from_flat(field, rows, chans, True)
    row_params = jnp.concatenate([up_bias.astype(wide), down_bias, gain_two, shift_two])
    param_count = row_params.shape[0]
    row_params = jnp.pad(row_params, (0, -param_count % (2 * SLOTS))).reshape(-1, 2, SLOTS)
    sums_ring = ring(jnp.concatenate([sums_part, row_params]), "blk")
    sums_cols = sum(piece[:rows] for piece in sums_ring)
    seen = presence.reshape(rows, 45, 2).transpose(0, 2, 1)
    seen = jnp.pad(seen, ((0, 0), (0, 0), (0, 3))).reshape(rows, 1, SLOTS).astype(wide)
    field_rows = swap_first(field_cols.reshape(2, half, SLOTS, chans), "lon")
    scalars = jnp.concatenate([sums_cols, seen], axis=1).reshape(2, half, 3, SLOTS)
    scalars = swap_first(scalars, "lon")
    sums_rows = scalars[:, :, :2]

    modes_a, modes_b = spread(
        (field_rows, sums_rows, gain_row, shift_row),
        [
            pl.BlockSpec((2, STEP, SLOTS, chans), lambda i: (0, i, 0, 0)),
            pl.BlockSpec((2, STEP, 2, SLOTS), lambda i: (0, i, 0, 0)),
            full(gain_row.shape),
            full(shift_row.shape),
        ],
        spread_norm_kernel,
        (ahead, ahead_rest),
        group,
        lanes,
        wide,
        "spread_norm",
    )
    cotangent, modes_a, modes_b, weights[0] = tied(cotangent, modes_a, modes_b, weights[0])
    modes_a = swap_first(modes_a, grid_axes)
    cot_cols = from_flat(cotangent, rows, chans, False).reshape(2, half, SLOTS, chans)
    cot_own, cot_other = pick(cot_cols, lon), other_core(pick(cot_cols, 1 - lon))
    cot_pairs = jnp.concatenate(
        [jnp.where(lon == 0, cot_own, cot_other), jnp.where(lon == 0, cot_other, cot_own)], axis=2
    )
    padded = half * SLOTS
    halves = [
        (first * SLOTS, -(-count * SLOTS // (blks * 16)) * 16) for first, count in TOKEN_HALVES
    ]
    tokens = blks * sum(share for _, share in halves)
    cot_pairs = jnp.pad(cot_pairs.reshape(padded, lanes), ((0, tokens - padded), (0, 0)))
    w1, w2 = block_matrices(spec_w1, spec_w2)
    b1, b2 = spec_b1.reshape(1, lanes), spec_b2.reshape(1, lanes)
    modes_b, cot_pairs, w1, w2, weights[1] = tied(modes_b, cot_pairs, w1, w2, weights[1])
    modes_b = swap_first(modes_b, grid_axes)
    cot_rings = [
        send(cot_pairs[first : first + blks * share].reshape(blks, share, lanes), "blk")
        for first, share in halves
    ]
    shrunk_a, *kept_a = spectral(modes_a, turn, turn_rest, w1, b1, w2, b2)
    modes_b, shrunk_a, cot_rings[0] = tied(modes_b, shrunk_a, cot_rings[0])
    shrunk_a = swap_first(shrunk_a, grid_axes)
    weights_other = [other_core(part) for part in weights]
    shrunk_b, *kept_b = spectral(modes_b, turn, turn_rest, w1, b1, w2, b2)
    cot_b = cot_rings[1]
    shrunk_b, shrunk_a, cot_b[1] = tied(shrunk_b, shrunk_a, cot_b[1])
    shrunk_b = swap_first(shrunk_b, grid_axes)
    per_token = jnp.stack(
        [scalars[:, :, 0] * (1.0 / C), (1.0 + scalars[:, :, 2]) * 0.25], axis=-1
    ).reshape(2, padded, 2)
    per_token = jnp.pad(per_token, ((0, 0), (0, tokens - padded), (0, 0)))
    per_token = [
        lax.dynamic_slice_in_dim(per_token, first + blk * share, share, 1).reshape(2 * share, 2)
        for first, share in halves
    ]
    params_ring = jnp.stack([piece[rows:].reshape(-1)[:param_count] for piece in sums_ring])
    params_all = jnp.concatenate([params_ring[:1], params_ring[:0:-1]])
    params_all = jnp.concatenate([params_all, params_all])
    params_all = lax.dynamic_slice_in_dim(params_all, blks - blk, blks, 0)
    bias_all = params_all[:, :ff_here].reshape(1, -1)
    token_params = [
        params_all[:, ff_here + i * chans : ff_here + (i + 1) * chans].reshape(1, C)
        for i in range(3)
    ]
    shrunk_b, shrunk_a, per_token, bias_all, cot_rings, token_params = tied(
        shrunk_b, shrunk_a, per_token, bias_all, cot_rings, token_params
    )

    middles = []
    for (first, share), spans in zip(halves, TOKEN_HALVES):
        middle = collect(
            (shrunk_a, shrunk_b),
            field_rows,
            sums_rows,
            gain_row,
            shift_row,
            doubled,
            spans,
            blks * share,
        )
        middle, shrunk_b = tied(middle, shrunk_b)
        middles.append(swap_first(middle.reshape(blks, share, lanes), "blk"))
    before, mixed_parts, grad_parts = (), [], []
    for middle, cot_ring, scalar in zip(middles, cot_rings, per_token):
        kept, sent, middle_grad, *before = mlp(
            middle,
            jnp.stack(cot_ring),
            scalar,
            token_params[1],
            token_params[2],
            [*weights, *weights_other],
            bias_all,
            token_params[0],
            before,
        )
        if grad_parts:
            middle_grad, before, grad_parts[0] = tied(middle_grad, before, grad_parts[0])
        mixed_parts.append((kept, sent))
        grad_parts.append(swap_first(middle_grad, "blk"))
    up_kept, up_sent, down_kept, down_sent, bias_part, small_part = before

    ff_half = ff_here // 2
    summed = jnp.stack(
        [
            (kept.astype(wide) + other_core(sent).astype(wide)).astype(narrow)
            for kept, sent in ((up_kept, up_sent), (down_kept, down_sent))
        ]
    ).reshape(2, blks, lats, ff_half // lats, C)
    summed = summed.transpose(2, 1, 0, 3, 4).reshape(-1, C)
    summed = lax.psum_scatter(summed, "lat", scatter_dimension=0, tiled=True)
    total = lax.psum_scatter(summed, "blk", scatter_dimension=0, tiled=True)
    total = total.reshape(2, ff_half // lats, C)
    mixed_rows = []
    for kept, sent in mixed_parts:
        sent = other_core(sent)
        mixed_rows.append(
            jnp.concatenate(
                [jnp.where(lon == 0, kept, sent), jnp.where(lon == 0, sent, kept)], axis=2
            )
        )
    owned = small_part[:3].reshape(3, blks, chans).transpose(1, 0, 2).reshape(blks, -1)
    owned = jnp.concatenate([owned, bias_part.reshape(blks, -1)], axis=1)
    owned = send(owned[:, None, :], "blk")
    grad_parts[1], mixed_rows, owned = tied(grad_parts[1], mixed_rows, owned)
    middle_grad = jnp.concatenate([part.reshape(-1, lanes) for part in grad_parts])

    back_a, back_b = spread(
        (middle_grad,),
        [pl.BlockSpec((STEP * SLOTS, lanes), lambda i: (i, 0))],
        spread_kernel,
        (doubled,),
        group,
        lanes,
        narrow,
        "spread_grad",
    )
    ring_a, ring_b = [send(mixed, "blk") for mixed in mixed_rows]
    back_a = swap_first(back_a, grid_axes)
    back_b, ring_a[1], ring_a[-1] = tied(back_b, ring_a[1], ring_a[-1])
    back_b = swap_first(back_b, grid_axes)
    back_a, *spec_sums = spectral_back(back_a, *kept_a, turn, w1, b1, w2, b2)
    back_a, back_b = tied(back_a, back_b)
    back_a = swap_first(back_a, grid_axes)
    back_b, spec_grads, spec_small = spectral_back(
        back_b, *kept_b, turn, w1, b1, w2, b2, tuple(spec_sums)
    )
    back_b, back_a, total, ring_a, ring_b[1] = tied(back_b, back_a, total, ring_a, ring_b[1])
    back_b = swap_first(back_b, grid_axes)
    total = lax.all_gather(total, grid_axes, axis=0, tiled=False)
    back_a, back_b, ring_b[-1], total, spec_grads = tied(
        back_a, back_b, ring_b[-1], total, spec_grads
    )

    vector = jnp.concatenate([spec_small[:2].reshape(-1), sum(owned).reshape(-1)])
    vector_size, vector_rows = vector.shape[0], -(-vector.shape[0] // (BS * group))
    vector = jnp.pad(vector, (0, group * vector_rows * BS - vector_size))
    shared = jnp.concatenate(
        [spec_grads.reshape(group, -1, BS), vector.reshape(group, vector_rows, BS)], axis=1
    )
    shared = jnp.sum(swap_first(shared, grid_axes), axis=0)

    base, part_sums, one_small = collect_back(
        (back_a, back_b), middle_grad, field_rows, sums_rows, gain_row, ahead
    )
    base, part_sums, total, ring_b, shared = tied(base, part_sums, total, ring_b, shared)
    grad_sums = swap_first(part_sums, "lon").reshape(rows, 2, SLOTS)
    base, grad_sums = tied(base, grad_sums)
    base = swap_first(base, "lon").reshape(rows, SLOTS, chans)
    mixed = in_order((ring_a, ring_b))
    base, mixed, one_small, total, shared = tied(base, mixed, one_small, total, shared)
    mixed = to_flat(mixed)
    up_grad, down_grad = weight_grads(total, lons, ff_here)
    own_rows = shared.shape[0]
    shared = grid_broadcast(jnp.concatenate([shared, one_small[:2].reshape(-1, BS)]))
    base, grad_sums, mixed, up_grad, down_grad = tied(
        base, sum(ring(grad_sums, "blk")), mixed, up_grad, down_grad
    )
    input_grad = final_flat(base, field_cols, sums_cols, grad_sums)

    one_small = jnp.sum(shared[:, own_rows:], axis=0).reshape(-1)
    vector = shared[:, own_rows - vector_rows : own_rows].reshape(-1)
    spec_grads = shared[:, : own_rows - vector_rows].reshape(2, 2, blocks, BS, BS)
    pieces, at = [one_small[:chans], one_small[chans:]], 0
    for size in (lanes, lanes, chans, chans, chans, ff_here):
        pieces.append(vector[at : at + size])
        at += size
    gain_one_grad, shift_one_grad, b1_grad, b2_grad = pieces[:4]
    down_bias_grad, gain_two_grad, shift_two_grad, up_bias_grad = pieces[4:]
    return (
        mixed,
        input_grad,
        gain_one_grad,
        shift_one_grad,
        spec_grads[0],
        b1_grad.reshape(spec_b1.shape),
        spec_grads[1],
        b2_grad.reshape(spec_b2.shape),
        gain_two_grad,
        shift_two_grad,
        up_grad,
        up_bias_grad,
        down_grad,
        down_bias_grad,
    )


def solution(mesh):
    placed = (
        P("lon", "blk", "lat"),
        P("blk"),
        P("blk"),
        P(None, "blk", None, None),
        P(None, "blk", None),
        P(None, "blk", None, None),
        P(None, "blk", None),
        P("blk"),
        P("blk"),
        P(None, "blk"),
        P("blk"),
        P("blk", None),
        P("blk"),
        P("lat", "lon"),
        P("lon", "blk", "lat"),
    )
    return jax.shard_map(
        per_device,
        mesh=mesh,
        in_specs=placed,
        out_specs=(
            P("lon", "blk", "lat"),
            P("lon", "blk", "lat"),
            P("blk"),
            P("blk"),
            P(None, "blk", None, None),
            P(None, "blk", None),
            P(None, "blk", None, None),
            P(None, "blk", None),
            P("blk"),
            P("blk"),
            P(None, "blk"),
            P("blk"),
            P("blk", None),
            P("blk"),
        ),
        check_vma=False,
    )
```

```python
import functools
import math

import jax
import jax.numpy as jnp
import ml_dtypes
import numpy as np
from jax import lax
from jax.experimental import pallas as pl
from jax.experimental.pallas import tpu as pltpu
from jax.sharding import PartitionSpec as P

C = 768
BS = 96
H = 90
W = 180
EPS = 1e-05
SHRINK = 0.01
SLOTS = 96
ROW_PAD = 48
VMEM = 60 << 20
wide = jnp.float32
narrow = jnp.bfloat16


def slot_columns():
    cols = np.full((2, SLOTS // 2), -1)
    cols[0, :45] = np.arange(0, 90, 2)
    cols[1, :45] = np.arange(1, 90, 2)
    return cols.reshape(-1)


def column_table(mode_total, doubled):
    cols = slot_columns()
    place = np.concatenate([cols, cols + W // 2])
    valid = np.concatenate([cols >= 0, cols >= 0])
    freq = np.arange(mode_total)
    angle = 2.0 * np.pi * (freq[:, None] * place[None, :] % W) / W
    keep = (freq <= W // 2).astype(np.float64)
    if doubled:
        keep = keep * np.where((freq == 0) | (freq == W // 2), 1.0, 2.0)
    keep = keep[:, None] * valid[None, :] / math.sqrt(W)
    return np.concatenate([np.cos(angle) * keep, -np.sin(angle) * keep], axis=0)


def row_table(rows_total, group):
    snaps = rows_total // H
    half = rows_total // group
    slot = np.arange(group * ROW_PAD)
    row = slot // ROW_PAD * half + slot % ROW_PAD
    valid = slot % ROW_PAD < half
    step, snap = row // snaps, row % snaps
    match = (snap[:, None] == snap[None, :]) & valid[:, None] & valid[None, :]
    angle = 2.0 * np.pi * (step[:, None] * step[None, :] % H) / H
    scale = match / math.sqrt(H)
    return np.concatenate([np.cos(angle) * scale, np.sin(angle) * scale], axis=0)


def split_table(table):
    high = table.astype(ml_dtypes.bfloat16)
    rest = (table - high.astype(np.float64)).astype(ml_dtypes.bfloat16)
    return jnp.asarray(high), jnp.asarray(rest)


def dot(left, right):
    return lax.dot_general(left, right, (((1,), (0,)), ((), ())), preferred_element_type=wide)


def dot_nt(left, right):
    return lax.dot_general(left, right, (((1,), (1,)), ((), ())), preferred_element_type=wide)


def dot_tn(left, right):
    return lax.dot_general(left, right, (((0,), (0,)), ((), ())), preferred_element_type=wide)


def token_sums(values):
    ones = jnp.ones((8, values.shape[1]), narrow)
    high, rest = split(values)
    return dot_nt(ones, high) + dot_nt(ones, rest)


def split(values):
    high = values.astype(narrow)
    return high, (values - high.astype(wide)).astype(narrow)


def fine_dot(table, table_rest, values):
    high, rest = split(values)
    return dot(table, high) + (dot(table, rest) + dot(table_rest, high))


def normal_parts(values):
    cumulative = 0.5 * (1.0 + lax.erf(values * (1.0 / math.sqrt(2.0))))
    density = jnp.exp(-0.5 * values * values) * (1.0 / math.sqrt(2.0 * math.pi))
    return cumulative, density


def gelu_value(values):
    return values * (0.5 * (1.0 + lax.erf(values * (1.0 / math.sqrt(2.0)))))


def gelu_slope(values):
    cumulative, density = normal_parts(values)
    return cumulative + values * density


def norm_columns(sums):
    rows = []
    for side in range(2):
        mean = sums[side, 0:1] * (1.0 / C)
        spread = sums[side, 1:2] * (1.0 / C) - mean * mean
        rows += [mean, lax.rsqrt(spread + EPS)]
    rows.append(jnp.zeros((4, SLOTS), wide))
    return jnp.transpose(jnp.concatenate(rows, axis=0))


def swap_parts(values):
    half = values.shape[1] // 2
    return jnp.concatenate([values[:, half:], values[:, :half]], axis=1)


def part_sign(shape):
    lane = lax.broadcasted_iota(jnp.int32, shape, 1)
    return jnp.where(lane < shape[1] // 2, 1.0, -1.0).astype(wide)


def lane_tiles(lanes):
    return -(-lanes // 128)


def store_modes(scratch, row, values):
    count, lanes = values.shape
    room = lane_tiles(lanes) * 128
    if room != lanes:
        values = jnp.concatenate([values, jnp.zeros((count, room - lanes), wide)], axis=1)
    for tile, ref in enumerate(scratch):
        ref[pl.ds(row, count, stride=ROW_PAD), :] = values[:, 128 * tile : 128 * (tile + 1)]


def load_modes(scratch, row, count, lanes):
    pieces = [ref[pl.ds(row, count, stride=ROW_PAD), :] for ref in scratch]
    return jnp.concatenate(pieces, axis=1)[:, :lanes]


def flush_modes(scratch, parts):
    group, _, _, lanes = parts[0].shape
    share = sum(part.shape[1] for part in parts)
    for tile, ref in enumerate(scratch):
        width = min(128, lanes - 128 * tile)
        block = ref[...].reshape(group, share, ROW_PAD, 128)
        first = 0
        for part in parts:
            last = first + part.shape[1]
            part[:, :, :, 128 * tile : 128 * tile + width] = block[
                :, first:last, :, :width
            ].astype(part.dtype)
            first = last


def fill_modes(scratch, parts):
    group, _, _, lanes = parts[0].shape
    share = sum(part.shape[1] for part in parts)
    for tile, ref in enumerate(scratch):
        width = min(128, lanes - 128 * tile)
        first = 0
        for part in parts:
            count = part.shape[1]
            block = part[:, :, :, 128 * tile : 128 * tile + width].astype(wide)
            for g in range(group):
                start = (g * share + first) * ROW_PAD
                ref[start : start + count * ROW_PAD, :width] = block[g].reshape(
                    count * ROW_PAD, width
                )
            first += count


def mode_parts(share):
    return (share - share // 2, share // 2)


def mode_scratch(mode_total, lanes):
    return [pltpu.VMEM((mode_total * ROW_PAD, 128), wide)] * lane_tiles(lanes)


def params():
    return pltpu.CompilerParams(vmem_limit_bytes=VMEM)


def cost(flops, moved):
    return pl.CostEstimate(flops=int(flops), bytes_accessed=int(moved), transcendentals=0)


def full(shape):
    return pl.BlockSpec(shape, lambda *_: (0,) * len(shape))


def once(shape, index):
    return pl.BlockSpec(shape, index, pipeline_mode=pl.Buffered(1))


def shape_of(shape, kind):
    return jax.ShapeDtypeStruct(shape, kind)


FLAT_ROWS = 18


def from_flat_kernel(with_sums, flat, out, *rest):
    scratch = rest[-1]
    scratch[...] = flat[0].astype(wide).reshape(scratch.shape)
    empty = jnp.zeros((3, 192), wide)
    for q in range(FLAT_ROWS):
        first = scratch[pl.ds(135 * q, 45, stride=3), :]
        second = scratch[pl.ds(135 * q + 1, 45, stride=3), :]
        third = scratch[pl.ds(135 * q + 2, 45, stride=3), :]
        even = jnp.concatenate([first, second[:, :64]], axis=1)
        odd = jnp.concatenate([second[:, 64:], third], axis=1)
        tile = jnp.concatenate([even, empty, odd, empty], axis=0)
        out[q] = tile.astype(narrow)
        if with_sums:
            total, total_sq = token_sums(tile), token_sums(tile * tile)
            rest[0][q] = jnp.concatenate([total[:1], total_sq[:1]], axis=0)


def from_flat(flat, rows, chans, with_sums):
    if chans != 192:
        grid = flat.reshape(rows, 45, 2, chans).transpose(0, 2, 1, 3)
        grid = jnp.pad(grid, ((0, 0), (0, 0), (0, 3), (0, 0))).reshape(rows, SLOTS, chans)
        if not with_sums:
            return grid
        wider = grid.astype(wide)
        return grid, jnp.stack([jnp.sum(wider, axis=2), jnp.sum(wider * wider, axis=2)], axis=1)
    block = FLAT_ROWS * 90 * chans
    out_specs = [pl.BlockSpec((FLAT_ROWS, SLOTS, chans), lambda i: (i, 0, 0))]
    out_shape = [shape_of((rows, SLOTS, chans), narrow)]
    if with_sums:
        out_specs.append(pl.BlockSpec((FLAT_ROWS, 2, SLOTS), lambda i: (i, 0, 0)))
        out_shape.append(shape_of((rows, 2, SLOTS), wide))
    outs = pl.pallas_call(
        functools.partial(from_flat_kernel, with_sums),
        grid=(rows // FLAT_ROWS,),
        in_specs=[pl.BlockSpec((1, 1, block), lambda i: (0, 0, i))],
        out_specs=out_specs,
        out_shape=out_shape,
        scratch_shapes=[pltpu.VMEM((block // 128, 128), wide)],
        compiler_params=params(),
        cost_estimate=cost(1e6, 1e5),
        name="from_flat",
    )(flat)
    return outs if with_sums else outs[0]


def write_flat(scratch, row, tile):
    even, odd = tile[0:45], tile[48:93]
    scratch[pl.ds(135 * row, 45, stride=3), :] = even[:, :128]
    scratch[pl.ds(135 * row + 1, 45, stride=3), :] = jnp.concatenate(
        [even[:, 128:], odd[:, :64]], axis=1
    )
    scratch[pl.ds(135 * row + 2, 45, stride=3), :] = odd[:, 64:]


PAIR_ROWS = 9


def place_pieces(blk, pieces, out):
    first, size = 0, len(pieces) // 2
    for half in (pieces[:size], pieces[size:]):
        share = half[0].shape[0]
        for by, piece in enumerate(half):
            place = first + lax.rem(blk + size - by, size) * share
            out[pl.ds(pl.multiple_of(place, 16), share), :] = piece[...]
        first += size * share


def to_flat_kernel(blk, *refs):
    *pieces, flat, rows, scratch = refs
    chans = rows.shape[1] // 2
    second = pl.program_id(0) == 1
    step = pl.program_id(1)

    @pl.when(jnp.logical_not(second) & (step == 0))
    def _():
        place_pieces(blk[0], pieces, rows)

    for q in range(PAIR_ROWS):
        start = pl.multiple_of((step * PAIR_ROWS + q) * SLOTS, SLOTS)
        pair = rows[pl.ds(start, SLOTS), :].astype(wide)
        write_flat(scratch, q, jnp.where(second, pair[:, chans:], pair[:, :chans]))
    flat[0] = scratch[...].reshape(1, scratch.shape[0] * 128).astype(flat.dtype)


def plain_flat(grid):
    rows, _, chans = grid.shape
    kept = grid.reshape(rows, 2, SLOTS // 2, chans)[:, :, :45].transpose(0, 2, 1, 3)
    return kept.reshape(1, 1, rows * 90 * chans)


def to_flat(halves):
    pieces = [piece for half in halves for piece in half]
    chans = pieces[0].shape[1] // 2
    if chans != 192:
        pairs = in_order(halves)
        grid = pairs[: 45 * SLOTS].reshape(45, SLOTS, 2, chans).transpose(2, 0, 1, 3)
        return plain_flat(grid.reshape(90, SLOTS, chans))
    block = PAIR_ROWS * 90 * chans
    steps = 45 // PAIR_ROWS
    tokens = sum(piece.shape[0] for piece in pieces)
    return pl.pallas_call(
        to_flat_kernel,
        grid_spec=pltpu.PrefetchScalarGridSpec(
            num_scalar_prefetch=1,
            grid=(2, steps),
            in_specs=[once(piece.shape, lambda *_: (0, 0)) for piece in pieces],
            out_specs=pl.BlockSpec((1, 1, block), lambda h, i, at: (0, 0, h * steps + i)),
            scratch_shapes=[
                pltpu.VMEM((tokens, 2 * chans), narrow),
                pltpu.VMEM((block // 128, 128), wide),
            ],
        ),
        out_shape=shape_of((1, 1, 90 * 90 * chans), narrow),
        compiler_params=params(),
        cost_estimate=cost(1e6, 1e5),
        name="to_flat",
    )(lax.axis_index("blk").astype(jnp.int32).reshape(1), *pieces)


def final_tile(base, field, sums, grad_sums):
    mean = sums[0:1] * (1.0 / C)
    spread = sums[1:2] * (1.0 / C) - mean * mean
    inverse = lax.rsqrt(spread + EPS)
    shift = inverse * grad_sums[0:1] * (1.0 / C)
    slope = inverse * inverse * grad_sums[1:2] * (1.0 / C)
    cols = jnp.transpose(
        jnp.concatenate([mean, shift, slope, jnp.zeros((5, SLOTS), wide)], axis=0)
    )
    return base - cols[:, 1:2] - (field.astype(wide) - cols[:, 0:1]) * cols[:, 2:3]


FINAL_ROWS = 15


def final_kernel(place, kept, other, field, sums, grad_sums, flat, *scratch):
    own = pl.program_id(0) // (45 // FINAL_ROWS) == place[0]
    for q in range(FINAL_ROWS):
        base = jnp.where(own, kept[q], other[q])
        tile = final_tile(base, field[q], sums[q], grad_sums[q])
        if scratch:
            write_flat(scratch[0], q, tile)
        else:
            flat[q] = tile
    if scratch:
        flat[0] = scratch[0][...].reshape(1, scratch[0].shape[0] * 128)


def final_flat(kept, other, field, sums, grad_sums):
    rows, _, chans = field.shape
    steps = 45 // FINAL_ROWS
    block = FINAL_ROWS * 90 * chans

    def half_of(which):
        def index(i, at):
            first = steps * (at[0] if which == 0 else 1 - at[0])
            return (jnp.clip(i - first, 0, steps - 1), 0, 0)

        return pl.BlockSpec((FINAL_ROWS, SLOTS, chans), index)

    tiles = pl.BlockSpec((FINAL_ROWS, SLOTS, chans), lambda i, at: (i, 0, 0))
    pairs = pl.BlockSpec((FINAL_ROWS, 2, SLOTS), lambda i, at: (i, 0, 0))
    simple = chans != 192
    out = pl.pallas_call(
        final_kernel,
        grid_spec=pltpu.PrefetchScalarGridSpec(
            num_scalar_prefetch=1,
            grid=(2 * steps,),
            in_specs=[half_of(0), half_of(1), tiles, pairs, pairs],
            out_specs=tiles if simple else pl.BlockSpec((1, 1, block), lambda i, at: (0, 0, i)),
            scratch_shapes=[] if simple else [pltpu.VMEM((block // 128, 128), wide)],
        ),
        out_shape=shape_of(field.shape if simple else (1, 1, rows * 90 * chans), wide),
        compiler_params=params(),
        cost_estimate=cost(1e6, 1e5),
        name="final_flat",
    )(lax.axis_index("lon").astype(jnp.int32).reshape(1), kept, other, field, sums, grad_sums)
    return plain_flat(out) if simple else out


STEP = 9
TOKEN_STEP = 8
TOKEN_HALVES = ((0, 24), (24, 21))


def spread_norm_kernel(field, sums, gain, shift, table, table_rest, out_a, out_b, *scratch):
    step = pl.program_id(0)
    for q in range(STEP):
        cols = norm_columns(sums[:, q])
        sides = []
        for side in range(2):
            centered = field[side, q].astype(wide) - cols[:, 2 * side : 2 * side + 1]
            normed = centered * cols[:, 2 * side + 1 : 2 * side + 2] * gain[...] + shift[...]
            sides.append(normed)
        modes = fine_dot(table[...], table_rest[...], jnp.concatenate(sides, axis=0))
        count = modes.shape[0] // 2
        store_modes(
            scratch, step * STEP + q, jnp.concatenate([modes[:count], modes[count:]], axis=1)
        )
    finish_spread(step, scratch, (out_a, out_b))


def spread_kernel(first, second, table, out_a, out_b, *scratch):
    step = pl.program_id(0)
    from_first = step < TOKEN_HALVES[0][1] // TOKEN_STEP
    for q in range(TOKEN_STEP):
        row = step * TOKEN_STEP + q
        rows = slice(q * SLOTS, (q + 1) * SLOTS)
        pair = jnp.where(from_first, first[rows, :], second[rows, :])
        chans = pair.shape[1] // 2
        modes = dot(table[...], jnp.concatenate([pair[:, :chans], pair[:, chans:]], axis=0))
        count = modes.shape[0] // 2
        modes = jnp.concatenate([modes[:count], modes[count:]], axis=1)
        store_modes(scratch, row, jnp.where(row < 45, modes, 0.0))

    @pl.when(step == pl.num_programs(0) - 1)
    def _():
        flush_modes(scratch, (out_a, out_b))


def finish_spread(step, scratch, out):
    @pl.when(step == 0)
    def _():
        count = scratch[0].shape[0] // ROW_PAD
        for row in range(45, ROW_PAD):
            for ref in scratch:
                ref[pl.ds(row, count, stride=ROW_PAD), :] = jnp.zeros((count, 128), wide)

    @pl.when(step == pl.num_programs(0) - 1)
    def _():
        flush_modes(scratch, out)


def spread(inputs, in_specs, kernel, tables, group, lanes, kind, steps, name):
    mode_total = tables[0].shape[0] // 2
    outs = [(group, count, ROW_PAD, lanes) for count in mode_parts(mode_total // group)]
    return pl.pallas_call(
        kernel,
        grid=(steps,),
        in_specs=in_specs + [full(table.shape) for table in tables],
        out_specs=[full(out) for out in outs],
        out_shape=[shape_of(out, kind) for out in outs],
        scratch_shapes=mode_scratch(mode_total, lanes),
        compiler_params=params(),
        cost_estimate=cost(1e6, 1e5),
        name=name,
    )(*inputs, *tables)


def collect_kernel(first, modes_a, modes_b, field, sums, gain, shift, table, out, *scratch):
    step = pl.program_id(0)

    @pl.when(step == 0)
    def _():
        fill_modes(scratch, (modes_a, modes_b))

    for q in range(TOKEN_STEP):
        row = first + step * TOKEN_STEP + q
        spatial = spatial_rows(scratch, row, table, modes_a.shape[3])
        cols = norm_columns(sums[:, q])
        sides = []
        for side in range(2):
            centered = field[side, q].astype(wide) - cols[:, 2 * side : 2 * side + 1]
            normed = centered * cols[:, 2 * side + 1 : 2 * side + 2] * gain[...] + shift[...]
            sides.append(spatial[side] + normed + centered)
        pair = jnp.where(row < 45, jnp.concatenate(sides, axis=1), 0.0)
        out[q * SLOTS : (q + 1) * SLOTS, :] = pair.astype(narrow)


def spatial_rows(scratch, row, table, lanes):
    count = table.shape[1] // 2
    pair = load_modes(scratch, row, count, lanes).astype(narrow)
    stacked = jnp.concatenate([pair[:, : lanes // 2], pair[:, lanes // 2 :]], axis=0)
    spatial = dot(table[...], stacked)
    return spatial[:SLOTS], spatial[SLOTS:]


def collect(modes, field, sums, gain, shift, table, rows, tokens):
    chans = field.shape[3]
    first, count = rows
    skip = first // TOKEN_STEP
    mode_total = table.shape[1] // 2
    return pl.pallas_call(
        functools.partial(collect_kernel, first),
        grid=(-(-count // TOKEN_STEP),),
        in_specs=[full(part.shape) for part in modes]
        + [
            pl.BlockSpec((2, TOKEN_STEP, SLOTS, chans), lambda i: (0, i + skip, 0, 0)),
            pl.BlockSpec((2, TOKEN_STEP, 2, SLOTS), lambda i: (0, i + skip, 0, 0)),
            full(gain.shape),
            full(shift.shape),
            full(table.shape),
        ],
        out_specs=pl.BlockSpec((TOKEN_STEP * SLOTS, 2 * chans), lambda i: (i, 0)),
        out_shape=shape_of((tokens, 2 * chans), narrow),
        scratch_shapes=mode_scratch(mode_total, 2 * chans),
        compiler_params=params(),
        cost_estimate=cost(1e6, 1e5),
        name="collect_norm",
    )(*modes, field, sums, gain, shift, table)


def collect_back_kernel(
    place, modes_a, modes_b, grad, field, sums, gain, table, kept, sent, parts, small, *scratch
):
    step = pl.program_id(0)

    @pl.when(step == 0)
    def _():
        fill_modes(scratch, (modes_a, modes_b))
        small[...] = jnp.zeros(small.shape, wide)

    gain_sum = jnp.zeros((1, gain.shape[1]), wide)
    shift_sum = jnp.zeros((1, gain.shape[1]), wide)
    for q in range(STEP):
        spatial = spatial_rows(scratch, step * STEP + q, table, modes_a.shape[3])
        cols = norm_columns(sums[:, q])
        pair = grad[q * SLOTS : (q + 1) * SLOTS, :].astype(wide)
        chans = pair.shape[1] // 2
        bases = []
        for side in range(2):
            inverse = cols[:, 2 * side + 1 : 2 * side + 2]
            normed = (field[side, q].astype(wide) - cols[:, 2 * side : 2 * side + 1]) * inverse
            middle = pair[:, side * chans : (side + 1) * chans]
            total = middle + spatial[side]
            scaled = total * gain[...]
            bases.append(middle + inverse * scaled)
            turned = scaled * normed
            parts[side, q] = jnp.concatenate(
                [token_sums(scaled)[:1], token_sums(turned)[:1]], axis=0
            )
            gain_sum = gain_sum + jnp.sum(total * normed, axis=0, keepdims=True)
            shift_sum = shift_sum + jnp.sum(total, axis=0, keepdims=True)
        kept[q] = jnp.where(place[0] == 0, bases[0], bases[1])
        sent[q] = jnp.where(place[0] == 0, bases[1], bases[0])
    small[0:1] += gain_sum
    small[1:2] += shift_sum


def collect_back(modes, grad, field, sums, gain, table):
    chans = field.shape[3]
    mode_total = table.shape[1] // 2
    half_rows = pl.BlockSpec((STEP, SLOTS, chans), lambda i, at: (i, 0, 0))
    pair_sums = pl.BlockSpec((2, STEP, 2, SLOTS), lambda i, at: (0, i, 0, 0))
    return pl.pallas_call(
        collect_back_kernel,
        grid_spec=pltpu.PrefetchScalarGridSpec(
            num_scalar_prefetch=1,
            grid=(45 // STEP,),
            in_specs=[
                *[full(part.shape) for part in modes],
                pl.BlockSpec((STEP * SLOTS, 2 * chans), lambda i, at: (i, 0)),
                pl.BlockSpec((2, STEP, SLOTS, chans), lambda i, at: (0, i, 0, 0)),
                pair_sums,
                full(gain.shape),
                full(table.shape),
            ],
            out_specs=[half_rows, half_rows, pair_sums, full((8, chans))],
            scratch_shapes=mode_scratch(mode_total, 2 * chans),
        ),
        out_shape=[
            shape_of(field.shape[1:], wide),
            shape_of(field.shape[1:], wide),
            shape_of(sums.shape, wide),
            shape_of((8, chans), wide),
        ],
        compiler_params=params(),
        cost_estimate=cost(1e6, 1e5),
        name="collect_back",
    )(lax.axis_index("lon").astype(jnp.int32).reshape(1), *modes, grad, field, sums, gain, table)


def turn_rows(both):
    count = both.shape[0] // 2
    turned = swap_parts(both[count:])
    return both[:count] + turned * part_sign(turned.shape)


def return_rows(table, values):
    both = dot(table[...], values.astype(narrow))
    count = both.shape[0] // 2
    turned = swap_parts(both[count:])
    return both[:count] - turned * part_sign(turned.shape)


def shrink_bend(values):
    return jnp.tanh(values * (1.0 / SHRINK))


def spectral_kernel(modes, table, table_rest, w1, b1, w2, b2, out, low, act):
    rows = modes.shape[0] * ROW_PAD
    lanes = modes.shape[3]
    exact = fine_dot(table[...], table_rest[...], modes[...].reshape(rows, lanes))
    coarse = turn_rows(exact).astype(narrow)
    low[0] = coarse
    bent = gelu_value(dot(coarse, w1[...]) + b1[...]).astype(narrow)
    act[0] = bent
    second = dot(bent, w2[...]) + b2[...]
    shrunk = second - SHRINK * shrink_bend(second)
    out[...] = return_rows(table, shrunk).astype(narrow).reshape(out.shape)


def spectral(modes, table, table_rest, w1, b1, w2, b2):
    group, share, _, lanes = modes.shape
    rows = group * ROW_PAD
    mode_block = pl.BlockSpec((group, 1, ROW_PAD, lanes), lambda i: (0, i, 0, 0))
    kept_block = pl.BlockSpec((1, rows, lanes), lambda i: (i, 0, 0))
    return pl.pallas_call(
        spectral_kernel,
        grid=(share,),
        in_specs=[mode_block] + [full(x.shape) for x in (table, table_rest, w1, b1, w2, b2)],
        out_specs=[mode_block, kept_block, kept_block],
        out_shape=[
            shape_of(modes.shape, narrow),
            shape_of((share, rows, lanes), narrow),
            shape_of((share, rows, lanes), narrow),
        ],
        compiler_params=params(),
        cost_estimate=cost(1e6, 1e5),
        name="spectral",
    )(modes, table, table_rest, w1, b1, w2, b2)


def spectral_back_kernel(modes, low, act, table, w1, b1, w2, b2, *rest):
    before, (out, *outs) = rest[: -4 - bool(len(rest) > 4)], rest[-4 - bool(len(rest) > 4) :]
    second_part = bool(before)
    grads, (small, g1, g2) = (outs[0] if second_part else None), outs[-3:]
    rows = modes.shape[0] * ROW_PAD
    lanes = modes.shape[3]

    @pl.when(pl.program_id(0) == 0)
    def _():
        for k, ref in enumerate((small, g1, g2)):
            ref[...] = before[k][...] if second_part else jnp.zeros(ref.shape, wide)

    back = turn_rows(dot(table[...], modes[...].reshape(rows, lanes)))
    bent = act[0]
    bend = shrink_bend(dot(bent, w2[...]) + b2[...])
    second = (back * (bend * bend)).astype(narrow)
    g2[...] += dot_tn(bent, second)
    small[1:2] += jnp.sum(second.astype(wide), axis=0, keepdims=True)
    coarse = low[0]
    slope = gelu_slope(dot(coarse, w1[...]) + b1[...])
    first = (dot_nt(second, w2[...]) * slope).astype(narrow)
    g1[...] += dot_tn(coarse, first)
    small[0:1] += jnp.sum(first.astype(wide), axis=0, keepdims=True)
    out[...] = return_rows(table, dot_nt(first, w1[...])).astype(narrow).reshape(out.shape)
    if not second_part:
        return

    @pl.when(pl.program_id(0) == pl.num_programs(0) - 1)
    def _():
        half = lanes // 2
        at = 0
        for outer in (g1[...], g2[...]):
            for part in (
                outer[:half, :half] + outer[half:, half:],
                outer[:half, half:] - outer[half:, :half],
            ):
                for j in range(half // BS):
                    block = slice(j * BS, (j + 1) * BS)
                    grads[at : at + BS, :] = part[block, block]
                    at += BS


def spectral_back(modes, low, act, table, w1, b1, w2, b2, before=()):
    group, share, _, lanes = modes.shape
    rows = group * ROW_PAD
    mode_block = pl.BlockSpec((group, 1, ROW_PAD, lanes), lambda i: (0, i, 0, 0))
    kept_block = pl.BlockSpec((1, rows, lanes), lambda i: (i, 0, 0))
    sums = [shape_of((8, lanes), wide)] + [shape_of((lanes, lanes), wide)] * 2
    outs = [shape_of(modes.shape, narrow)]
    scratch = []
    if before:
        outs += [shape_of((2 * lanes, BS), wide), sums[0]]
        scratch = [pltpu.VMEM(sums[1].shape, wide)] * 2
    else:
        outs += sums
    return pl.pallas_call(
        spectral_back_kernel,
        grid=(share,),
        in_specs=[mode_block, kept_block, kept_block]
        + [full(x.shape) for x in (table, w1, b1, w2, b2, *before)],
        out_specs=[mode_block] + [full(out.shape) for out in outs[1:]],
        out_shape=outs,
        scratch_shapes=scratch,
        compiler_params=params(),
        cost_estimate=cost(1e6, 1e5),
        name="spectral_back",
    )(modes, low, act, table, w1, b1, w2, b2, *before)


def block_matrix_kernel(w1, w2, out1, out2):
    for weight, out in ((w1, out1), (w2, out2)):
        blocks = weight.shape[1]
        empty = jnp.zeros((BS, BS), wide)
        rows = []
        for part in range(2):
            for block in range(blocks):
                real, imag = weight[0, block].astype(wide), weight[1, block].astype(wide)
                pair = (real, imag) if part == 0 else (-imag, real)
                rows.append(
                    jnp.concatenate(
                        [piece if k == block else empty for piece in pair for k in range(blocks)],
                        axis=1,
                    )
                )
        out[...] = jnp.concatenate(rows, axis=0).astype(narrow)


def block_matrices(w1, w2):
    lanes = 2 * w1.shape[1] * BS
    return pl.pallas_call(
        block_matrix_kernel,
        out_shape=[shape_of((lanes, lanes), narrow)] * 2,
        compiler_params=params(),
        cost_estimate=cost(1e6, 1e5),
        name="block_matrices",
    )(w1, w2)


FF_TILE = 256
CHUNKS = 4


def token_tile(values, side, start, count):
    chans = values[0].shape[2] // 2
    return jnp.concatenate(
        [
            source[0, pl.ds(start, count), side * chans : (side + 1) * chans]
            for source in values
        ],
        axis=1,
    ).astype(wide)


def norm_two(values):
    mean = jnp.mean(values, axis=1, keepdims=True)
    offset = values - mean
    inverse = lax.rsqrt(jnp.mean(offset * offset, axis=1, keepdims=True) + EPS)
    return offset * inverse, inverse


def mlp_kernel(
    tile,
    blks,
    place,
    *refs,
):
    middle, pieces = refs[:blks], refs[blks : 2 * blks]
    *refs, cot_all = refs[2 * blks :]

    @pl.when(pl.program_id(0) == 0)
    def _():
        for by, piece in enumerate(pieces):
            cot_all[pl.ds(lax.rem(place[0] + blks - by, blks), 1)] = piece[...][None]

    cot = [cot_all.at[pl.ds(b, 1)] for b in range(blks)]
    mlp_body(tile, place, middle, cot, *refs[:3], refs[3:5], refs[5:7], *refs[7:])


def mlp_body(
    tile,
    here,
    middle,
    cot,
    cols,
    gain,
    shift,
    ups,
    downs,
    up_bias,
    down_bias,
    *rest,
):
    before_refs = rest[:-13]
    mixed_kept, mixed_sent, middle_grad = rest[-13:-10]
    weight_grads, (bias_grad, small) = rest[-10:-6], rest[-6:-4]
    tokens_in, grads_in, branch, grad_sum = rest[-4:]
    first_core = here[1] == 0
    step = pl.program_id(0)
    share = middle[0].shape[1]
    pieces = share // tile

    @pl.when(step == 0)
    def _():
        small[...] = before_refs[5][...] if before_refs else jnp.zeros(small.shape, wide)
        for side in range(2):

            @pl.loop(0, pieces)
            def _(piece):
                start = pl.multiple_of(piece * tile, 16)
                place = pl.ds(pl.multiple_of(side * share + piece * tile, 16), tile)
                normed, _ = norm_two(token_tile(middle, side, start, tile))
                tokens_in[place, :] = (normed * gain[...] + shift[...]).astype(narrow)
                weight = cols[place, 1:2]
                grad = (token_tile(cot, side, start, tile) * weight).astype(narrow)
                grads_in[place, :] = grad
                small[0:1] += jnp.sum(grad.astype(wide), axis=0, keepdims=True)
                branch[place, :] = jnp.zeros((tile, C), wide)
                grad_sum[place, :] = jnp.zeros((tile, C), wide)

    up_tile = jnp.where(first_core, ups[0][0], ups[1][0])
    down_tile = jnp.where(first_core, downs[1][0], downs[0][0])
    tokens, grads = tokens_in[...], grads_in[...]
    count = tokens.shape[0]
    piece = count // CHUNKS
    hidden, before_grad = [], []
    for c in range(CHUNKS):
        place = slice(c * piece, (c + 1) * piece)
        before = dot(tokens[place], up_tile) + up_bias[...]
        into = dot_nt(grads[place], down_tile)
        cumulative, density = normal_parts(before)
        hidden.append((before * cumulative).astype(narrow))
        before_grad.append((into * (cumulative + before * density)).astype(narrow))
    hidden, before_grad = jnp.concatenate(hidden, axis=0), jnp.concatenate(before_grad, axis=0)
    branch[...] += dot(hidden, down_tile)
    grad_sum[...] += dot_nt(before_grad, up_tile)
    rows = up_tile.shape[1] // 2
    for which, total in enumerate((dot_tn(before_grad, tokens), dot_tn(hidden, grads))):
        first, second = (
            half.reshape(weight_grads[0].shape) for half in (total[:rows], total[rows:])
        )
        parts = (
            jnp.where(first_core, first, second),
            jnp.where(first_core, second, first),
        )
        for k, part in enumerate(parts):
            if before_refs:
                part = part + before_refs[2 * which + k][...].astype(wide)
            weight_grads[2 * which + k][...] = part.astype(narrow)
    bias_total = jnp.sum(before_grad.astype(wide), axis=0, keepdims=True)
    bias_grad[...] = bias_total + before_refs[4][...] if before_refs else bias_total

    @pl.when(step == pl.num_programs(0) - 1)
    def _():
        for side in range(2):

            @pl.loop(0, pieces)
            def _(piece):
                start = pl.multiple_of(piece * tile, 16)
                place = pl.ds(pl.multiple_of(side * share + piece * tile, 16), tile)
                values = token_tile(middle, side, start, tile)
                normed, inverse = norm_two(values)
                result = (
                    values + cols[place, 0:1] + (branch[place, :] + down_bias[...])
                ).astype(narrow)
                grad = grad_sum[place, :]
                small[1:2] += jnp.sum(grad * normed, axis=0, keepdims=True)
                small[2:3] += jnp.sum(grad, axis=0, keepdims=True)
                scaled = grad * gain[...]
                back = inverse * (
                    scaled
                    - jnp.mean(scaled, axis=1, keepdims=True)
                    - normed * jnp.mean(scaled * normed, axis=1, keepdims=True)
                )
                whole = token_tile(cot, side, start, tile) * cols[place, 1:2] + back
                whole = whole.astype(narrow)
                chans = middle[0].shape[2] // 2

                def put(out):
                    for b in range(len(middle)):
                        out[b, pl.ds(start, tile), :] = result[:, b * chans : (b + 1) * chans]

                pl.when(here[1] == side)(lambda: put(mixed_kept))
                pl.when(here[1] != side)(lambda: put(mixed_sent))
                for b in range(len(middle)):
                    lanes = slice(side * chans, (side + 1) * chans)
                    middle_grad[b, pl.ds(start, tile), lanes] = whole[
                        :, b * chans : (b + 1) * chans
                    ]


def mlp(middle, cot, cols, gain, shift, weights, up_bias, down_bias, before):
    blks, share, lanes = middle.shape
    count = 2 * share
    ff_here = weights[0].shape[2]
    per = ff_here // FF_TILE if ff_here % FF_TILE == 0 else 1
    width = ff_here // per
    tile = share
    by_source = [
        once((1, share, lanes), lambda i, at, b=b: (b, 0, 0)) for b in range(blks)
    ]
    by_ring = [once((share, lanes), lambda i, at: (0, 0))] * blks
    lats = lax.axis_size("lat")
    grad_shape = (lats, blks * per, width // 2 // lats, C)
    grad_out = pl.BlockSpec((lats, 1) + grad_shape[2:], lambda i, at: (0, i, 0, 0))
    bias_out = pl.BlockSpec((1, width), lambda i, at: (0, i))
    down_weights = [part.reshape(blks, ff_here, C) for part in weights]
    return pl.pallas_call(
        functools.partial(mlp_kernel, tile, blks),
        grid_spec=pltpu.PrefetchScalarGridSpec(
            num_scalar_prefetch=1,
            grid=(blks * per,),
            in_specs=by_source
            + by_ring
            + [
                full(cols.shape),
                full(gain.shape),
                full(shift.shape),
                *[pl.BlockSpec((1, C, width), lambda i, at: (i // per, 0, i % per))] * 2,
                *[pl.BlockSpec((1, width, C), lambda i, at: (i // per, i % per, 0))] * 2,
                bias_out,
                full(down_bias.shape),
            ]
            + ([grad_out] * 4 + [bias_out, full((8, C))] if before else []),
            out_specs=[
                full((blks, share, lanes // 2)),
                full((blks, share, lanes // 2)),
                full(middle.shape),
                *[grad_out] * 4,
                bias_out,
                full((8, C)),
            ],
            scratch_shapes=[
                pltpu.VMEM((count, C), narrow),
                pltpu.VMEM((count, C), narrow),
                pltpu.VMEM((count, C), wide),
                pltpu.VMEM((count, C), wide),
                pltpu.VMEM(middle.shape, narrow),
            ],
        ),
        out_shape=[
            shape_of((blks, share, lanes // 2), narrow),
            shape_of((blks, share, lanes // 2), narrow),
            shape_of(middle.shape, narrow),
            *[shape_of(grad_shape, narrow)] * 4,
            shape_of((1, blks * ff_here), wide),
            shape_of((8, C), wide),
        ],
        compiler_params=params(),
        cost_estimate=cost(1e6, 1e5),
        name="channel_mlp",
    )(
        jnp.stack([lax.axis_index("blk"), lax.axis_index("lon")]).astype(jnp.int32),
        *([middle] * blks),
        *cot,
        cols,
        gain,
        shift,
        *weights,
        *down_weights,
        up_bias,
        down_bias,
        *before,
    )


def weight_grads_kernel(pieces, up, down):
    lats, lons, tiles = pieces.shape[:3]
    for which, out in ((0, up), (1, down)):
        rows = [
            pieces[lat, lon, tile, which]
            for tile in range(tiles)
            for lon in range(lons)
            for lat in range(lats)
        ]
        grad = jnp.concatenate(rows, axis=0).astype(wide)
        out[...] = jnp.transpose(grad) if which == 0 else grad


def weight_grads(pieces, lons, ff_here):
    pieces = pieces.reshape((-1, lons) + pieces.shape[1:])
    return pl.pallas_call(
        weight_grads_kernel,
        out_shape=[shape_of((C, ff_here), wide), shape_of((ff_here, C), wide)],
        compiler_params=params(),
        cost_estimate=cost(1e6, 1e5),
        name="weight_grads",
    )(pieces)


def swap_first(values, axes):
    return lax.all_to_all(values, axes, split_axis=0, concat_axis=0, tiled=True)


def shifted(values, axis, by):
    size = lax.axis_size(axis)
    return lax.ppermute(values, axis, [(i, (i + by) % size) for i in range(size)])


def other_core(values):
    return lax.ppermute(values, "lon", [(0, 1), (1, 0)])


def pick(values, index):
    return lax.dynamic_index_in_dim(values, index, 0, keepdims=False)


def ring(values, axis):
    return [values] + [shifted(values, axis, by) for by in range(1, lax.axis_size(axis))]


def send_slices(values, axis):
    size, here = lax.axis_size(axis), lax.axis_index(axis)
    return [pick(values, here)] + [pick(values, (here + by) % size) for by in range(1, size)]


def send_pieces(pieces, axis):
    return pieces[:1] + [shifted(piece, axis, by) for by, piece in enumerate(pieces) if by]


def send(values, axis):
    return send_pieces(send_slices(values, axis), axis)


def in_order(halves):
    size, blk = len(halves[0]), lax.axis_index("blk")
    lanes = halves[0][0].shape[1]
    out = jnp.zeros((sum(size * half[0].shape[0] for half in halves), lanes), halves[0][0].dtype)
    first = 0
    for half in halves:
        share = half[0].shape[0]
        for by, piece in enumerate(half):
            place = first + (blk - by) % size * share
            out = lax.dynamic_update_slice_in_dim(out, piece, place, 0)
        first += size * share
    return out


def lat_broadcast(values):
    count = lax.axis_size("lat")
    return swap_first(jnp.broadcast_to(values[None], (count,) + values.shape), "lat")


def grid_broadcast(values):
    count = lax.axis_size("lat") * lax.axis_size("lon")
    return swap_first(jnp.broadcast_to(values[None], (count,) + values.shape), ("lat", "lon"))


def tied(*values):
    return lax.optimization_barrier(values)


def per_device(
    field,
    gain_one,
    shift_one,
    spec_w1,
    spec_b1,
    spec_w2,
    spec_b2,
    gain_two,
    shift_two,
    up_weight,
    up_bias,
    down_weight,
    down_bias,
    presence,
    cotangent,
):
    rows, cols = presence.shape
    chans = gain_one.shape[0]
    lats, lons, blks = (lax.axis_size(name) for name in ("lat", "lon", "blk"))
    blk, lon = lax.axis_index("blk"), lax.axis_index("lon")
    grid_axes = ("lat", "lon")
    group = lats * lons
    half = rows // lons
    blocks = spec_w1.shape[1]
    mode_total = (W // 2 + group) // group * group
    lanes = 2 * chans
    ff_here = up_bias.shape[0]
    ahead, ahead_rest = split_table(column_table(mode_total, False))
    ahead_back, _ = split_table(column_table(mode_total, False).T)
    doubled, _ = split_table(column_table(mode_total, True))
    doubled_back, _ = split_table(column_table(mode_total, True).T)
    turn, turn_rest = split_table(row_table(rows * lats, group))
    gain_row, shift_row = gain_one[None, :], shift_one[None, :]

    weight_own = jnp.where(lon == 0, up_weight, down_weight.reshape(up_weight.shape))
    weights = lax.all_gather(weight_own, "blk", axis=0, tiled=False)

    field_cols, sums_part = from_flat(field, rows, chans, True)
    row_params = jnp.concatenate([up_bias.astype(wide), down_bias, gain_two, shift_two])
    param_count = row_params.shape[0]
    row_params = jnp.pad(row_params, (0, -param_count % (2 * SLOTS))).reshape(-1, 2, SLOTS)
    sums_ring = ring(jnp.concatenate([sums_part, row_params]), "blk")
    field_rows = swap_first(field_cols.reshape(2, half, SLOTS, chans), "lon")
    field_rows, *sums_ring = tied(field_rows, *sums_ring)
    sums_cols = sum(piece[:rows] for piece in sums_ring)
    seen = presence.reshape(rows, 45, 2).transpose(0, 2, 1)
    seen = jnp.pad(seen, ((0, 0), (0, 0), (0, 3))).reshape(rows, 1, SLOTS).astype(wide)
    scalars = jnp.concatenate([sums_cols, seen], axis=1).reshape(2, half, 3, SLOTS)
    scalars = swap_first(scalars, "lon")
    sums_rows = scalars[:, :, :2]

    modes_a, modes_b = spread(
        (field_rows, sums_rows, gain_row, shift_row),
        [
            pl.BlockSpec((2, STEP, SLOTS, chans), lambda i: (0, i, 0, 0)),
            pl.BlockSpec((2, STEP, 2, SLOTS), lambda i: (0, i, 0, 0)),
            full(gain_row.shape),
            full(shift_row.shape),
        ],
        spread_norm_kernel,
        (ahead, ahead_rest),
        group,
        lanes,
        wide,
        45 // STEP,
        "spread_norm",
    )
    cotangent, modes_a, modes_b = tied(cotangent, modes_a, modes_b)
    modes_a = swap_first(modes_a, grid_axes)
    cot_cols = from_flat(cotangent, rows, chans, False).reshape(2, half, SLOTS, chans)
    cot_own, cot_other = pick(cot_cols, lon), other_core(pick(cot_cols, 1 - lon))
    cot_pairs = jnp.concatenate(
        [jnp.where(lon == 0, cot_own, cot_other), jnp.where(lon == 0, cot_other, cot_own)], axis=2
    )
    padded = half * SLOTS
    halves = [
        (first * SLOTS, -(-count * SLOTS // (blks * 16)) * 16) for first, count in TOKEN_HALVES
    ]
    tokens = blks * sum(share for _, share in halves)
    cot_pairs = jnp.pad(cot_pairs.reshape(padded, lanes), ((0, tokens - padded), (0, 0)))
    w1, w2 = block_matrices(spec_w1, spec_w2)
    b1, b2 = spec_b1.reshape(1, lanes), spec_b2.reshape(1, lanes)
    per_token = jnp.stack(
        [scalars[:, :, 0] * (1.0 / C), (1.0 + scalars[:, :, 2]) * 0.25], axis=-1
    ).reshape(2, padded, 2)
    per_token = jnp.pad(per_token, ((0, 0), (0, tokens - padded), (0, 0)))
    per_token = [
        lax.dynamic_slice_in_dim(per_token, first + blk * share, share, 1).reshape(2 * share, 2)
        for first, share in halves
    ]
    params_ring = jnp.stack([piece[rows:].reshape(-1)[:param_count] for piece in sums_ring])
    params_ring = [params_ring[k] for k in [0] + list(range(blks - 1, 0, -1))] * 2
    params_all = lax.dynamic_slice_in_dim(jnp.stack(params_ring), blks - blk, blks, 0)
    bias_all = params_all[:, :ff_here].reshape(1, -1)
    token_params = [
        params_all[:, ff_here + i * chans : ff_here + (i + 1) * chans].reshape(1, C)
        for i in range(3)
    ]
    modes_b, cot_pairs, w1, w2, weights, per_token, bias_all, token_params = tied(
        modes_b, cot_pairs, w1, w2, weights, per_token, bias_all, token_params
    )
    modes_b = swap_first(modes_b, grid_axes)
    cot_rings = [
        send(cot_pairs[first : first + blks * share].reshape(blks, share, lanes), "blk")
        for first, share in halves
    ]
    shrunk_a, *kept_a = spectral(modes_a, turn, turn_rest, w1, b1, w2, b2)
    modes_b, shrunk_a, cot_rings[0] = tied(modes_b, shrunk_a, cot_rings[0])
    shrunk_a = swap_first(shrunk_a, grid_axes)
    weights_other = other_core(weights)
    shrunk_b, *kept_b = spectral(modes_b, turn, turn_rest, w1, b1, w2, b2)
    cot_b = cot_rings[1]
    shrunk_b, shrunk_a, cot_b[1], cot_b[-1] = tied(shrunk_b, shrunk_a, cot_b[1], cot_b[-1])
    shrunk_b = swap_first(shrunk_b, grid_axes)
    shrunk_b, shrunk_a, cot_rings = tied(shrunk_b, shrunk_a, cot_rings)

    middles = []
    for (first, share), spans in zip(halves, TOKEN_HALVES):
        middle = collect(
            (shrunk_a, shrunk_b),
            field_rows,
            sums_rows,
            gain_row,
            shift_row,
            doubled_back,
            spans,
            blks * share,
        )
        middle, shrunk_b = tied(middle, shrunk_b)
        middles.append(swap_first(middle.reshape(blks, share, lanes), "blk"))
    before, mixed_parts, grad_parts = (), [], []
    for middle, cot_ring, scalar in zip(middles, cot_rings, per_token):
        kept, sent, middle_grad, *before = mlp(
            middle,
            cot_ring,
            scalar,
            token_params[1],
            token_params[2],
            (weights, weights_other),
            bias_all,
            token_params[0],
            before,
        )
        if grad_parts:
            middle_grad, before, grad_parts[0] = tied(middle_grad, before, grad_parts[0])
        mixed_parts.append((kept, sent))
        grad_parts.append(swap_first(middle_grad, "blk"))
    up_kept, up_sent, down_kept, down_sent, bias_part, small_part = before

    summed = jnp.stack(
        [
            (kept.astype(wide) + other_core(sent).astype(wide)).astype(narrow)
            for kept, sent in ((up_kept, up_sent), (down_kept, down_sent))
        ],
        axis=2,
    )
    tile_shape = (-1,) + summed.shape[2:]
    summed = lax.psum_scatter(summed.reshape(-1, C), "lat", scatter_dimension=0, tiled=True)
    total = lax.psum_scatter(summed, "blk", scatter_dimension=0, tiled=True)
    total = total.reshape(tile_shape)
    mixed_rows = []
    for kept, sent in mixed_parts:
        sent = other_core(sent)
        mixed_rows.append(
            jnp.concatenate(
                [jnp.where(lon == 0, kept, sent), jnp.where(lon == 0, sent, kept)], axis=2
            )
        )
    owned = small_part[:3].reshape(3, blks, chans).transpose(1, 0, 2).reshape(blks, -1)
    owned = jnp.concatenate([owned, bias_part.reshape(blks, -1)], axis=1)[:, None, :]
    grad_parts[1], mixed_rows, owned = tied(grad_parts[1], mixed_rows, owned)
    owned = send(owned, "blk")

    back_a, back_b = spread(
        [part.reshape(-1, lanes) for part in grad_parts],
        [
            pl.BlockSpec((TOKEN_STEP * SLOTS, lanes), lambda i: (jnp.minimum(i, 2), 0)),
            pl.BlockSpec((TOKEN_STEP * SLOTS, lanes), lambda i: (jnp.maximum(i - 3, 0), 0)),
        ],
        spread_kernel,
        (doubled,),
        group,
        lanes,
        narrow,
        6,
        "spread_grad",
    )
    ring_a = send(mixed_rows[0], "blk")
    blk_pieces = send_slices(mixed_rows[1], "blk")
    middle_grad = jnp.concatenate([part.reshape(-1, lanes) for part in grad_parts])
    back_a = swap_first(back_a, grid_axes)
    back_b, ring_a[1], ring_a[-1] = tied(back_b, ring_a[1], ring_a[-1])
    back_b = swap_first(back_b, grid_axes)
    back_a, *spec_sums = spectral_back(back_a, *kept_a, turn, w1, b1, w2, b2)
    back_a, back_b, owned = tied(back_a, back_b, owned)
    back_a = swap_first(back_a, grid_axes)
    back_b, spec_grads, spec_small = spectral_back(
        back_b, *kept_b, turn, w1, b1, w2, b2, tuple(spec_sums)
    )
    back_b, back_a = tied(back_b, back_a)
    back_b = swap_first(back_b, grid_axes)
    vector = jnp.concatenate([spec_small[:2].reshape(-1), sum(owned).reshape(-1)])
    vector_size, vector_rows = vector.shape[0], -(-vector.shape[0] // (BS * group))
    vector = jnp.pad(vector, (0, group * vector_rows * BS - vector_size))
    shared = jnp.concatenate(
        [spec_grads.reshape(group, -1, BS), vector.reshape(group, vector_rows, BS)], axis=1
    )
    back_a, back_b, total, shared, ring_a, blk_pieces, middle_grad = tied(
        back_a, back_b, total, shared, ring_a, blk_pieces, middle_grad
    )
    total = lax.all_gather(total, grid_axes, axis=0, tiled=False)
    ring_b = send_pieces(blk_pieces, "blk")
    shared = jnp.sum(swap_first(shared, grid_axes), axis=0)

    base_kept, base_sent, part_sums, one_small = collect_back(
        (back_a, back_b), middle_grad, field_rows, sums_rows, gain_row, ahead_back
    )
    base_kept, base_sent, part_sums, ring_b, shared = tied(
        base_kept, base_sent, part_sums, ring_b, shared
    )
    grad_sums = jnp.broadcast_to(part_sums[:, None], (lons, blks) + part_sums.shape[1:])
    grad_sums = swap_first(grad_sums.reshape((-1,) + part_sums.shape[1:]), ("lon", "blk"))
    grad_sums = jnp.sum(grad_sums.reshape((lons, blks) + part_sums.shape[1:]), axis=1)
    grad_sums = grad_sums.reshape(rows, 2, SLOTS)
    base_other = other_core(base_sent)
    mixed = to_flat((ring_a, ring_b))
    base_other, grad_sums, one_small, total, shared, mixed = tied(
        base_other, grad_sums, one_small, total, shared, mixed
    )
    up_grad, down_grad = weight_grads(total, lons, ff_here)
    own_rows = shared.shape[0]
    shared = grid_broadcast(jnp.concatenate([shared, one_small[:2].reshape(-1, BS)]))
    grad_sums, mixed, up_grad, down_grad = tied(grad_sums, mixed, up_grad, down_grad)
    input_grad = final_flat(base_kept, base_other, field_cols, sums_cols, grad_sums)

    one_small = jnp.sum(shared[:, own_rows:], axis=0).reshape(-1)
    vector = shared[:, own_rows - vector_rows : own_rows].reshape(-1)
    spec_grads = shared[:, : own_rows - vector_rows].reshape(2, 2, blocks, BS, BS)
    pieces, at = [one_small[:chans], one_small[chans:]], 0
    for size in (lanes, lanes, chans, chans, chans, ff_here):
        pieces.append(vector[at : at + size])
        at += size
    gain_one_grad, shift_one_grad, b1_grad, b2_grad = pieces[:4]
    down_bias_grad, gain_two_grad, shift_two_grad, up_bias_grad = pieces[4:]
    return (
        mixed,
        input_grad,
        gain_one_grad,
        shift_one_grad,
        spec_grads[0],
        b1_grad.reshape(spec_b1.shape),
        spec_grads[1],
        b2_grad.reshape(spec_b2.shape),
        gain_two_grad,
        shift_two_grad,
        up_grad,
        up_bias_grad,
        down_grad,
        down_bias_grad,
    )


def solution(mesh):
    placed = (
        P("lon", "blk", "lat"),
        P("blk"),
        P("blk"),
        P(None, "blk", None, None),
        P(None, "blk", None),
        P(None, "blk", None, None),
        P(None, "blk", None),
        P("blk"),
        P("blk"),
        P(None, "blk"),
        P("blk"),
        P("blk", None),
        P("blk"),
        P("lat", "lon"),
        P("lon", "blk", "lat"),
    )
    return jax.shard_map(
        per_device,
        mesh=mesh,
        in_specs=placed,
        out_specs=(
            P("lon", "blk", "lat"),
            P("lon", "blk", "lat"),
            P("blk"),
            P("blk"),
            P(None, "blk", None, None),
            P(None, "blk", None),
            P(None, "blk", None, None),
            P(None, "blk", None),
            P("blk"),
            P("blk"),
            P(None, "blk"),
            P("blk"),
            P("blk", None),
            P("blk"),
        ),
        check_vma=False,
    )
```

```python
import functools
import math

import jax
import jax.numpy as jnp
import ml_dtypes
import numpy as np
from jax import lax
from jax.experimental import pallas as pl
from jax.experimental.pallas import tpu as pltpu
from jax.sharding import PartitionSpec as P

C = 768
BS = 96
H = 90
W = 180
EPS = 1e-05
SHRINK = 0.01
SLOTS = 96
ROW_PAD = 48
VMEM = 60 << 20
wide = jnp.float32
narrow = jnp.bfloat16


def slot_columns():
    cols = np.full((2, SLOTS // 2), -1)
    cols[0, :45] = np.arange(0, 90, 2)
    cols[1, :45] = np.arange(1, 90, 2)
    return cols.reshape(-1)


def column_table(mode_total, doubled):
    cols = slot_columns()
    place = np.concatenate([cols, cols + W // 2])
    valid = np.concatenate([cols >= 0, cols >= 0])
    freq = np.arange(mode_total)
    angle = 2.0 * np.pi * (freq[:, None] * place[None, :] % W) / W
    keep = (freq <= W // 2).astype(np.float64)
    if doubled:
        keep = keep * np.where((freq == 0) | (freq == W // 2), 1.0, 2.0)
    keep = keep[:, None] * valid[None, :] / math.sqrt(W)
    return np.concatenate([np.cos(angle) * keep, -np.sin(angle) * keep], axis=0)


def row_table(rows_total, group):
    snaps = rows_total // H
    half = rows_total // group
    slot = np.arange(group * ROW_PAD)
    row = slot // ROW_PAD * half + slot % ROW_PAD
    valid = slot % ROW_PAD < half
    step, snap = row // snaps, row % snaps
    match = (snap[:, None] == snap[None, :]) & valid[:, None] & valid[None, :]
    angle = 2.0 * np.pi * (step[:, None] * step[None, :] % H) / H
    scale = match / math.sqrt(H)
    return np.concatenate([np.cos(angle) * scale, np.sin(angle) * scale], axis=0)


def split_table(table):
    high = table.astype(ml_dtypes.bfloat16)
    rest = (table - high.astype(np.float64)).astype(ml_dtypes.bfloat16)
    return jnp.asarray(high), jnp.asarray(rest)


def dot(left, right):
    return lax.dot_general(left, right, (((1,), (0,)), ((), ())), preferred_element_type=wide)


def dot_nt(left, right):
    return lax.dot_general(left, right, (((1,), (1,)), ((), ())), preferred_element_type=wide)


def dot_tn(left, right):
    return lax.dot_general(left, right, (((0,), (0,)), ((), ())), preferred_element_type=wide)


def token_sums(values):
    ones = jnp.ones((8, values.shape[1]), narrow)
    high, rest = split(values)
    return dot_nt(ones, high) + dot_nt(ones, rest)


def split(values):
    high = values.astype(narrow)
    return high, (values - high.astype(wide)).astype(narrow)


def fine_dot(table, table_rest, values):
    high, rest = split(values)
    return dot(table, high) + (dot(table, rest) + dot(table_rest, high))


def normal_parts(values):
    cumulative = 0.5 * (1.0 + lax.erf(values * (1.0 / math.sqrt(2.0))))
    density = jnp.exp(-0.5 * values * values) * (1.0 / math.sqrt(2.0 * math.pi))
    return cumulative, density


def gelu_value(values):
    return values * (0.5 * (1.0 + lax.erf(values * (1.0 / math.sqrt(2.0)))))


def gelu_slope(values):
    cumulative, density = normal_parts(values)
    return cumulative + values * density


def norm_columns(sums):
    rows = []
    for side in range(2):
        mean = sums[side, 0:1] * (1.0 / C)
        spread = sums[side, 1:2] * (1.0 / C) - mean * mean
        rows += [mean, lax.rsqrt(spread + EPS)]
    rows.append(jnp.zeros((4, SLOTS), wide))
    return jnp.transpose(jnp.concatenate(rows, axis=0))


def swap_parts(values):
    half = values.shape[1] // 2
    return jnp.concatenate([values[:, half:], values[:, :half]], axis=1)


def part_sign(shape):
    lane = lax.broadcasted_iota(jnp.int32, shape, 1)
    return jnp.where(lane < shape[1] // 2, 1.0, -1.0).astype(wide)


def lane_tiles(lanes):
    return -(-lanes // 128)


def store_modes(scratch, row, values):
    count, lanes = values.shape
    room = lane_tiles(lanes) * 128
    if room != lanes:
        values = jnp.concatenate([values, jnp.zeros((count, room - lanes), wide)], axis=1)
    for tile, ref in enumerate(scratch):
        ref[pl.ds(row, count, stride=ROW_PAD), :] = values[:, 128 * tile : 128 * (tile + 1)]


def load_modes(scratch, row, count, lanes):
    pieces = [ref[pl.ds(row, count, stride=ROW_PAD), :] for ref in scratch]
    return jnp.concatenate(pieces, axis=1)[:, :lanes]


def flush_modes(scratch, parts):
    group, _, _, lanes = parts[0].shape
    share = sum(part.shape[1] for part in parts)
    for tile, ref in enumerate(scratch):
        width = min(128, lanes - 128 * tile)
        block = ref[...].reshape(group, share, ROW_PAD, 128)
        first = 0
        for part in parts:
            last = first + part.shape[1]
            part[:, :, :, 128 * tile : 128 * tile + width] = block[
                :, first:last, :, :width
            ].astype(part.dtype)
            first = last


def fill_modes(scratch, parts):
    group, _, _, lanes = parts[0].shape
    share = sum(part.shape[1] for part in parts)
    for tile, ref in enumerate(scratch):
        width = min(128, lanes - 128 * tile)
        first = 0
        for part in parts:
            count = part.shape[1]
            block = part[:, :, :, 128 * tile : 128 * tile + width].astype(wide)
            for g in range(group):
                start = (g * share + first) * ROW_PAD
                ref[start : start + count * ROW_PAD, :width] = block[g].reshape(
                    count * ROW_PAD, width
                )
            first += count


def mode_parts(share):
    return (share - share // 2, share // 2)


def mode_scratch(mode_total, lanes):
    return [pltpu.VMEM((mode_total * ROW_PAD, 128), wide)] * lane_tiles(lanes)


def params():
    return pltpu.CompilerParams(vmem_limit_bytes=VMEM)


def cost(flops, moved):
    return pl.CostEstimate(flops=int(flops), bytes_accessed=int(moved), transcendentals=0)


def full(shape):
    return pl.BlockSpec(shape, lambda *_: (0,) * len(shape))


def once(shape, index):
    return pl.BlockSpec(shape, index, pipeline_mode=pl.Buffered(1))


def shape_of(shape, kind):
    return jax.ShapeDtypeStruct(shape, kind)


FLAT_ROWS = 18


def from_flat_kernel(with_sums, flat, out, *rest):
    scratch = rest[-1]
    scratch[...] = flat[0].astype(wide).reshape(scratch.shape)
    empty = jnp.zeros((3, 192), wide)
    for q in range(FLAT_ROWS):
        first = scratch[pl.ds(135 * q, 45, stride=3), :]
        second = scratch[pl.ds(135 * q + 1, 45, stride=3), :]
        third = scratch[pl.ds(135 * q + 2, 45, stride=3), :]
        even = jnp.concatenate([first, second[:, :64]], axis=1)
        odd = jnp.concatenate([second[:, 64:], third], axis=1)
        tile = jnp.concatenate([even, empty, odd, empty], axis=0)
        out[q] = tile.astype(narrow)
        if with_sums:
            total, total_sq = token_sums(tile), token_sums(tile * tile)
            rest[0][q] = jnp.concatenate([total[:1], total_sq[:1]], axis=0)


def from_flat(flat, rows, chans, with_sums):
    if chans != 192:
        grid = flat.reshape(rows, 45, 2, chans).transpose(0, 2, 1, 3)
        grid = jnp.pad(grid, ((0, 0), (0, 0), (0, 3), (0, 0))).reshape(rows, SLOTS, chans)
        if not with_sums:
            return grid
        wider = grid.astype(wide)
        return grid, jnp.stack([jnp.sum(wider, axis=2), jnp.sum(wider * wider, axis=2)], axis=1)
    block = FLAT_ROWS * 90 * chans
    out_specs = [pl.BlockSpec((FLAT_ROWS, SLOTS, chans), lambda i: (i, 0, 0))]
    out_shape = [shape_of((rows, SLOTS, chans), narrow)]
    if with_sums:
        out_specs.append(pl.BlockSpec((FLAT_ROWS, 2, SLOTS), lambda i: (i, 0, 0)))
        out_shape.append(shape_of((rows, 2, SLOTS), wide))
    outs = pl.pallas_call(
        functools.partial(from_flat_kernel, with_sums),
        grid=(rows // FLAT_ROWS,),
        in_specs=[pl.BlockSpec((1, 1, block), lambda i: (0, 0, i))],
        out_specs=out_specs,
        out_shape=out_shape,
        scratch_shapes=[pltpu.VMEM((block // 128, 128), wide)],
        compiler_params=params(),
        cost_estimate=cost(1e6, 1e5),
        name="from_flat",
    )(flat)
    return outs if with_sums else outs[0]


def write_flat(scratch, row, tile):
    even, odd = tile[0:45], tile[48:93]
    scratch[pl.ds(135 * row, 45, stride=3), :] = even[:, :128]
    scratch[pl.ds(135 * row + 1, 45, stride=3), :] = jnp.concatenate(
        [even[:, 128:], odd[:, :64]], axis=1
    )
    scratch[pl.ds(135 * row + 2, 45, stride=3), :] = odd[:, 64:]


PAIR_ROWS = 9


def place_pieces(blk, pieces, out):
    first, size = 0, len(pieces) // 2
    for half in (pieces[:size], pieces[size:]):
        share = half[0].shape[0]
        for by, piece in enumerate(half):
            place = first + lax.rem(blk + size - by, size) * share
            out[pl.ds(pl.multiple_of(place, 16), share), :] = piece[...]
        first += size * share


def to_flat_kernel(blk, *refs):
    *pieces, flat, rows, scratch = refs
    chans = rows.shape[1] // 2
    second = pl.program_id(0) == 1
    step = pl.program_id(1)

    @pl.when(jnp.logical_not(second) & (step == 0))
    def _():
        place_pieces(blk[0], pieces, rows)

    for q in range(PAIR_ROWS):
        start = pl.multiple_of((step * PAIR_ROWS + q) * SLOTS, SLOTS)
        pair = rows[pl.ds(start, SLOTS), :].astype(wide)
        write_flat(scratch, q, jnp.where(second, pair[:, chans:], pair[:, :chans]))
    flat[0] = scratch[...].reshape(1, scratch.shape[0] * 128).astype(flat.dtype)


def plain_flat(grid):
    rows, _, chans = grid.shape
    kept = grid.reshape(rows, 2, SLOTS // 2, chans)[:, :, :45].transpose(0, 2, 1, 3)
    return kept.reshape(1, 1, rows * 90 * chans)


def to_flat(halves):
    pieces = [piece for half in halves for piece in half]
    chans = pieces[0].shape[1] // 2
    if chans != 192:
        pairs = in_order(halves)
        grid = pairs[: 45 * SLOTS].reshape(45, SLOTS, 2, chans).transpose(2, 0, 1, 3)
        return plain_flat(grid.reshape(90, SLOTS, chans))
    block = PAIR_ROWS * 90 * chans
    steps = 45 // PAIR_ROWS
    tokens = sum(piece.shape[0] for piece in pieces)
    return pl.pallas_call(
        to_flat_kernel,
        grid_spec=pltpu.PrefetchScalarGridSpec(
            num_scalar_prefetch=1,
            grid=(2, steps),
            in_specs=[once(piece.shape, lambda *_: (0, 0)) for piece in pieces],
            out_specs=pl.BlockSpec((1, 1, block), lambda h, i, at: (0, 0, h * steps + i)),
            scratch_shapes=[
                pltpu.VMEM((tokens, 2 * chans), narrow),
                pltpu.VMEM((block // 128, 128), wide),
            ],
        ),
        out_shape=shape_of((1, 1, 90 * 90 * chans), narrow),
        compiler_params=params(),
        cost_estimate=cost(1e6, 1e5),
        name="to_flat",
    )(lax.axis_index("blk").astype(jnp.int32).reshape(1), *pieces)


def final_tile(base, field, sums, grad_sums):
    mean = sums[0:1] * (1.0 / C)
    spread = sums[1:2] * (1.0 / C) - mean * mean
    inverse = lax.rsqrt(spread + EPS)
    shift = inverse * grad_sums[0:1] * (1.0 / C)
    slope = inverse * inverse * grad_sums[1:2] * (1.0 / C)
    cols = jnp.transpose(
        jnp.concatenate([mean * slope - shift, slope, jnp.zeros((6, SLOTS), wide)], axis=0)
    )
    return (base + cols[:, 0:1]) - field.astype(wide) * cols[:, 1:2]


FINAL_ROWS = 15


def final_kernel(place, kept, other, field, sums, grad_sums, flat, *scratch):
    own = pl.program_id(0) // (45 // FINAL_ROWS) == place[0]
    for q in range(FINAL_ROWS):
        base = jnp.where(own, kept[q], other[q])
        tile = final_tile(base, field[q], sums[q], grad_sums[q])
        if scratch:
            write_flat(scratch[0], q, tile)
        else:
            flat[q] = tile
    if scratch:
        flat[0] = scratch[0][...].reshape(1, scratch[0].shape[0] * 128)


def final_flat(kept, other, field, sums, grad_sums):
    rows, _, chans = field.shape
    steps = 45 // FINAL_ROWS
    block = FINAL_ROWS * 90 * chans

    def half_of(which):
        def index(i, at):
            first = steps * (at[0] if which == 0 else 1 - at[0])
            return (jnp.clip(i - first, 0, steps - 1), 0, 0)

        return pl.BlockSpec((FINAL_ROWS, SLOTS, chans), index)

    tiles = pl.BlockSpec((FINAL_ROWS, SLOTS, chans), lambda i, at: (i, 0, 0))
    pairs = pl.BlockSpec((FINAL_ROWS, 2, SLOTS), lambda i, at: (i, 0, 0))
    simple = chans != 192
    out = pl.pallas_call(
        final_kernel,
        grid_spec=pltpu.PrefetchScalarGridSpec(
            num_scalar_prefetch=1,
            grid=(2 * steps,),
            in_specs=[half_of(0), half_of(1), tiles, pairs, pairs],
            out_specs=tiles if simple else pl.BlockSpec((1, 1, block), lambda i, at: (0, 0, i)),
            scratch_shapes=[] if simple else [pltpu.VMEM((block // 128, 128), wide)],
        ),
        out_shape=shape_of(field.shape if simple else (1, 1, rows * 90 * chans), wide),
        compiler_params=params(),
        cost_estimate=cost(1e6, 1e5),
        name="final_flat",
    )(lax.axis_index("lon").astype(jnp.int32).reshape(1), kept, other, field, sums, grad_sums)
    return plain_flat(out) if simple else out


STEP = 9
TOKEN_STEP = 8
TOKEN_HALVES = ((0, 24), (24, 21))


def spread_norm_kernel(field, sums, gain, shift, table, table_rest, out_a, out_b, *scratch):
    step = pl.program_id(0)
    for q in range(STEP):
        cols = norm_columns(sums[:, q])
        sides = []
        for side in range(2):
            centered = field[side, q].astype(wide) - cols[:, 2 * side : 2 * side + 1]
            normed = centered * cols[:, 2 * side + 1 : 2 * side + 2] * gain[...] + shift[...]
            sides.append(normed)
        modes = fine_dot(table[...], table_rest[...], jnp.concatenate(sides, axis=0))
        count = modes.shape[0] // 2
        store_modes(
            scratch, step * STEP + q, jnp.concatenate([modes[:count], modes[count:]], axis=1)
        )
    finish_spread(step, scratch, (out_a, out_b))


def spread_kernel(first, second, table, out_a, out_b, *scratch):
    step = pl.program_id(0)
    from_first = step < TOKEN_HALVES[0][1] // TOKEN_STEP
    for q in range(TOKEN_STEP):
        row = step * TOKEN_STEP + q
        rows = slice(q * SLOTS, (q + 1) * SLOTS)
        pair = jnp.where(from_first, first[rows, :], second[rows, :])
        chans = pair.shape[1] // 2
        modes = dot(table[...], jnp.concatenate([pair[:, :chans], pair[:, chans:]], axis=0))
        count = modes.shape[0] // 2
        modes = jnp.concatenate([modes[:count], modes[count:]], axis=1)
        store_modes(scratch, row, jnp.where(row < 45, modes, 0.0))

    @pl.when(step == pl.num_programs(0) - 1)
    def _():
        flush_modes(scratch, (out_a, out_b))


def finish_spread(step, scratch, out):
    @pl.when(step == 0)
    def _():
        count = scratch[0].shape[0] // ROW_PAD
        for row in range(45, ROW_PAD):
            for ref in scratch:
                ref[pl.ds(row, count, stride=ROW_PAD), :] = jnp.zeros((count, 128), wide)

    @pl.when(step == pl.num_programs(0) - 1)
    def _():
        flush_modes(scratch, out)


def spread(inputs, in_specs, kernel, tables, group, lanes, kind, steps, name):
    mode_total = tables[0].shape[0] // 2
    outs = [(group, count, ROW_PAD, lanes) for count in mode_parts(mode_total // group)]
    return pl.pallas_call(
        kernel,
        grid=(steps,),
        in_specs=in_specs + [full(table.shape) for table in tables],
        out_specs=[full(out) for out in outs],
        out_shape=[shape_of(out, kind) for out in outs],
        scratch_shapes=mode_scratch(mode_total, lanes),
        compiler_params=params(),
        cost_estimate=cost(1e6, 1e5),
        name=name,
    )(*inputs, *tables)


def collect_kernel(first, modes_a, modes_b, field, sums, gain, shift, table, out, *scratch):
    step = pl.program_id(0)

    @pl.when(step == 0)
    def _():
        fill_modes(scratch, (modes_a, modes_b))

    for q in range(TOKEN_STEP):
        row = first + step * TOKEN_STEP + q
        spatial = spatial_rows(scratch, row, table, modes_a.shape[3])
        cols = norm_columns(sums[:, q])
        sides = []
        for side in range(2):
            centered = field[side, q].astype(wide) - cols[:, 2 * side : 2 * side + 1]
            normed = centered * cols[:, 2 * side + 1 : 2 * side + 2] * gain[...] + shift[...]
            sides.append(spatial[side] + normed + centered)
        pair = jnp.where(row < 45, jnp.concatenate(sides, axis=1), 0.0)
        out[q * SLOTS : (q + 1) * SLOTS, :] = pair.astype(narrow)


def spatial_rows(scratch, row, table, lanes):
    count = table.shape[1] // 2
    pair = load_modes(scratch, row, count, lanes).astype(narrow)
    stacked = jnp.concatenate([pair[:, : lanes // 2], pair[:, lanes // 2 :]], axis=0)
    spatial = dot(table[...], stacked)
    return spatial[:SLOTS], spatial[SLOTS:]


def collect(modes, field, sums, gain, shift, table, rows, tokens):
    chans = field.shape[3]
    first, count = rows
    skip = first // TOKEN_STEP
    mode_total = table.shape[1] // 2
    return pl.pallas_call(
        functools.partial(collect_kernel, first),
        grid=(-(-count // TOKEN_STEP),),
        in_specs=[full(part.shape) for part in modes]
        + [
            pl.BlockSpec((2, TOKEN_STEP, SLOTS, chans), lambda i: (0, i + skip, 0, 0)),
            pl.BlockSpec((2, TOKEN_STEP, 2, SLOTS), lambda i: (0, i + skip, 0, 0)),
            full(gain.shape),
            full(shift.shape),
            full(table.shape),
        ],
        out_specs=pl.BlockSpec((TOKEN_STEP * SLOTS, 2 * chans), lambda i: (i, 0)),
        out_shape=shape_of((tokens, 2 * chans), narrow),
        scratch_shapes=mode_scratch(mode_total, 2 * chans),
        compiler_params=params(),
        cost_estimate=cost(1e6, 1e5),
        name="collect_norm",
    )(*modes, field, sums, gain, shift, table)


def collect_back_kernel(
    place, modes_a, modes_b, grad, field, sums, gain, table, kept, sent, parts, small, *scratch
):
    step = pl.program_id(0)

    @pl.when(step == 0)
    def _():
        fill_modes(scratch, (modes_a, modes_b))
        small[...] = jnp.zeros(small.shape, wide)

    gain_sum = jnp.zeros((1, gain.shape[1]), wide)
    shift_sum = jnp.zeros((1, gain.shape[1]), wide)
    for q in range(STEP):
        spatial = spatial_rows(scratch, step * STEP + q, table, modes_a.shape[3])
        cols = norm_columns(sums[:, q])
        pair = grad[q * SLOTS : (q + 1) * SLOTS, :].astype(wide)
        chans = pair.shape[1] // 2
        bases = []
        for side in range(2):
            inverse = cols[:, 2 * side + 1 : 2 * side + 2]
            normed = (field[side, q].astype(wide) - cols[:, 2 * side : 2 * side + 1]) * inverse
            middle = pair[:, side * chans : (side + 1) * chans]
            total = middle + spatial[side]
            scaled = total * gain[...]
            bases.append(middle + inverse * scaled)
            turned = scaled * normed
            parts[side, q] = jnp.concatenate(
                [token_sums(scaled)[:1], token_sums(turned)[:1]], axis=0
            )
            gain_sum = gain_sum + jnp.sum(total * normed, axis=0, keepdims=True)
            shift_sum = shift_sum + jnp.sum(total, axis=0, keepdims=True)
        kept[q] = jnp.where(place[0] == 0, bases[0], bases[1])
        sent[q] = jnp.where(place[0] == 0, bases[1], bases[0])
    small[0:1] += gain_sum
    small[1:2] += shift_sum


def collect_back(modes, grad, field, sums, gain, table):
    chans = field.shape[3]
    mode_total = table.shape[1] // 2
    half_rows = pl.BlockSpec((STEP, SLOTS, chans), lambda i, at: (i, 0, 0))
    pair_sums = pl.BlockSpec((2, STEP, 2, SLOTS), lambda i, at: (0, i, 0, 0))
    return pl.pallas_call(
        collect_back_kernel,
        grid_spec=pltpu.PrefetchScalarGridSpec(
            num_scalar_prefetch=1,
            grid=(45 // STEP,),
            in_specs=[
                *[full(part.shape) for part in modes],
                pl.BlockSpec((STEP * SLOTS, 2 * chans), lambda i, at: (i, 0)),
                pl.BlockSpec((2, STEP, SLOTS, chans), lambda i, at: (0, i, 0, 0)),
                pair_sums,
                full(gain.shape),
                full(table.shape),
            ],
            out_specs=[half_rows, half_rows, pair_sums, full((8, chans))],
            scratch_shapes=mode_scratch(mode_total, 2 * chans),
        ),
        out_shape=[
            shape_of(field.shape[1:], wide),
            shape_of(field.shape[1:], wide),
            shape_of(sums.shape, wide),
            shape_of((8, chans), wide),
        ],
        compiler_params=params(),
        cost_estimate=cost(1e6, 1e5),
        name="collect_back",
    )(lax.axis_index("lon").astype(jnp.int32).reshape(1), *modes, grad, field, sums, gain, table)


def turn_rows(both):
    count = both.shape[0] // 2
    turned = swap_parts(both[count:])
    return both[:count] + turned * part_sign(turned.shape)


def return_rows(table, values):
    both = dot(table[...], values.astype(narrow))
    count = both.shape[0] // 2
    turned = swap_parts(both[count:])
    return both[:count] - turned * part_sign(turned.shape)


def shrink_bend(values):
    return jnp.tanh(values * (1.0 / SHRINK))


def spectral_kernel(modes, table, table_rest, w1, b1, w2, b2, out, low, act):
    rows = modes.shape[0] * ROW_PAD
    lanes = modes.shape[3]
    exact = fine_dot(table[...], table_rest[...], modes[...].reshape(rows, lanes))
    coarse = turn_rows(exact).astype(narrow)
    low[0] = coarse
    bent = gelu_value(dot(coarse, w1[...]) + b1[...]).astype(narrow)
    act[0] = bent
    second = dot(bent, w2[...]) + b2[...]
    shrunk = second - SHRINK * shrink_bend(second)
    out[...] = return_rows(table, shrunk).astype(narrow).reshape(out.shape)


def spectral(modes, table, table_rest, w1, b1, w2, b2):
    group, share, _, lanes = modes.shape
    rows = group * ROW_PAD
    mode_block = pl.BlockSpec((group, 1, ROW_PAD, lanes), lambda i: (0, i, 0, 0))
    kept_block = pl.BlockSpec((1, rows, lanes), lambda i: (i, 0, 0))
    return pl.pallas_call(
        spectral_kernel,
        grid=(share,),
        in_specs=[mode_block] + [full(x.shape) for x in (table, table_rest, w1, b1, w2, b2)],
        out_specs=[mode_block, kept_block, kept_block],
        out_shape=[
            shape_of(modes.shape, narrow),
            shape_of((share, rows, lanes), narrow),
            shape_of((share, rows, lanes), narrow),
        ],
        compiler_params=params(),
        cost_estimate=cost(1e6, 1e5),
        name="spectral",
    )(modes, table, table_rest, w1, b1, w2, b2)


def spectral_back_kernel(modes, low, act, table, w1, b1, w2, b2, *rest):
    before, (out, *outs) = rest[: -4 - bool(len(rest) > 4)], rest[-4 - bool(len(rest) > 4) :]
    second_part = bool(before)
    grads, (small, g1, g2) = (outs[0] if second_part else None), outs[-3:]
    rows = modes.shape[0] * ROW_PAD
    lanes = modes.shape[3]

    @pl.when(pl.program_id(0) == 0)
    def _():
        for k, ref in enumerate((small, g1, g2)):
            ref[...] = before[k][...] if second_part else jnp.zeros(ref.shape, wide)

    back = turn_rows(dot(table[...], modes[...].reshape(rows, lanes)))
    bent = act[0]
    bend = shrink_bend(dot(bent, w2[...]) + b2[...])
    second = (back * (bend * bend)).astype(narrow)
    g2[...] += dot_tn(bent, second)
    small[1:2] += jnp.sum(second.astype(wide), axis=0, keepdims=True)
    coarse = low[0]
    slope = gelu_slope(dot(coarse, w1[...]) + b1[...])
    first = (dot_nt(second, w2[...]) * slope).astype(narrow)
    g1[...] += dot_tn(coarse, first)
    small[0:1] += jnp.sum(first.astype(wide), axis=0, keepdims=True)
    out[...] = return_rows(table, dot_nt(first, w1[...])).astype(narrow).reshape(out.shape)
    if not second_part:
        return

    @pl.when(pl.program_id(0) == pl.num_programs(0) - 1)
    def _():
        half = lanes // 2
        at = 0
        for outer in (g1[...], g2[...]):
            for part in (
                outer[:half, :half] + outer[half:, half:],
                outer[:half, half:] - outer[half:, :half],
            ):
                for j in range(half // BS):
                    block = slice(j * BS, (j + 1) * BS)
                    grads[at : at + BS, :] = part[block, block]
                    at += BS


def spectral_back(modes, low, act, table, w1, b1, w2, b2, before=()):
    group, share, _, lanes = modes.shape
    rows = group * ROW_PAD
    mode_block = pl.BlockSpec((group, 1, ROW_PAD, lanes), lambda i: (0, i, 0, 0))
    kept_block = pl.BlockSpec((1, rows, lanes), lambda i: (i, 0, 0))
    sums = [shape_of((8, lanes), wide)] + [shape_of((lanes, lanes), wide)] * 2
    outs = [shape_of(modes.shape, narrow)]
    scratch = []
    if before:
        outs += [shape_of((2 * lanes, BS), wide), sums[0]]
        scratch = [pltpu.VMEM(sums[1].shape, wide)] * 2
    else:
        outs += sums
    return pl.pallas_call(
        spectral_back_kernel,
        grid=(share,),
        in_specs=[mode_block, kept_block, kept_block]
        + [full(x.shape) for x in (table, w1, b1, w2, b2, *before)],
        out_specs=[mode_block] + [full(out.shape) for out in outs[1:]],
        out_shape=outs,
        scratch_shapes=scratch,
        compiler_params=params(),
        cost_estimate=cost(1e6, 1e5),
        name="spectral_back",
    )(modes, low, act, table, w1, b1, w2, b2, *before)


def block_matrix_kernel(w1, w2, out1, out2):
    for weight, out in ((w1, out1), (w2, out2)):
        blocks = weight.shape[1]
        empty = jnp.zeros((BS, BS), wide)
        rows = []
        for part in range(2):
            for block in range(blocks):
                real, imag = weight[0, block].astype(wide), weight[1, block].astype(wide)
                pair = (real, imag) if part == 0 else (-imag, real)
                rows.append(
                    jnp.concatenate(
                        [piece if k == block else empty for piece in pair for k in range(blocks)],
                        axis=1,
                    )
                )
        out[...] = jnp.concatenate(rows, axis=0).astype(narrow)


def block_matrices(w1, w2):
    lanes = 2 * w1.shape[1] * BS
    return pl.pallas_call(
        block_matrix_kernel,
        out_shape=[shape_of((lanes, lanes), narrow)] * 2,
        compiler_params=params(),
        cost_estimate=cost(1e6, 1e5),
        name="block_matrices",
    )(w1, w2)


FF_TILE = 256
CHUNKS = 4


def token_tile(values, side, start, count):
    chans = values[0].shape[2] // 2
    return jnp.concatenate(
        [
            source[0, pl.ds(start, count), side * chans : (side + 1) * chans]
            for source in values
        ],
        axis=1,
    ).astype(wide)


def norm_two(values):
    mean = jnp.mean(values, axis=1, keepdims=True)
    offset = values - mean
    inverse = lax.rsqrt(jnp.mean(offset * offset, axis=1, keepdims=True) + EPS)
    return offset * inverse, mean, inverse


def mlp_kernel(
    tile,
    blks,
    place,
    *refs,
):
    middle, pieces = refs[:blks], refs[blks : 2 * blks]
    *refs, cot_all = refs[2 * blks :]

    @pl.when(pl.program_id(0) == 0)
    def _():
        for by, piece in enumerate(pieces):
            cot_all[pl.ds(lax.rem(place[0] + blks - by, blks), 1)] = piece[...][None]

    cot = [cot_all.at[pl.ds(b, 1)] for b in range(blks)]
    mlp_body(tile, place, middle, cot, *refs[:3], refs[3:5], refs[5:7], *refs[7:])


def mlp_body(
    tile,
    here,
    middle,
    cot,
    cols,
    gain,
    shift,
    ups,
    downs,
    up_bias,
    down_bias,
    *rest,
):
    before_refs = rest[:-14]
    mixed_kept, mixed_sent, middle_grad = rest[-14:-11]
    weight_grads, (bias_grad, small) = rest[-11:-7], rest[-7:-5]
    tokens_in, grads_in, branch, grad_sum, norm_cols = rest[-5:]
    first_core = here[1] == 0
    step = pl.program_id(0)
    share = middle[0].shape[1]
    pieces = share // tile

    @pl.when(step == 0)
    def _():
        small[...] = before_refs[5][...] if before_refs else jnp.zeros(small.shape, wide)
        for side in range(2):

            @pl.loop(0, pieces)
            def _(piece):
                start = pl.multiple_of(piece * tile, 16)
                place = pl.ds(pl.multiple_of(side * share + piece * tile, 16), tile)
                normed, mean, inverse = norm_two(token_tile(middle, side, start, tile))
                norm_cols[place, 0:1] = mean
                norm_cols[place, 1:2] = inverse
                tokens_in[place, :] = (normed * gain[...] + shift[...]).astype(narrow)
                weight = cols[place, 1:2]
                grad = (token_tile(cot, side, start, tile) * weight).astype(narrow)
                grads_in[place, :] = grad
                small[0:1] += jnp.sum(grad.astype(wide), axis=0, keepdims=True)
                branch[place, :] = jnp.zeros((tile, C), wide)
                grad_sum[place, :] = jnp.zeros((tile, C), wide)

    up_tile = jnp.where(first_core, ups[0][0], ups[1][0])
    down_tile = jnp.where(first_core, downs[1][0], downs[0][0])
    tokens, grads = tokens_in[...], grads_in[...]
    count = tokens.shape[0]
    piece = count // CHUNKS
    hidden, before_grad = [], []
    for c in range(CHUNKS):
        place = slice(c * piece, (c + 1) * piece)
        before = dot(tokens[place], up_tile) + up_bias[...]
        into = dot_nt(grads[place], down_tile)
        cumulative, density = normal_parts(before)
        hidden.append((before * cumulative).astype(narrow))
        before_grad.append((into * (cumulative + before * density)).astype(narrow))
    hidden, before_grad = jnp.concatenate(hidden, axis=0), jnp.concatenate(before_grad, axis=0)
    branch[...] += dot(hidden, down_tile)
    grad_sum[...] += dot_nt(before_grad, up_tile)
    rows = up_tile.shape[1] // 2
    for which, total in enumerate((dot_tn(before_grad, tokens), dot_tn(hidden, grads))):
        first, second = (
            half.reshape(weight_grads[0].shape) for half in (total[:rows], total[rows:])
        )
        parts = (
            jnp.where(first_core, first, second),
            jnp.where(first_core, second, first),
        )
        for k, part in enumerate(parts):
            if before_refs:
                part = part + before_refs[2 * which + k][...].astype(wide)
            weight_grads[2 * which + k][...] = part.astype(narrow)
    bias_total = jnp.sum(before_grad.astype(wide), axis=0, keepdims=True)
    bias_grad[...] = bias_total + before_refs[4][...] if before_refs else bias_total

    @pl.when(step == pl.num_programs(0) - 1)
    def _():
        for side in range(2):

            @pl.loop(0, pieces)
            def _(piece):
                start = pl.multiple_of(piece * tile, 16)
                place = pl.ds(pl.multiple_of(side * share + piece * tile, 16), tile)
                values = token_tile(middle, side, start, tile)
                inverse = norm_cols[place, 1:2]
                normed = (values - norm_cols[place, 0:1]) * inverse
                result = (
                    values + cols[place, 0:1] + (branch[place, :] + down_bias[...])
                ).astype(narrow)
                grad = grad_sum[place, :]
                small[1:2] += jnp.sum(grad * normed, axis=0, keepdims=True)
                small[2:3] += jnp.sum(grad, axis=0, keepdims=True)
                scaled = grad * gain[...]
                back = inverse * (
                    scaled
                    - jnp.mean(scaled, axis=1, keepdims=True)
                    - normed * jnp.mean(scaled * normed, axis=1, keepdims=True)
                )
                whole = token_tile(cot, side, start, tile) * cols[place, 1:2] + back
                whole = whole.astype(narrow)
                chans = middle[0].shape[2] // 2

                def put(out):
                    for b in range(len(middle)):
                        out[b, pl.ds(start, tile), :] = result[:, b * chans : (b + 1) * chans]

                pl.when(here[1] == side)(lambda: put(mixed_kept))
                pl.when(here[1] != side)(lambda: put(mixed_sent))
                for b in range(len(middle)):
                    lanes = slice(side * chans, (side + 1) * chans)
                    middle_grad[b, pl.ds(start, tile), lanes] = whole[
                        :, b * chans : (b + 1) * chans
                    ]


def mlp(middle, cot, cols, gain, shift, weights, up_bias, down_bias, before):
    blks, share, lanes = middle.shape
    count = 2 * share
    ff_here = weights[0].shape[2]
    per = ff_here // FF_TILE if ff_here % FF_TILE == 0 else 1
    width = ff_here // per
    tile = share
    by_source = [
        once((1, share, lanes), lambda i, at, b=b: (b, 0, 0)) for b in range(blks)
    ]
    by_ring = [once((share, lanes), lambda i, at: (0, 0))] * blks
    lats = lax.axis_size("lat")
    grad_shape = (lats, blks * per, width // 2 // lats, C)
    grad_out = pl.BlockSpec((lats, 1) + grad_shape[2:], lambda i, at: (0, i, 0, 0))
    bias_out = pl.BlockSpec((1, width), lambda i, at: (0, i))
    down_weights = [part.reshape(blks, ff_here, C) for part in weights]
    return pl.pallas_call(
        functools.partial(mlp_kernel, tile, blks),
        grid_spec=pltpu.PrefetchScalarGridSpec(
            num_scalar_prefetch=1,
            grid=(blks * per,),
            in_specs=by_source
            + by_ring
            + [
                full(cols.shape),
                full(gain.shape),
                full(shift.shape),
                *[pl.BlockSpec((1, C, width), lambda i, at: (i // per, 0, i % per))] * 2,
                *[pl.BlockSpec((1, width, C), lambda i, at: (i // per, i % per, 0))] * 2,
                bias_out,
                full(down_bias.shape),
            ]
            + ([grad_out] * 4 + [bias_out, full((8, C))] if before else []),
            out_specs=[
                full((blks, share, lanes // 2)),
                full((blks, share, lanes // 2)),
                full(middle.shape),
                *[grad_out] * 4,
                bias_out,
                full((8, C)),
            ],
            scratch_shapes=[
                pltpu.VMEM((count, C), narrow),
                pltpu.VMEM((count, C), narrow),
                pltpu.VMEM((count, C), wide),
                pltpu.VMEM((count, C), wide),
                pltpu.VMEM((count, 2), wide),
                pltpu.VMEM(middle.shape, narrow),
            ],
        ),
        out_shape=[
            shape_of((blks, share, lanes // 2), narrow),
            shape_of((blks, share, lanes // 2), narrow),
            shape_of(middle.shape, narrow),
            *[shape_of(grad_shape, narrow)] * 4,
            shape_of((1, blks * ff_here), wide),
            shape_of((8, C), wide),
        ],
        compiler_params=params(),
        cost_estimate=cost(1e6, 1e5),
        name="channel_mlp",
    )(
        jnp.stack([lax.axis_index("blk"), lax.axis_index("lon")]).astype(jnp.int32),
        *([middle] * blks),
        *cot,
        cols,
        gain,
        shift,
        *weights,
        *down_weights,
        up_bias,
        down_bias,
        *before,
    )


def weight_grads_kernel(pieces, up, down):
    lats, lons, tiles = pieces.shape[:3]
    for which, out in ((0, up), (1, down)):
        rows = [
            pieces[lat, lon, tile, which]
            for tile in range(tiles)
            for lon in range(lons)
            for lat in range(lats)
        ]
        grad = jnp.concatenate(rows, axis=0).astype(wide)
        out[...] = jnp.transpose(grad) if which == 0 else grad


def weight_grads(pieces, lons, ff_here):
    pieces = pieces.reshape((-1, lons) + pieces.shape[1:])
    return pl.pallas_call(
        weight_grads_kernel,
        out_shape=[shape_of((C, ff_here), wide), shape_of((ff_here, C), wide)],
        compiler_params=params(),
        cost_estimate=cost(1e6, 1e5),
        name="weight_grads",
    )(pieces)


def swap_first(values, axes):
    return lax.all_to_all(values, axes, split_axis=0, concat_axis=0, tiled=True)


def shifted(values, axis, by):
    size = lax.axis_size(axis)
    return lax.ppermute(values, axis, [(i, (i + by) % size) for i in range(size)])


def other_core(values):
    return lax.ppermute(values, "lon", [(0, 1), (1, 0)])


def pick(values, index):
    return lax.dynamic_index_in_dim(values, index, 0, keepdims=False)


def ring(values, axis):
    return [values] + [shifted(values, axis, by) for by in range(1, lax.axis_size(axis))]


def send_slices(values, axis):
    size, here = lax.axis_size(axis), lax.axis_index(axis)
    return [pick(values, here)] + [pick(values, (here + by) % size) for by in range(1, size)]


def send_pieces(pieces, axis):
    return pieces[:1] + [shifted(piece, axis, by) for by, piece in enumerate(pieces) if by]


def send(values, axis):
    return send_pieces(send_slices(values, axis), axis)


def in_order(halves):
    size, blk = len(halves[0]), lax.axis_index("blk")
    lanes = halves[0][0].shape[1]
    out = jnp.zeros((sum(size * half[0].shape[0] for half in halves), lanes), halves[0][0].dtype)
    first = 0
    for half in halves:
        share = half[0].shape[0]
        for by, piece in enumerate(half):
            place = first + (blk - by) % size * share
            out = lax.dynamic_update_slice_in_dim(out, piece, place, 0)
        first += size * share
    return out


def lat_broadcast(values):
    count = lax.axis_size("lat")
    return swap_first(jnp.broadcast_to(values[None], (count,) + values.shape), "lat")


def grid_broadcast(values):
    count = lax.axis_size("lat") * lax.axis_size("lon")
    return swap_first(jnp.broadcast_to(values[None], (count,) + values.shape), ("lat", "lon"))


def tied(*values):
    return lax.optimization_barrier(values)


def per_device(
    field,
    gain_one,
    shift_one,
    spec_w1,
    spec_b1,
    spec_w2,
    spec_b2,
    gain_two,
    shift_two,
    up_weight,
    up_bias,
    down_weight,
    down_bias,
    presence,
    cotangent,
):
    rows, cols = presence.shape
    chans = gain_one.shape[0]
    lats, lons, blks = (lax.axis_size(name) for name in ("lat", "lon", "blk"))
    blk, lon = lax.axis_index("blk"), lax.axis_index("lon")
    grid_axes = ("lat", "lon")
    group = lats * lons
    half = rows // lons
    blocks = spec_w1.shape[1]
    mode_total = (W // 2 + group) // group * group
    lanes = 2 * chans
    ff_here = up_bias.shape[0]
    ahead, ahead_rest = split_table(column_table(mode_total, False))
    ahead_back, _ = split_table(column_table(mode_total, False).T)
    doubled, _ = split_table(column_table(mode_total, True))
    doubled_back, _ = split_table(column_table(mode_total, True).T)
    turn, turn_rest = split_table(row_table(rows * lats, group))
    gain_row, shift_row = gain_one[None, :], shift_one[None, :]

    weight_own = jnp.where(lon == 0, up_weight, down_weight.reshape(up_weight.shape))
    weights = lax.all_gather(weight_own, "blk", axis=0, tiled=False)

    field_cols, sums_part = from_flat(field, rows, chans, True)
    row_params = jnp.concatenate([up_bias.astype(wide), down_bias, gain_two, shift_two])
    param_count = row_params.shape[0]
    row_params = jnp.pad(row_params, (0, -param_count % (2 * SLOTS))).reshape(-1, 2, SLOTS)
    sums_ring = ring(jnp.concatenate([sums_part, row_params]), "blk")
    field_rows = swap_first(field_cols.reshape(2, half, SLOTS, chans), "lon")
    field_rows, *sums_ring = tied(field_rows, *sums_ring)
    sums_cols = sum(piece[:rows] for piece in sums_ring)
    seen = presence.reshape(rows, 45, 2).transpose(0, 2, 1)
    seen = jnp.pad(seen, ((0, 0), (0, 0), (0, 3))).reshape(rows, 1, SLOTS).astype(wide)
    scalars = jnp.concatenate([sums_cols, seen], axis=1).reshape(2, half, 3, SLOTS)
    scalars = swap_first(scalars, "lon")
    sums_rows = scalars[:, :, :2]

    modes_a, modes_b = spread(
        (field_rows, sums_rows, gain_row, shift_row),
        [
            pl.BlockSpec((2, STEP, SLOTS, chans), lambda i: (0, i, 0, 0)),
            pl.BlockSpec((2, STEP, 2, SLOTS), lambda i: (0, i, 0, 0)),
            full(gain_row.shape),
            full(shift_row.shape),
        ],
        spread_norm_kernel,
        (ahead, ahead_rest),
        group,
        lanes,
        wide,
        45 // STEP,
        "spread_norm",
    )
    cotangent, modes_a, modes_b = tied(cotangent, modes_a, modes_b)
    modes_a = swap_first(modes_a, grid_axes)
    cot_cols = from_flat(cotangent, rows, chans, False).reshape(2, half, SLOTS, chans)
    cot_own, cot_other = pick(cot_cols, lon), other_core(pick(cot_cols, 1 - lon))
    cot_pairs = jnp.concatenate(
        [jnp.where(lon == 0, cot_own, cot_other), jnp.where(lon == 0, cot_other, cot_own)], axis=2
    )
    padded = half * SLOTS
    halves = [
        (first * SLOTS, -(-count * SLOTS // (blks * 16)) * 16) for first, count in TOKEN_HALVES
    ]
    tokens = blks * sum(share for _, share in halves)
    cot_pairs = jnp.pad(cot_pairs.reshape(padded, lanes), ((0, tokens - padded), (0, 0)))
    w1, w2 = block_matrices(spec_w1, spec_w2)
    b1, b2 = spec_b1.reshape(1, lanes), spec_b2.reshape(1, lanes)
    per_token = jnp.stack(
        [scalars[:, :, 0] * (1.0 / C), (1.0 + scalars[:, :, 2]) * 0.25], axis=-1
    ).reshape(2, padded, 2)
    per_token = jnp.pad(per_token, ((0, 0), (0, tokens - padded), (0, 0)))
    per_token = [
        lax.dynamic_slice_in_dim(per_token, first + blk * share, share, 1).reshape(2 * share, 2)
        for first, share in halves
    ]
    params_ring = jnp.stack([piece[rows:].reshape(-1)[:param_count] for piece in sums_ring])
    params_ring = [params_ring[k] for k in [0] + list(range(blks - 1, 0, -1))] * 2
    params_all = lax.dynamic_slice_in_dim(jnp.stack(params_ring), blks - blk, blks, 0)
    bias_all = params_all[:, :ff_here].reshape(1, -1)
    token_params = [
        params_all[:, ff_here + i * chans : ff_here + (i + 1) * chans].reshape(1, C)
        for i in range(3)
    ]
    modes_b, cot_pairs, w1, w2, weights, per_token, bias_all, token_params = tied(
        modes_b, cot_pairs, w1, w2, weights, per_token, bias_all, token_params
    )
    modes_b = swap_first(modes_b, grid_axes)
    cot_rings = [
        send(cot_pairs[first : first + blks * share].reshape(blks, share, lanes), "blk")
        for first, share in halves
    ]
    shrunk_a, *kept_a = spectral(modes_a, turn, turn_rest, w1, b1, w2, b2)
    modes_b, shrunk_a, cot_rings[0] = tied(modes_b, shrunk_a, cot_rings[0])
    shrunk_a = swap_first(shrunk_a, grid_axes)
    weights_other = other_core(weights)
    shrunk_b, *kept_b = spectral(modes_b, turn, turn_rest, w1, b1, w2, b2)
    cot_b = cot_rings[1]
    shrunk_b, shrunk_a, cot_b[1], cot_b[-1] = tied(shrunk_b, shrunk_a, cot_b[1], cot_b[-1])
    shrunk_b = swap_first(shrunk_b, grid_axes)
    shrunk_b, shrunk_a, cot_rings = tied(shrunk_b, shrunk_a, cot_rings)

    middles = []
    for (first, share), spans in zip(halves, TOKEN_HALVES):
        middle = collect(
            (shrunk_a, shrunk_b),
            field_rows,
            sums_rows,
            gain_row,
            shift_row,
            doubled_back,
            spans,
            blks * share,
        )
        middle, shrunk_b = tied(middle, shrunk_b)
        middles.append(swap_first(middle.reshape(blks, share, lanes), "blk"))
    before, mixed_parts, grad_parts = (), [], []
    for middle, cot_ring, scalar in zip(middles, cot_rings, per_token):
        kept, sent, middle_grad, *before = mlp(
            middle,
            cot_ring,
            scalar,
            token_params[1],
            token_params[2],
            (weights, weights_other),
            bias_all,
            token_params[0],
            before,
        )
        if grad_parts:
            middle_grad, before, grad_parts[0] = tied(middle_grad, before, grad_parts[0])
        mixed_parts.append((kept, sent))
        grad_parts.append(swap_first(middle_grad, "blk"))
    up_kept, up_sent, down_kept, down_sent, bias_part, small_part = before

    summed = jnp.stack(
        [
            (kept.astype(wide) + other_core(sent).astype(wide)).astype(narrow)
            for kept, sent in ((up_kept, up_sent), (down_kept, down_sent))
        ],
        axis=2,
    )
    tile_shape = (-1,) + summed.shape[2:]
    summed = lax.psum_scatter(summed.reshape(-1, C), "lat", scatter_dimension=0, tiled=True)
    total = lax.psum_scatter(summed, "blk", scatter_dimension=0, tiled=True)
    total = total.reshape(tile_shape)
    mixed_rows = []
    for kept, sent in mixed_parts:
        sent = other_core(sent)
        mixed_rows.append(
            jnp.concatenate(
                [jnp.where(lon == 0, kept, sent), jnp.where(lon == 0, sent, kept)], axis=2
            )
        )
    owned = small_part[:3].reshape(3, blks, chans).transpose(1, 0, 2).reshape(blks, -1)
    owned = jnp.concatenate([owned, bias_part.reshape(blks, -1)], axis=1)[:, None, :]
    grad_parts[1], mixed_rows, owned = tied(grad_parts[1], mixed_rows, owned)
    owned = send(owned, "blk")

    back_a, back_b = spread(
        [part.reshape(-1, lanes) for part in grad_parts],
        [
            pl.BlockSpec((TOKEN_STEP * SLOTS, lanes), lambda i: (jnp.minimum(i, 2), 0)),
            pl.BlockSpec((TOKEN_STEP * SLOTS, lanes), lambda i: (jnp.maximum(i - 3, 0), 0)),
        ],
        spread_kernel,
        (doubled,),
        group,
        lanes,
        narrow,
        6,
        "spread_grad",
    )
    ring_a = send(mixed_rows[0], "blk")
    blk_pieces = send_slices(mixed_rows[1], "blk")
    middle_grad = jnp.concatenate([part.reshape(-1, lanes) for part in grad_parts])
    back_a = swap_first(back_a, grid_axes)
    back_b, ring_a[1], ring_a[-1] = tied(back_b, ring_a[1], ring_a[-1])
    back_b = swap_first(back_b, grid_axes)
    back_a, *spec_sums = spectral_back(back_a, *kept_a, turn, w1, b1, w2, b2)
    back_a, back_b, owned = tied(back_a, back_b, owned)
    back_a = swap_first(back_a, grid_axes)
    back_b, spec_grads, spec_small = spectral_back(
        back_b, *kept_b, turn, w1, b1, w2, b2, tuple(spec_sums)
    )
    back_b, back_a = tied(back_b, back_a)
    back_b = swap_first(back_b, grid_axes)
    vector = jnp.concatenate([spec_small[:2].reshape(-1), sum(owned).reshape(-1)])
    vector_size, vector_rows = vector.shape[0], -(-vector.shape[0] // (BS * group))
    vector = jnp.pad(vector, (0, group * vector_rows * BS - vector_size))
    shared = jnp.concatenate(
        [spec_grads.reshape(group, -1, BS), vector.reshape(group, vector_rows, BS)], axis=1
    )
    back_a, back_b, total, shared, ring_a, blk_pieces, middle_grad = tied(
        back_a, back_b, total, shared, ring_a, blk_pieces, middle_grad
    )
    total = lax.all_gather(total, grid_axes, axis=0, tiled=False)
    ring_b = send_pieces(blk_pieces, "blk")
    shared = jnp.sum(swap_first(shared, grid_axes), axis=0)

    base_kept, base_sent, part_sums, one_small = collect_back(
        (back_a, back_b), middle_grad, field_rows, sums_rows, gain_row, ahead_back
    )
    base_kept, base_sent, part_sums, ring_b, shared = tied(
        base_kept, base_sent, part_sums, ring_b, shared
    )
    grad_sums = jnp.broadcast_to(part_sums[:, None], (lons, blks) + part_sums.shape[1:])
    grad_sums = swap_first(grad_sums.reshape((-1,) + part_sums.shape[1:]), ("lon", "blk"))
    grad_sums = jnp.sum(grad_sums.reshape((lons, blks) + part_sums.shape[1:]), axis=1)
    grad_sums = grad_sums.reshape(rows, 2, SLOTS)
    base_other = other_core(base_sent)
    mixed = to_flat((ring_a, ring_b))
    base_other, grad_sums, one_small, total, shared, mixed = tied(
        base_other, grad_sums, one_small, total, shared, mixed
    )
    up_grad, down_grad = weight_grads(total, lons, ff_here)
    own_rows = shared.shape[0]
    shared = grid_broadcast(jnp.concatenate([shared, one_small[:2].reshape(-1, BS)]))
    grad_sums, mixed, up_grad, down_grad = tied(grad_sums, mixed, up_grad, down_grad)
    input_grad = final_flat(base_kept, base_other, field_cols, sums_cols, grad_sums)

    one_small = jnp.sum(shared[:, own_rows:], axis=0).reshape(-1)
    vector = shared[:, own_rows - vector_rows : own_rows].reshape(-1)
    spec_grads = shared[:, : own_rows - vector_rows].reshape(2, 2, blocks, BS, BS)
    pieces, at = [one_small[:chans], one_small[chans:]], 0
    for size in (lanes, lanes, chans, chans, chans, ff_here):
        pieces.append(vector[at : at + size])
        at += size
    gain_one_grad, shift_one_grad, b1_grad, b2_grad = pieces[:4]
    down_bias_grad, gain_two_grad, shift_two_grad, up_bias_grad = pieces[4:]
    return (
        mixed,
        input_grad,
        gain_one_grad,
        shift_one_grad,
        spec_grads[0],
        b1_grad.reshape(spec_b1.shape),
        spec_grads[1],
        b2_grad.reshape(spec_b2.shape),
        gain_two_grad,
        shift_two_grad,
        up_grad,
        up_bias_grad,
        down_grad,
        down_bias_grad,
    )


def solution(mesh):
    placed = (
        P("lon", "blk", "lat"),
        P("blk"),
        P("blk"),
        P(None, "blk", None, None),
        P(None, "blk", None),
        P(None, "blk", None, None),
        P(None, "blk", None),
        P("blk"),
        P("blk"),
        P(None, "blk"),
        P("blk"),
        P("blk", None),
        P("blk"),
        P("lat", "lon"),
        P("lon", "blk", "lat"),
    )
    return jax.shard_map(
        per_device,
        mesh=mesh,
        in_specs=placed,
        out_specs=(
            P("lon", "blk", "lat"),
            P("lon", "blk", "lat"),
            P("blk"),
            P("blk"),
            P(None, "blk", None, None),
            P(None, "blk", None),
            P(None, "blk", None, None),
            P(None, "blk", None),
            P("blk"),
            P("blk"),
            P(None, "blk"),
            P("blk"),
            P("blk", None),
            P("blk"),
        ),
        check_vma=False,
    )
```

```python
import functools
import math

import jax
import jax.numpy as jnp
import ml_dtypes
import numpy as np
from jax import lax
from jax.experimental import pallas as pl
from jax.experimental.pallas import tpu as pltpu
from jax.sharding import PartitionSpec as P

C = 768
BS = 96
H = 90
W = 180
EPS = 1e-05
SHRINK = 0.01
SLOTS = 96
ROW_PAD = 48
VMEM = 60 << 20
wide = jnp.float32
narrow = jnp.bfloat16


def slot_columns():
    cols = np.full((2, SLOTS // 2), -1)
    cols[0, :45] = np.arange(0, 90, 2)
    cols[1, :45] = np.arange(1, 90, 2)
    return cols.reshape(-1)


def column_table(mode_total, doubled):
    cols = slot_columns()
    place = np.concatenate([cols, cols + W // 2])
    valid = np.concatenate([cols >= 0, cols >= 0])
    freq = np.arange(mode_total)
    angle = 2.0 * np.pi * (freq[:, None] * place[None, :] % W) / W
    keep = (freq <= W // 2).astype(np.float64)
    if doubled:
        keep = keep * np.where((freq == 0) | (freq == W // 2), 1.0, 2.0)
    keep = keep[:, None] * valid[None, :] / math.sqrt(W)
    return np.concatenate([np.cos(angle) * keep, -np.sin(angle) * keep], axis=0)


def row_table(rows_total, group):
    snaps = rows_total // H
    half = rows_total // group
    slot = np.arange(group * ROW_PAD)
    row = slot // ROW_PAD * half + slot % ROW_PAD
    valid = slot % ROW_PAD < half
    step, snap = row // snaps, row % snaps
    match = (snap[:, None] == snap[None, :]) & valid[:, None] & valid[None, :]
    angle = 2.0 * np.pi * (step[:, None] * step[None, :] % H) / H
    scale = match / math.sqrt(H)
    return np.concatenate([np.cos(angle) * scale, np.sin(angle) * scale], axis=0)


def split_table(table):
    high = table.astype(ml_dtypes.bfloat16)
    rest = (table - high.astype(np.float64)).astype(ml_dtypes.bfloat16)
    return jnp.asarray(high), jnp.asarray(rest)


def dot(left, right):
    return lax.dot_general(left, right, (((1,), (0,)), ((), ())), preferred_element_type=wide)


def dot_nt(left, right):
    return lax.dot_general(left, right, (((1,), (1,)), ((), ())), preferred_element_type=wide)


def dot_tn(left, right):
    return lax.dot_general(left, right, (((0,), (0,)), ((), ())), preferred_element_type=wide)


def token_sums(values):
    ones = jnp.ones((8, values.shape[1]), narrow)
    high, rest = split(values)
    return dot_nt(ones, high) + dot_nt(ones, rest)


def split(values):
    high = values.astype(narrow)
    return high, (values - high.astype(wide)).astype(narrow)


def fine_dot(table, table_rest, values):
    high, rest = split(values)
    return dot(table, high) + (dot(table, rest) + dot(table_rest, high))


def normal_parts(values):
    cumulative = 0.5 * (1.0 + lax.erf(values * (1.0 / math.sqrt(2.0))))
    density = jnp.exp(-0.5 * values * values) * (1.0 / math.sqrt(2.0 * math.pi))
    return cumulative, density


def gelu_value(values):
    return values * (0.5 * (1.0 + lax.erf(values * (1.0 / math.sqrt(2.0)))))


def gelu_slope(values):
    cumulative, density = normal_parts(values)
    return cumulative + values * density


def norm_columns(sums):
    rows = []
    for side in range(2):
        mean = sums[side, 0:1] * (1.0 / C)
        spread = sums[side, 1:2] * (1.0 / C) - mean * mean
        rows += [mean, lax.rsqrt(spread + EPS)]
    rows.append(jnp.zeros((4, SLOTS), wide))
    return jnp.transpose(jnp.concatenate(rows, axis=0))


def swap_parts(values):
    half = values.shape[1] // 2
    return jnp.concatenate([values[:, half:], values[:, :half]], axis=1)


def part_sign(shape):
    lane = lax.broadcasted_iota(jnp.int32, shape, 1)
    return jnp.where(lane < shape[1] // 2, 1.0, -1.0).astype(wide)


def lane_tiles(lanes):
    return -(-lanes // 128)


def store_modes(scratch, row, values):
    count, lanes = values.shape
    room = lane_tiles(lanes) * 128
    if room != lanes:
        values = jnp.concatenate([values, jnp.zeros((count, room - lanes), wide)], axis=1)
    for tile, ref in enumerate(scratch):
        ref[pl.ds(row, count, stride=ROW_PAD), :] = values[:, 128 * tile : 128 * (tile + 1)]


def load_modes(scratch, row, count, lanes):
    pieces = [ref[pl.ds(row, count, stride=ROW_PAD), :] for ref in scratch]
    return jnp.concatenate(pieces, axis=1)[:, :lanes]


def flush_modes(scratch, parts):
    group, _, _, lanes = parts[0].shape
    share = sum(part.shape[1] for part in parts)
    for tile, ref in enumerate(scratch):
        width = min(128, lanes - 128 * tile)
        block = ref[...].reshape(group, share, ROW_PAD, 128)
        first = 0
        for part in parts:
            last = first + part.shape[1]
            part[:, :, :, 128 * tile : 128 * tile + width] = block[
                :, first:last, :, :width
            ].astype(part.dtype)
            first = last


def fill_modes(scratch, parts):
    group, _, _, lanes = parts[0].shape
    share = sum(part.shape[1] for part in parts)
    for tile, ref in enumerate(scratch):
        width = min(128, lanes - 128 * tile)
        first = 0
        for part in parts:
            count = part.shape[1]
            block = part[:, :, :, 128 * tile : 128 * tile + width].astype(wide)
            for g in range(group):
                start = (g * share + first) * ROW_PAD
                ref[start : start + count * ROW_PAD, :width] = block[g].reshape(
                    count * ROW_PAD, width
                )
            first += count


def mode_parts(share):
    return (share - share // 2, share // 2)


def mode_scratch(mode_total, lanes):
    return [pltpu.VMEM((mode_total * ROW_PAD, 128), wide)] * lane_tiles(lanes)


def params():
    return pltpu.CompilerParams(vmem_limit_bytes=VMEM)


def cost(flops, moved):
    return pl.CostEstimate(flops=int(flops), bytes_accessed=int(moved), transcendentals=0)


def full(shape):
    return pl.BlockSpec(shape, lambda *_: (0,) * len(shape))


def once(shape, index):
    return pl.BlockSpec(shape, index, pipeline_mode=pl.Buffered(1))


def shape_of(shape, kind):
    return jax.ShapeDtypeStruct(shape, kind)


FLAT_ROWS = 18


def from_flat_kernel(with_sums, flat, out, *rest):
    scratch = rest[-1]
    scratch[...] = flat[0].astype(wide).reshape(scratch.shape)
    empty = jnp.zeros((3, 192), wide)
    for q in range(FLAT_ROWS):
        first = scratch[pl.ds(135 * q, 45, stride=3), :]
        second = scratch[pl.ds(135 * q + 1, 45, stride=3), :]
        third = scratch[pl.ds(135 * q + 2, 45, stride=3), :]
        even = jnp.concatenate([first, second[:, :64]], axis=1)
        odd = jnp.concatenate([second[:, 64:], third], axis=1)
        tile = jnp.concatenate([even, empty, odd, empty], axis=0)
        out[q] = tile.astype(narrow)
        if with_sums:
            total, total_sq = token_sums(tile), token_sums(tile * tile)
            rest[0][q] = jnp.concatenate([total[:1], total_sq[:1]], axis=0)


def from_flat(flat, rows, chans, with_sums):
    if chans != 192:
        grid = flat.reshape(rows, 45, 2, chans).transpose(0, 2, 1, 3)
        grid = jnp.pad(grid, ((0, 0), (0, 0), (0, 3), (0, 0))).reshape(rows, SLOTS, chans)
        if not with_sums:
            return grid
        wider = grid.astype(wide)
        return grid, jnp.stack([jnp.sum(wider, axis=2), jnp.sum(wider * wider, axis=2)], axis=1)
    block = FLAT_ROWS * 90 * chans
    out_specs = [pl.BlockSpec((FLAT_ROWS, SLOTS, chans), lambda i: (i, 0, 0))]
    out_shape = [shape_of((rows, SLOTS, chans), narrow)]
    if with_sums:
        out_specs.append(pl.BlockSpec((FLAT_ROWS, 2, SLOTS), lambda i: (i, 0, 0)))
        out_shape.append(shape_of((rows, 2, SLOTS), wide))
    outs = pl.pallas_call(
        functools.partial(from_flat_kernel, with_sums),
        grid=(rows // FLAT_ROWS,),
        in_specs=[pl.BlockSpec((1, 1, block), lambda i: (0, 0, i))],
        out_specs=out_specs,
        out_shape=out_shape,
        scratch_shapes=[pltpu.VMEM((block // 128, 128), wide)],
        compiler_params=params(),
        cost_estimate=cost(1e6, 1e5),
        name="from_flat",
    )(flat)
    return outs if with_sums else outs[0]


def write_flat(scratch, row, tile):
    even, odd = tile[0:45], tile[48:93]
    scratch[pl.ds(135 * row, 45, stride=3), :] = even[:, :128]
    scratch[pl.ds(135 * row + 1, 45, stride=3), :] = jnp.concatenate(
        [even[:, 128:], odd[:, :64]], axis=1
    )
    scratch[pl.ds(135 * row + 2, 45, stride=3), :] = odd[:, 64:]


PAIR_ROWS = 9


def place_pieces(blk, pieces, out):
    first, size = 0, len(pieces) // 2
    for half in (pieces[:size], pieces[size:]):
        share = half[0].shape[0]
        for by, piece in enumerate(half):
            place = first + lax.rem(blk + size - by, size) * share
            out[pl.ds(pl.multiple_of(place, 16), share), :] = piece[...]
        first += size * share


def to_flat_kernel(blk, *refs):
    *pieces, flat, rows, scratch = refs
    chans = rows.shape[1] // 2
    second = pl.program_id(0) == 1
    step = pl.program_id(1)

    @pl.when(jnp.logical_not(second) & (step == 0))
    def _():
        place_pieces(blk[0], pieces, rows)

    for q in range(PAIR_ROWS):
        start = pl.multiple_of((step * PAIR_ROWS + q) * SLOTS, SLOTS)
        pair = rows[pl.ds(start, SLOTS), :].astype(wide)
        write_flat(scratch, q, jnp.where(second, pair[:, chans:], pair[:, :chans]))
    flat[0] = scratch[...].reshape(1, scratch.shape[0] * 128).astype(flat.dtype)


def plain_flat(grid):
    rows, _, chans = grid.shape
    kept = grid.reshape(rows, 2, SLOTS // 2, chans)[:, :, :45].transpose(0, 2, 1, 3)
    return kept.reshape(1, 1, rows * 90 * chans)


def to_flat(halves):
    pieces = [piece for half in halves for piece in half]
    chans = pieces[0].shape[1] // 2
    if chans != 192:
        pairs = in_order(halves)
        grid = pairs[: 45 * SLOTS].reshape(45, SLOTS, 2, chans).transpose(2, 0, 1, 3)
        return plain_flat(grid.reshape(90, SLOTS, chans))
    block = PAIR_ROWS * 90 * chans
    steps = 45 // PAIR_ROWS
    tokens = sum(piece.shape[0] for piece in pieces)
    return pl.pallas_call(
        to_flat_kernel,
        grid_spec=pltpu.PrefetchScalarGridSpec(
            num_scalar_prefetch=1,
            grid=(2, steps),
            in_specs=[once(piece.shape, lambda *_: (0, 0)) for piece in pieces],
            out_specs=pl.BlockSpec((1, 1, block), lambda h, i, at: (0, 0, h * steps + i)),
            scratch_shapes=[
                pltpu.VMEM((tokens, 2 * chans), narrow),
                pltpu.VMEM((block // 128, 128), wide),
            ],
        ),
        out_shape=shape_of((1, 1, 90 * 90 * chans), narrow),
        compiler_params=params(),
        cost_estimate=cost(1e6, 1e5),
        name="to_flat",
    )(lax.axis_index("blk").astype(jnp.int32).reshape(1), *pieces)


def final_tile(base, field, sums, grad_sums):
    mean = sums[0:1] * (1.0 / C)
    spread = sums[1:2] * (1.0 / C) - mean * mean
    inverse = lax.rsqrt(spread + EPS)
    shift = inverse * grad_sums[0:1] * (1.0 / C)
    slope = inverse * inverse * grad_sums[1:2] * (1.0 / C)
    cols = jnp.transpose(
        jnp.concatenate([mean * slope - shift, slope, jnp.zeros((6, SLOTS), wide)], axis=0)
    )
    return (base + cols[:, 0:1]) - field.astype(wide) * cols[:, 1:2]


FINAL_ROWS = 9


def final_kernel(place, kept, other, field, sums, grad_sums, flat, *scratch):
    own = pl.program_id(0) // (45 // FINAL_ROWS) == place[0]
    for q in range(FINAL_ROWS):
        base = jnp.where(own, kept[q], other[q])
        tile = final_tile(base, field[q], sums[q], grad_sums[q])
        if scratch:
            write_flat(scratch[0], q, tile)
        else:
            flat[q] = tile
    if scratch:
        flat[0] = scratch[0][...].reshape(1, scratch[0].shape[0] * 128)


def final_flat(kept, other, field, sums, grad_sums):
    rows, _, chans = field.shape
    steps = 45 // FINAL_ROWS
    block = FINAL_ROWS * 90 * chans

    def half_of(which):
        def index(i, at):
            first = steps * (at[0] if which == 0 else 1 - at[0])
            return (jnp.clip(i - first, 0, steps - 1), 0, 0)

        return pl.BlockSpec((FINAL_ROWS, SLOTS, chans), index)

    tiles = pl.BlockSpec((FINAL_ROWS, SLOTS, chans), lambda i, at: (i, 0, 0))
    pairs = pl.BlockSpec((FINAL_ROWS, 2, SLOTS), lambda i, at: (i, 0, 0))
    simple = chans != 192
    out = pl.pallas_call(
        final_kernel,
        grid_spec=pltpu.PrefetchScalarGridSpec(
            num_scalar_prefetch=1,
            grid=(2 * steps,),
            in_specs=[half_of(0), half_of(1), tiles, pairs, pairs],
            out_specs=tiles if simple else pl.BlockSpec((1, 1, block), lambda i, at: (0, 0, i)),
            scratch_shapes=[] if simple else [pltpu.VMEM((block // 128, 128), wide)],
        ),
        out_shape=shape_of(field.shape if simple else (1, 1, rows * 90 * chans), wide),
        compiler_params=params(),
        cost_estimate=cost(1e6, 1e5),
        name="final_flat",
    )(lax.axis_index("lon").astype(jnp.int32).reshape(1), kept, other, field, sums, grad_sums)
    return plain_flat(out) if simple else out


STEP = 9
BACK_STEP = 5
TOKEN_STEP = 8
TOKEN_HALVES = ((0, 24), (24, 21))


def spread_norm_kernel(field, sums, gain, shift, table, table_rest, out_a, out_b, *scratch):
    step = pl.program_id(0)
    for q in range(STEP):
        cols = norm_columns(sums[:, q])
        sides = []
        for side in range(2):
            centered = field[side, q].astype(wide) - cols[:, 2 * side : 2 * side + 1]
            normed = centered * cols[:, 2 * side + 1 : 2 * side + 2] * gain[...] + shift[...]
            sides.append(normed)
        modes = fine_dot(table[...], table_rest[...], jnp.concatenate(sides, axis=0))
        count = modes.shape[0] // 2
        store_modes(
            scratch, step * STEP + q, jnp.concatenate([modes[:count], modes[count:]], axis=1)
        )
    finish_spread(step, scratch, (out_a, out_b))


def spread_kernel(first, second, table, out_a, out_b, *scratch):
    step = pl.program_id(0)
    from_first = step < TOKEN_HALVES[0][1] // TOKEN_STEP
    for q in range(TOKEN_STEP):
        row = step * TOKEN_STEP + q
        rows = slice(q * SLOTS, (q + 1) * SLOTS)
        pair = jnp.where(from_first, first[rows, :], second[rows, :])
        chans = pair.shape[1] // 2
        modes = dot(table[...], jnp.concatenate([pair[:, :chans], pair[:, chans:]], axis=0))
        count = modes.shape[0] // 2
        modes = jnp.concatenate([modes[:count], modes[count:]], axis=1)
        store_modes(scratch, row, jnp.where(row < 45, modes, 0.0))

    @pl.when(step == pl.num_programs(0) - 1)
    def _():
        flush_modes(scratch, (out_a, out_b))


def finish_spread(step, scratch, out):
    @pl.when(step == 0)
    def _():
        count = scratch[0].shape[0] // ROW_PAD
        for row in range(45, ROW_PAD):
            for ref in scratch:
                ref[pl.ds(row, count, stride=ROW_PAD), :] = jnp.zeros((count, 128), wide)

    @pl.when(step == pl.num_programs(0) - 1)
    def _():
        flush_modes(scratch, out)


def spread(inputs, in_specs, kernel, tables, group, lanes, kind, steps, name):
    mode_total = tables[0].shape[0] // 2
    outs = [(group, count, ROW_PAD, lanes) for count in mode_parts(mode_total // group)]
    return pl.pallas_call(
        kernel,
        grid=(steps,),
        in_specs=in_specs + [full(table.shape) for table in tables],
        out_specs=[full(out) for out in outs],
        out_shape=[shape_of(out, kind) for out in outs],
        scratch_shapes=mode_scratch(mode_total, lanes),
        compiler_params=params(),
        cost_estimate=cost(1e6, 1e5),
        name=name,
    )(*inputs, *tables)


def collect_kernel(first, modes_a, modes_b, field, sums, gain, shift, table, out, *scratch):
    step = pl.program_id(0)

    @pl.when(step == 0)
    def _():
        fill_modes(scratch, (modes_a, modes_b))

    for q in range(TOKEN_STEP):
        row = first + step * TOKEN_STEP + q
        spatial = spatial_rows(scratch, row, table, modes_a.shape[3])
        cols = norm_columns(sums[:, q])
        sides = []
        for side in range(2):
            centered = field[side, q].astype(wide) - cols[:, 2 * side : 2 * side + 1]
            normed = centered * cols[:, 2 * side + 1 : 2 * side + 2] * gain[...] + shift[...]
            sides.append(spatial[side] + normed + centered)
        pair = jnp.where(row < 45, jnp.concatenate(sides, axis=1), 0.0)
        out[q * SLOTS : (q + 1) * SLOTS, :] = pair.astype(narrow)


def spatial_rows(scratch, row, table, lanes):
    count = table.shape[1] // 2
    pair = load_modes(scratch, row, count, lanes).astype(narrow)
    stacked = jnp.concatenate([pair[:, : lanes // 2], pair[:, lanes // 2 :]], axis=0)
    spatial = dot(table[...], stacked)
    return spatial[:SLOTS], spatial[SLOTS:]


def collect(modes, field, sums, gain, shift, table, rows, tokens):
    chans = field.shape[3]
    first, count = rows
    skip = first // TOKEN_STEP
    mode_total = table.shape[1] // 2
    return pl.pallas_call(
        functools.partial(collect_kernel, first),
        grid=(-(-count // TOKEN_STEP),),
        in_specs=[full(part.shape) for part in modes]
        + [
            pl.BlockSpec((2, TOKEN_STEP, SLOTS, chans), lambda i: (0, i + skip, 0, 0)),
            pl.BlockSpec((2, TOKEN_STEP, 2, SLOTS), lambda i: (0, i + skip, 0, 0)),
            full(gain.shape),
            full(shift.shape),
            full(table.shape),
        ],
        out_specs=pl.BlockSpec((TOKEN_STEP * SLOTS, 2 * chans), lambda i: (i, 0)),
        out_shape=shape_of((tokens, 2 * chans), narrow),
        scratch_shapes=mode_scratch(mode_total, 2 * chans),
        compiler_params=params(),
        cost_estimate=cost(1e6, 1e5),
        name="collect_norm",
    )(*modes, field, sums, gain, shift, table)


def collect_back_kernel(
    place, modes_a, modes_b, grad, field, sums, gain, table, kept, sent, parts, small, *scratch
):
    step = pl.program_id(0)

    @pl.when(step == 0)
    def _():
        fill_modes(scratch, (modes_a, modes_b))
        small[...] = jnp.zeros(small.shape, wide)

    gain_sum = jnp.zeros((1, gain.shape[1]), wide)
    shift_sum = jnp.zeros((1, gain.shape[1]), wide)
    for q in range(BACK_STEP):
        spatial = spatial_rows(scratch, step * BACK_STEP + q, table, modes_a.shape[3])
        cols = norm_columns(sums[:, q])
        pair = grad[q * SLOTS : (q + 1) * SLOTS, :].astype(wide)
        chans = pair.shape[1] // 2
        bases = []
        for side in range(2):
            inverse = cols[:, 2 * side + 1 : 2 * side + 2]
            normed = (field[side, q].astype(wide) - cols[:, 2 * side : 2 * side + 1]) * inverse
            middle = pair[:, side * chans : (side + 1) * chans]
            total = middle + spatial[side]
            scaled = total * gain[...]
            bases.append(middle + inverse * scaled)
            turned = scaled * normed
            parts[side, q] = jnp.concatenate(
                [token_sums(scaled)[:1], token_sums(turned)[:1]], axis=0
            )
            gain_sum = gain_sum + jnp.sum(total * normed, axis=0, keepdims=True)
            shift_sum = shift_sum + jnp.sum(total, axis=0, keepdims=True)
        kept[q] = jnp.where(place[0] == 0, bases[0], bases[1])
        sent[q] = jnp.where(place[0] == 0, bases[1], bases[0])
    small[0:1] += gain_sum
    small[1:2] += shift_sum


def collect_back(modes, grad, field, sums, gain, table):
    chans = field.shape[3]
    mode_total = table.shape[1] // 2
    half_rows = pl.BlockSpec((BACK_STEP, SLOTS, chans), lambda i, at: (i, 0, 0))
    pair_sums = pl.BlockSpec((2, BACK_STEP, 2, SLOTS), lambda i, at: (0, i, 0, 0))
    return pl.pallas_call(
        collect_back_kernel,
        grid_spec=pltpu.PrefetchScalarGridSpec(
            num_scalar_prefetch=1,
            grid=(45 // BACK_STEP,),
            in_specs=[
                *[full(part.shape) for part in modes],
                pl.BlockSpec((BACK_STEP * SLOTS, 2 * chans), lambda i, at: (i, 0)),
                pl.BlockSpec((2, BACK_STEP, SLOTS, chans), lambda i, at: (0, i, 0, 0)),
                pair_sums,
                full(gain.shape),
                full(table.shape),
            ],
            out_specs=[half_rows, half_rows, pair_sums, full((8, chans))],
            scratch_shapes=mode_scratch(mode_total, 2 * chans),
        ),
        out_shape=[
            shape_of(field.shape[1:], wide),
            shape_of(field.shape[1:], wide),
            shape_of(sums.shape, wide),
            shape_of((8, chans), wide),
        ],
        compiler_params=params(),
        cost_estimate=cost(1e6, 1e5),
        name="collect_back",
    )(lax.axis_index("lon").astype(jnp.int32).reshape(1), *modes, grad, field, sums, gain, table)


def turn_rows(both):
    count = both.shape[0] // 2
    turned = swap_parts(both[count:])
    return both[:count] + turned * part_sign(turned.shape)


def return_rows(table, values):
    both = dot(table[...], values.astype(narrow))
    count = both.shape[0] // 2
    turned = swap_parts(both[count:])
    return both[:count] - turned * part_sign(turned.shape)


def shrink_bend(values):
    return jnp.tanh(values * (1.0 / SHRINK))


def spectral_kernel(modes, table, table_rest, w1, b1, w2, b2, out, low, act):
    rows = modes.shape[0] * ROW_PAD
    lanes = modes.shape[3]
    exact = fine_dot(table[...], table_rest[...], modes[...].reshape(rows, lanes))
    coarse = turn_rows(exact).astype(narrow)
    low[0] = coarse
    bent = gelu_value(dot(coarse, w1[...]) + b1[...]).astype(narrow)
    act[0] = bent
    second = dot(bent, w2[...]) + b2[...]
    shrunk = second - SHRINK * shrink_bend(second)
    out[...] = return_rows(table, shrunk).astype(narrow).reshape(out.shape)


def spectral(modes, table, table_rest, w1, b1, w2, b2):
    group, share, _, lanes = modes.shape
    rows = group * ROW_PAD
    mode_block = pl.BlockSpec((group, 1, ROW_PAD, lanes), lambda i: (0, i, 0, 0))
    kept_block = pl.BlockSpec((1, rows, lanes), lambda i: (i, 0, 0))
    return pl.pallas_call(
        spectral_kernel,
        grid=(share,),
        in_specs=[mode_block] + [full(x.shape) for x in (table, table_rest, w1, b1, w2, b2)],
        out_specs=[mode_block, kept_block, kept_block],
        out_shape=[
            shape_of(modes.shape, narrow),
            shape_of((share, rows, lanes), narrow),
            shape_of((share, rows, lanes), narrow),
        ],
        compiler_params=params(),
        cost_estimate=cost(1e6, 1e5),
        name="spectral",
    )(modes, table, table_rest, w1, b1, w2, b2)


def spectral_back_kernel(modes, low, act, table, w1, b1, w2, b2, *rest):
    before, (out, *outs) = rest[: -4 - bool(len(rest) > 4)], rest[-4 - bool(len(rest) > 4) :]
    second_part = bool(before)
    grads, (small, g1, g2) = (outs[0] if second_part else None), outs[-3:]
    rows = modes.shape[0] * ROW_PAD
    lanes = modes.shape[3]

    @pl.when(pl.program_id(0) == 0)
    def _():
        for k, ref in enumerate((small, g1, g2)):
            ref[...] = before[k][...] if second_part else jnp.zeros(ref.shape, wide)

    back = turn_rows(dot(table[...], modes[...].reshape(rows, lanes)))
    bent = act[0]
    bend = shrink_bend(dot(bent, w2[...]) + b2[...])
    second = (back * (bend * bend)).astype(narrow)
    g2[...] += dot_tn(bent, second)
    small[1:2] += jnp.sum(second.astype(wide), axis=0, keepdims=True)
    coarse = low[0]
    slope = gelu_slope(dot(coarse, w1[...]) + b1[...])
    first = (dot_nt(second, w2[...]) * slope).astype(narrow)
    g1[...] += dot_tn(coarse, first)
    small[0:1] += jnp.sum(first.astype(wide), axis=0, keepdims=True)
    out[...] = return_rows(table, dot_nt(first, w1[...])).astype(narrow).reshape(out.shape)
    if not second_part:
        return

    @pl.when(pl.program_id(0) == pl.num_programs(0) - 1)
    def _():
        half = lanes // 2
        at = 0
        for outer in (g1[...], g2[...]):
            for part in (
                outer[:half, :half] + outer[half:, half:],
                outer[:half, half:] - outer[half:, :half],
            ):
                for j in range(half // BS):
                    block = slice(j * BS, (j + 1) * BS)
                    grads[at : at + BS, :] = part[block, block]
                    at += BS


def spectral_back(modes, low, act, table, w1, b1, w2, b2, before=()):
    group, share, _, lanes = modes.shape
    rows = group * ROW_PAD
    mode_block = pl.BlockSpec((group, 1, ROW_PAD, lanes), lambda i: (0, i, 0, 0))
    kept_block = pl.BlockSpec((1, rows, lanes), lambda i: (i, 0, 0))
    sums = [shape_of((8, lanes), wide)] + [shape_of((lanes, lanes), wide)] * 2
    outs = [shape_of(modes.shape, narrow)]
    scratch = []
    if before:
        outs += [shape_of((2 * lanes, BS), wide), sums[0]]
        scratch = [pltpu.VMEM(sums[1].shape, wide)] * 2
    else:
        outs += sums
    return pl.pallas_call(
        spectral_back_kernel,
        grid=(share,),
        in_specs=[mode_block, kept_block, kept_block]
        + [full(x.shape) for x in (table, w1, b1, w2, b2, *before)],
        out_specs=[mode_block] + [full(out.shape) for out in outs[1:]],
        out_shape=outs,
        scratch_shapes=scratch,
        compiler_params=params(),
        cost_estimate=cost(1e6, 1e5),
        name="spectral_back",
    )(modes, low, act, table, w1, b1, w2, b2, *before)


def block_matrix_kernel(w1, w2, out1, out2):
    for weight, out in ((w1, out1), (w2, out2)):
        blocks = weight.shape[1]
        empty = jnp.zeros((BS, BS), wide)
        rows = []
        for part in range(2):
            for block in range(blocks):
                real, imag = weight[0, block].astype(wide), weight[1, block].astype(wide)
                pair = (real, imag) if part == 0 else (-imag, real)
                rows.append(
                    jnp.concatenate(
                        [piece if k == block else empty for piece in pair for k in range(blocks)],
                        axis=1,
                    )
                )
        out[...] = jnp.concatenate(rows, axis=0).astype(narrow)


def block_matrices(w1, w2):
    lanes = 2 * w1.shape[1] * BS
    return pl.pallas_call(
        block_matrix_kernel,
        out_shape=[shape_of((lanes, lanes), narrow)] * 2,
        compiler_params=params(),
        cost_estimate=cost(1e6, 1e5),
        name="block_matrices",
    )(w1, w2)


FF_TILE = 256
CHUNKS = 4


def token_tile(values, side, start, count):
    chans = values[0].shape[2] // 2
    return jnp.concatenate(
        [
            source[0, pl.ds(start, count), side * chans : (side + 1) * chans]
            for source in values
        ],
        axis=1,
    ).astype(wide)


def norm_two(values):
    mean = jnp.mean(values, axis=1, keepdims=True)
    offset = values - mean
    inverse = lax.rsqrt(jnp.mean(offset * offset, axis=1, keepdims=True) + EPS)
    return offset * inverse, mean, inverse


def mlp_kernel(
    tile,
    blks,
    place,
    *refs,
):
    middle, pieces = refs[:blks], refs[blks : 2 * blks]
    *refs, cot_all = refs[2 * blks :]

    @pl.when(pl.program_id(0) == 0)
    def _():
        for by, piece in enumerate(pieces):
            cot_all[pl.ds(lax.rem(place[0] + blks - by, blks), 1)] = piece[...][None]

    cot = [cot_all.at[pl.ds(b, 1)] for b in range(blks)]
    mlp_body(tile, place, middle, cot, *refs[:3], refs[3:5], refs[5:7], *refs[7:])


def mlp_body(
    tile,
    here,
    middle,
    cot,
    cols,
    gain,
    shift,
    ups,
    downs,
    up_bias,
    down_bias,
    *rest,
):
    before_refs = rest[:-14]
    mixed_kept, mixed_sent, middle_grad = rest[-14:-11]
    weight_grads, (bias_grad, small) = rest[-11:-7], rest[-7:-5]
    tokens_in, grads_in, branch, grad_sum, norm_cols = rest[-5:]
    first_core = here[1] == 0
    step = pl.program_id(0)
    share = middle[0].shape[1]
    pieces = share // tile

    @pl.when(step == 0)
    def _():
        small[...] = before_refs[5][...] if before_refs else jnp.zeros(small.shape, wide)
        for side in range(2):

            @pl.loop(0, pieces)
            def _(piece):
                start = pl.multiple_of(piece * tile, 16)
                place = pl.ds(pl.multiple_of(side * share + piece * tile, 16), tile)
                normed, mean, inverse = norm_two(token_tile(middle, side, start, tile))
                norm_cols[place, 0:1] = mean
                norm_cols[place, 1:2] = inverse
                tokens_in[place, :] = (normed * gain[...] + shift[...]).astype(narrow)
                weight = cols[place, 1:2]
                grad = (token_tile(cot, side, start, tile) * weight).astype(narrow)
                grads_in[place, :] = grad
                small[0:1] += jnp.sum(grad.astype(wide), axis=0, keepdims=True)
                branch[place, :] = jnp.zeros((tile, C), wide)
                grad_sum[place, :] = jnp.zeros((tile, C), wide)

    up_tile = jnp.where(first_core, ups[0][0], ups[1][0])
    down_tile = jnp.where(first_core, downs[1][0], downs[0][0])
    tokens, grads = tokens_in[...], grads_in[...]
    count = tokens.shape[0]
    piece = count // CHUNKS
    hidden, before_grad = [], []
    for c in range(CHUNKS):
        place = slice(c * piece, (c + 1) * piece)
        before = dot(tokens[place], up_tile) + up_bias[...]
        into = dot_nt(grads[place], down_tile)
        cumulative, density = normal_parts(before)
        hidden.append((before * cumulative).astype(narrow))
        before_grad.append((into * (cumulative + before * density)).astype(narrow))
    hidden, before_grad = jnp.concatenate(hidden, axis=0), jnp.concatenate(before_grad, axis=0)
    branch[...] += dot(hidden, down_tile)
    grad_sum[...] += dot_nt(before_grad, up_tile)
    rows = up_tile.shape[1] // 2
    for which, total in enumerate((dot_tn(before_grad, tokens), dot_tn(hidden, grads))):
        first, second = (
            half.reshape(weight_grads[0].shape) for half in (total[:rows], total[rows:])
        )
        parts = (
            jnp.where(first_core, first, second),
            jnp.where(first_core, second, first),
        )
        for k, part in enumerate(parts):
            if before_refs:
                part = part + before_refs[2 * which + k][...].astype(wide)
            weight_grads[2 * which + k][...] = part.astype(narrow)
    bias_total = jnp.sum(before_grad.astype(wide), axis=0, keepdims=True)
    bias_grad[...] = bias_total + before_refs[4][...] if before_refs else bias_total

    @pl.when(step == pl.num_programs(0) - 1)
    def _():
        for side in range(2):

            @pl.loop(0, pieces)
            def _(piece):
                start = pl.multiple_of(piece * tile, 16)
                place = pl.ds(pl.multiple_of(side * share + piece * tile, 16), tile)
                values = token_tile(middle, side, start, tile)
                inverse = norm_cols[place, 1:2]
                normed = (values - norm_cols[place, 0:1]) * inverse
                result = (
                    values + cols[place, 0:1] + (branch[place, :] + down_bias[...])
                ).astype(narrow)
                grad = grad_sum[place, :]
                small[1:2] += jnp.sum(grad * normed, axis=0, keepdims=True)
                small[2:3] += jnp.sum(grad, axis=0, keepdims=True)
                scaled = grad * gain[...]
                back = inverse * (
                    scaled
                    - jnp.mean(scaled, axis=1, keepdims=True)
                    - normed * jnp.mean(scaled * normed, axis=1, keepdims=True)
                )
                whole = token_tile(cot, side, start, tile) * cols[place, 1:2] + back
                whole = whole.astype(narrow)
                chans = middle[0].shape[2] // 2

                def put(out):
                    for b in range(len(middle)):
                        out[b, pl.ds(start, tile), :] = result[:, b * chans : (b + 1) * chans]

                pl.when(here[1] == side)(lambda: put(mixed_kept))
                pl.when(here[1] != side)(lambda: put(mixed_sent))
                for b in range(len(middle)):
                    lanes = slice(side * chans, (side + 1) * chans)
                    middle_grad[b, pl.ds(start, tile), lanes] = whole[
                        :, b * chans : (b + 1) * chans
                    ]


def mlp(middle, cot, cols, gain, shift, weights, up_bias, down_bias, before):
    blks, share, lanes = middle.shape
    count = 2 * share
    ff_here = weights[0].shape[2]
    per = ff_here // FF_TILE if ff_here % FF_TILE == 0 else 1
    width = ff_here // per
    tile = share
    by_source = [
        once((1, share, lanes), lambda i, at, b=b: (b, 0, 0)) for b in range(blks)
    ]
    by_ring = [once((share, lanes), lambda i, at: (0, 0))] * blks
    lats = lax.axis_size("lat")
    grad_shape = (lats, blks * per, width // 2 // lats, C)
    grad_out = pl.BlockSpec((lats, 1) + grad_shape[2:], lambda i, at: (0, i, 0, 0))
    bias_out = pl.BlockSpec((1, width), lambda i, at: (0, i))
    down_weights = [part.reshape(blks, ff_here, C) for part in weights]
    return pl.pallas_call(
        functools.partial(mlp_kernel, tile, blks),
        grid_spec=pltpu.PrefetchScalarGridSpec(
            num_scalar_prefetch=1,
            grid=(blks * per,),
            in_specs=by_source
            + by_ring
            + [
                full(cols.shape),
                full(gain.shape),
                full(shift.shape),
                *[pl.BlockSpec((1, C, width), lambda i, at: (i // per, 0, i % per))] * 2,
                *[pl.BlockSpec((1, width, C), lambda i, at: (i // per, i % per, 0))] * 2,
                bias_out,
                full(down_bias.shape),
            ]
            + ([grad_out] * 4 + [bias_out, full((8, C))] if before else []),
            out_specs=[
                full((blks, share, lanes // 2)),
                full((blks, share, lanes // 2)),
                full(middle.shape),
                *[grad_out] * 4,
                bias_out,
                full((8, C)),
            ],
            scratch_shapes=[
                pltpu.VMEM((count, C), narrow),
                pltpu.VMEM((count, C), narrow),
                pltpu.VMEM((count, C), wide),
                pltpu.VMEM((count, C), wide),
                pltpu.VMEM((count, 2), wide),
                pltpu.VMEM(middle.shape, narrow),
            ],
        ),
        out_shape=[
            shape_of((blks, share, lanes // 2), narrow),
            shape_of((blks, share, lanes // 2), narrow),
            shape_of(middle.shape, narrow),
            *[shape_of(grad_shape, narrow)] * 4,
            shape_of((1, blks * ff_here), wide),
            shape_of((8, C), wide),
        ],
        compiler_params=params(),
        cost_estimate=cost(1e6, 1e5),
        name="channel_mlp",
    )(
        jnp.stack([lax.axis_index("blk"), lax.axis_index("lon")]).astype(jnp.int32),
        *([middle] * blks),
        *cot,
        cols,
        gain,
        shift,
        *weights,
        *down_weights,
        up_bias,
        down_bias,
        *before,
    )


def weight_grads_kernel(pieces, up, down):
    lats, lons, tiles = pieces.shape[:3]
    for which, out in ((0, up), (1, down)):
        rows = [
            pieces[lat, lon, tile, which]
            for tile in range(tiles)
            for lon in range(lons)
            for lat in range(lats)
        ]
        grad = jnp.concatenate(rows, axis=0).astype(wide)
        out[...] = jnp.transpose(grad) if which == 0 else grad


def weight_grads(pieces, lons, ff_here):
    pieces = pieces.reshape((-1, lons) + pieces.shape[1:])
    return pl.pallas_call(
        weight_grads_kernel,
        out_shape=[shape_of((C, ff_here), wide), shape_of((ff_here, C), wide)],
        compiler_params=params(),
        cost_estimate=cost(1e6, 1e5),
        name="weight_grads",
    )(pieces)


def swap_first(values, axes):
    return lax.all_to_all(values, axes, split_axis=0, concat_axis=0, tiled=True)


def shifted(values, axis, by):
    size = lax.axis_size(axis)
    return lax.ppermute(values, axis, [(i, (i + by) % size) for i in range(size)])


def other_core(values):
    return lax.ppermute(values, "lon", [(0, 1), (1, 0)])


def pick(values, index):
    return lax.dynamic_index_in_dim(values, index, 0, keepdims=False)


def ring(values, axis):
    return [values] + [shifted(values, axis, by) for by in range(1, lax.axis_size(axis))]


def send_slices(values, axis):
    size, here = lax.axis_size(axis), lax.axis_index(axis)
    return [pick(values, here)] + [pick(values, (here + by) % size) for by in range(1, size)]


def send_pieces(pieces, axis):
    return pieces[:1] + [shifted(piece, axis, by) for by, piece in enumerate(pieces) if by]


def send(values, axis):
    return send_pieces(send_slices(values, axis), axis)


def in_order(halves):
    size, blk = len(halves[0]), lax.axis_index("blk")
    lanes = halves[0][0].shape[1]
    out = jnp.zeros((sum(size * half[0].shape[0] for half in halves), lanes), halves[0][0].dtype)
    first = 0
    for half in halves:
        share = half[0].shape[0]
        for by, piece in enumerate(half):
            place = first + (blk - by) % size * share
            out = lax.dynamic_update_slice_in_dim(out, piece, place, 0)
        first += size * share
    return out


def lat_broadcast(values):
    count = lax.axis_size("lat")
    return swap_first(jnp.broadcast_to(values[None], (count,) + values.shape), "lat")


def grid_broadcast(values):
    count = lax.axis_size("lat") * lax.axis_size("lon")
    return swap_first(jnp.broadcast_to(values[None], (count,) + values.shape), ("lat", "lon"))


def tied(*values):
    return lax.optimization_barrier(values)


def per_device(
    field,
    gain_one,
    shift_one,
    spec_w1,
    spec_b1,
    spec_w2,
    spec_b2,
    gain_two,
    shift_two,
    up_weight,
    up_bias,
    down_weight,
    down_bias,
    presence,
    cotangent,
):
    rows, cols = presence.shape
    chans = gain_one.shape[0]
    lats, lons, blks = (lax.axis_size(name) for name in ("lat", "lon", "blk"))
    blk, lon = lax.axis_index("blk"), lax.axis_index("lon")
    grid_axes = ("lat", "lon")
    group = lats * lons
    half = rows // lons
    blocks = spec_w1.shape[1]
    mode_total = (W // 2 + group) // group * group
    lanes = 2 * chans
    ff_here = up_bias.shape[0]
    ahead, ahead_rest = split_table(column_table(mode_total, False))
    ahead_back, _ = split_table(column_table(mode_total, False).T)
    doubled, _ = split_table(column_table(mode_total, True))
    doubled_back, _ = split_table(column_table(mode_total, True).T)
    turn, turn_rest = split_table(row_table(rows * lats, group))
    gain_row, shift_row = gain_one[None, :], shift_one[None, :]

    weight_own = jnp.where(lon == 0, up_weight, down_weight.reshape(up_weight.shape))
    weights = lax.all_gather(weight_own, "blk", axis=0, tiled=False)

    field_cols, sums_part = from_flat(field, rows, chans, True)
    row_params = jnp.concatenate([up_bias.astype(wide), down_bias, gain_two, shift_two])
    param_count = row_params.shape[0]
    row_params = jnp.pad(row_params, (0, -param_count % (2 * SLOTS))).reshape(-1, 2, SLOTS)
    sums_ring = ring(jnp.concatenate([sums_part, row_params]), "blk")
    field_rows = swap_first(field_cols.reshape(2, half, SLOTS, chans), "lon")
    field_rows, *sums_ring = tied(field_rows, *sums_ring)
    sums_cols = sum(piece[:rows] for piece in sums_ring)
    seen = presence.reshape(rows, 45, 2).transpose(0, 2, 1)
    seen = jnp.pad(seen, ((0, 0), (0, 0), (0, 3))).reshape(rows, 1, SLOTS).astype(wide)
    scalars = jnp.concatenate([sums_cols, seen], axis=1).reshape(2, half, 3, SLOTS)
    scalars = swap_first(scalars, "lon")
    sums_rows = scalars[:, :, :2]

    modes_a, modes_b = spread(
        (field_rows, sums_rows, gain_row, shift_row),
        [
            pl.BlockSpec((2, STEP, SLOTS, chans), lambda i: (0, i, 0, 0)),
            pl.BlockSpec((2, STEP, 2, SLOTS), lambda i: (0, i, 0, 0)),
            full(gain_row.shape),
            full(shift_row.shape),
        ],
        spread_norm_kernel,
        (ahead, ahead_rest),
        group,
        lanes,
        wide,
        45 // STEP,
        "spread_norm",
    )
    cotangent, modes_a, modes_b = tied(cotangent, modes_a, modes_b)
    modes_a = swap_first(modes_a, grid_axes)
    cot_cols = from_flat(cotangent, rows, chans, False).reshape(2, half, SLOTS, chans)
    cot_own, cot_other = pick(cot_cols, lon), other_core(pick(cot_cols, 1 - lon))
    cot_pairs = jnp.concatenate(
        [jnp.where(lon == 0, cot_own, cot_other), jnp.where(lon == 0, cot_other, cot_own)], axis=2
    )
    padded = half * SLOTS
    halves = [
        (first * SLOTS, -(-count * SLOTS // (blks * 16)) * 16) for first, count in TOKEN_HALVES
    ]
    tokens = blks * sum(share for _, share in halves)
    cot_pairs = jnp.pad(cot_pairs.reshape(padded, lanes), ((0, tokens - padded), (0, 0)))
    w1, w2 = block_matrices(spec_w1, spec_w2)
    b1, b2 = spec_b1.reshape(1, lanes), spec_b2.reshape(1, lanes)
    per_token = jnp.stack(
        [scalars[:, :, 0] * (1.0 / C), (1.0 + scalars[:, :, 2]) * 0.25], axis=-1
    ).reshape(2, padded, 2)
    per_token = jnp.pad(per_token, ((0, 0), (0, tokens - padded), (0, 0)))
    per_token = [
        lax.dynamic_slice_in_dim(per_token, first + blk * share, share, 1).reshape(2 * share, 2)
        for first, share in halves
    ]
    params_ring = jnp.stack([piece[rows:].reshape(-1)[:param_count] for piece in sums_ring])
    params_ring = [params_ring[k] for k in [0] + list(range(blks - 1, 0, -1))] * 2
    params_all = lax.dynamic_slice_in_dim(jnp.stack(params_ring), blks - blk, blks, 0)
    bias_all = params_all[:, :ff_here].reshape(1, -1)
    token_params = [
        params_all[:, ff_here + i * chans : ff_here + (i + 1) * chans].reshape(1, C)
        for i in range(3)
    ]
    modes_b, cot_pairs, w1, w2, weights, per_token, bias_all, token_params = tied(
        modes_b, cot_pairs, w1, w2, weights, per_token, bias_all, token_params
    )
    modes_b = swap_first(modes_b, grid_axes)
    cot_rings = [
        send(cot_pairs[first : first + blks * share].reshape(blks, share, lanes), "blk")
        for first, share in halves
    ]
    shrunk_a, *kept_a = spectral(modes_a, turn, turn_rest, w1, b1, w2, b2)
    modes_b, shrunk_a, cot_rings[0] = tied(modes_b, shrunk_a, cot_rings[0])
    shrunk_a = swap_first(shrunk_a, grid_axes)
    weights_other = other_core(weights)
    shrunk_b, *kept_b = spectral(modes_b, turn, turn_rest, w1, b1, w2, b2)
    cot_b = cot_rings[1]
    shrunk_b, shrunk_a, cot_b[1], cot_b[-1] = tied(shrunk_b, shrunk_a, cot_b[1], cot_b[-1])
    shrunk_b = swap_first(shrunk_b, grid_axes)
    shrunk_b, shrunk_a, cot_rings = tied(shrunk_b, shrunk_a, cot_rings)

    middles = []
    for (first, share), spans in zip(halves, TOKEN_HALVES):
        middle = collect(
            (shrunk_a, shrunk_b),
            field_rows,
            sums_rows,
            gain_row,
            shift_row,
            doubled_back,
            spans,
            blks * share,
        )
        middle, shrunk_b = tied(middle, shrunk_b)
        middles.append(swap_first(middle.reshape(blks, share, lanes), "blk"))
    before, mixed_parts, grad_parts = (), [], []
    for middle, cot_ring, scalar in zip(middles, cot_rings, per_token):
        kept, sent, middle_grad, *before = mlp(
            middle,
            cot_ring,
            scalar,
            token_params[1],
            token_params[2],
            (weights, weights_other),
            bias_all,
            token_params[0],
            before,
        )
        if grad_parts:
            middle_grad, before, grad_parts[0] = tied(middle_grad, before, grad_parts[0])
        mixed_parts.append((kept, sent))
        grad_parts.append(swap_first(middle_grad, "blk"))
    up_kept, up_sent, down_kept, down_sent, bias_part, small_part = before

    summed = jnp.stack(
        [
            (kept.astype(wide) + other_core(sent).astype(wide)).astype(narrow)
            for kept, sent in ((up_kept, up_sent), (down_kept, down_sent))
        ],
        axis=2,
    )
    tile_shape = (-1,) + summed.shape[2:]
    summed = lax.psum_scatter(summed.reshape(-1, C), "lat", scatter_dimension=0, tiled=True)
    total = lax.psum_scatter(summed, "blk", scatter_dimension=0, tiled=True)
    total = total.reshape(tile_shape)
    mixed_rows = []
    for kept, sent in mixed_parts:
        sent = other_core(sent)
        mixed_rows.append(
            jnp.concatenate(
                [jnp.where(lon == 0, kept, sent), jnp.where(lon == 0, sent, kept)], axis=2
            )
        )
    owned = small_part[:3].reshape(3, blks, chans).transpose(1, 0, 2).reshape(blks, -1)
    owned = jnp.concatenate([owned, bias_part.reshape(blks, -1)], axis=1)[:, None, :]
    grad_parts[1], mixed_rows, owned = tied(grad_parts[1], mixed_rows, owned)
    owned = send(owned, "blk")

    back_a, back_b = spread(
        [part.reshape(-1, lanes) for part in grad_parts],
        [
            pl.BlockSpec((TOKEN_STEP * SLOTS, lanes), lambda i: (jnp.minimum(i, 2), 0)),
            pl.BlockSpec((TOKEN_STEP * SLOTS, lanes), lambda i: (jnp.maximum(i - 3, 0), 0)),
        ],
        spread_kernel,
        (doubled,),
        group,
        lanes,
        narrow,
        6,
        "spread_grad",
    )
    ring_a = send(mixed_rows[0], "blk")
    blk_pieces = send_slices(mixed_rows[1], "blk")
    middle_grad = jnp.concatenate([part.reshape(-1, lanes) for part in grad_parts])
    back_a = swap_first(back_a, grid_axes)
    back_b, ring_a[1], ring_a[-1] = tied(back_b, ring_a[1], ring_a[-1])
    back_b = swap_first(back_b, grid_axes)
    back_a, *spec_sums = spectral_back(back_a, *kept_a, turn, w1, b1, w2, b2)
    back_a, back_b, owned = tied(back_a, back_b, owned)
    back_a = swap_first(back_a, grid_axes)
    back_b, spec_grads, spec_small = spectral_back(
        back_b, *kept_b, turn, w1, b1, w2, b2, tuple(spec_sums)
    )
    back_b, back_a = tied(back_b, back_a)
    back_b = swap_first(back_b, grid_axes)
    vector = jnp.concatenate([spec_small[:2].reshape(-1), sum(owned).reshape(-1)])
    vector_size, vector_rows = vector.shape[0], -(-vector.shape[0] // (BS * group))
    vector = jnp.pad(vector, (0, group * vector_rows * BS - vector_size))
    shared = jnp.concatenate(
        [spec_grads.reshape(group, -1, BS), vector.reshape(group, vector_rows, BS)], axis=1
    )
    back_a, back_b, total, shared, ring_a, blk_pieces, middle_grad = tied(
        back_a, back_b, total, shared, ring_a, blk_pieces, middle_grad
    )
    total = lax.all_gather(total, grid_axes, axis=0, tiled=False)
    ring_b = send_pieces(blk_pieces, "blk")
    shared = jnp.sum(swap_first(shared, grid_axes), axis=0)

    base_kept, base_sent, part_sums, one_small = collect_back(
        (back_a, back_b), middle_grad, field_rows, sums_rows, gain_row, ahead_back
    )
    base_kept, base_sent, part_sums, ring_b, shared = tied(
        base_kept, base_sent, part_sums, ring_b, shared
    )
    grad_sums = jnp.broadcast_to(part_sums[:, None], (lons, blks) + part_sums.shape[1:])
    grad_sums = swap_first(grad_sums.reshape((-1,) + part_sums.shape[1:]), ("lon", "blk"))
    grad_sums = jnp.sum(grad_sums.reshape((lons, blks) + part_sums.shape[1:]), axis=1)
    grad_sums = grad_sums.reshape(rows, 2, SLOTS)
    base_other = other_core(base_sent)
    mixed = to_flat((ring_a, ring_b))
    base_other, grad_sums, one_small, total, shared, mixed = tied(
        base_other, grad_sums, one_small, total, shared, mixed
    )
    up_grad, down_grad = weight_grads(total, lons, ff_here)
    own_rows = shared.shape[0]
    shared = grid_broadcast(jnp.concatenate([shared, one_small[:2].reshape(-1, BS)]))
    grad_sums, mixed, up_grad, down_grad = tied(grad_sums, mixed, up_grad, down_grad)
    input_grad = final_flat(base_kept, base_other, field_cols, sums_cols, grad_sums)

    one_small = jnp.sum(shared[:, own_rows:], axis=0).reshape(-1)
    vector = shared[:, own_rows - vector_rows : own_rows].reshape(-1)
    spec_grads = shared[:, : own_rows - vector_rows].reshape(2, 2, blocks, BS, BS)
    pieces, at = [one_small[:chans], one_small[chans:]], 0
    for size in (lanes, lanes, chans, chans, chans, ff_here):
        pieces.append(vector[at : at + size])
        at += size
    gain_one_grad, shift_one_grad, b1_grad, b2_grad = pieces[:4]
    down_bias_grad, gain_two_grad, shift_two_grad, up_bias_grad = pieces[4:]
    return (
        mixed,
        input_grad,
        gain_one_grad,
        shift_one_grad,
        spec_grads[0],
        b1_grad.reshape(spec_b1.shape),
        spec_grads[1],
        b2_grad.reshape(spec_b2.shape),
        gain_two_grad,
        shift_two_grad,
        up_grad,
        up_bias_grad,
        down_grad,
        down_bias_grad,
    )


def solution(mesh):
    placed = (
        P("lon", "blk", "lat"),
        P("blk"),
        P("blk"),
        P(None, "blk", None, None),
        P(None, "blk", None),
        P(None, "blk", None, None),
        P(None, "blk", None),
        P("blk"),
        P("blk"),
        P(None, "blk"),
        P("blk"),
        P("blk", None),
        P("blk"),
        P("lat", "lon"),
        P("lon", "blk", "lat"),
    )
    return jax.shard_map(
        per_device,
        mesh=mesh,
        in_specs=placed,
        out_specs=(
            P("lon", "blk", "lat"),
            P("lon", "blk", "lat"),
            P("blk"),
            P("blk"),
            P(None, "blk", None, None),
            P(None, "blk", None),
            P(None, "blk", None, None),
            P(None, "blk", None),
            P("blk"),
            P("blk"),
            P(None, "blk"),
            P("blk"),
            P("blk", None),
            P("blk"),
        ),
        check_vma=False,
    )
```
